32 devices in a mesh: section: 4 (over y, x), dp: 8 (over z, core).
Axes of the slice: x: 2, y: 2, z: 4, core: 2. Of those that a mesh axis runs over, the one named last changes fastest.
Arguments:
- spikes: bfloat16 [32, 8, 4, 4, 1024], P('dp'), may hold values from 0 to 2
- labels: int32 [32], P('dp'), may hold values from 0 to 999
- readout: float32 [1024, 1000], replicated, may hold values from -0.1875 to 0.1875
- weights: float32 [4, 9216, 1024], P('section', 'dp'), may hold values from -6 to 6
- first_moment: float32 [4, 9216, 1024], P('section', 'dp'), may hold values from -4 to 4
- second_moment: float32 [4, 9216, 1024], P('section', 'dp'), may hold values from 1 to 16
Outputs:
- new_weights: float32 [4, 9216, 1024], P('section', 'dp')
- new_first: float32 [4, 9216, 1024], P('section', 'dp')
- new_second: float32 [4, 9216, 1024], P('section', 'dp')
The draws below stay inside these ranges and needn't reach their ends.
All inputs are finite; a program needn't handle non-finite values.
Results may differ from the reference program's by a relative error of at most 0.015.
Values may be sent and summed in bfloat16 or wider, within the bound.
No kernel may reach another device: no remote copies, remote signals or barrier semaphores. Data moves between devices by JAX's collectives and lax.ppermute only.
A program may use at most 192 MiB of HBM per device.

```python
import math
import jax
import jax.numpy as jnp
from jax import lax

C = 1024
CLASSES = 1000
TIMESTEPS = 8
SIDE = 4
IMG_DEV = 4
BLOCKS = 4
IMAGES = 32
N_SECTION = 4
N_DP = 8


def with_ends(result, key, least, top_value):
    longest = result.shape.index(max(result.shape))
    spots = []
    for shift in (0, 1):
        where = [jax.random.randint(jax.random.fold_in(key, axis), (), 0, length) for axis, length in enumerate(result.shape)]
        where[longest] = (where[longest] + shift) % result.shape[longest]
        spots.append(tuple(where))
    return result.at[spots[0]].set(least).at[spots[1]].set(top_value)


def shard_levels(own_key, shape, split, least, top_value):
    gain, own = 1.0, jax.random.fold_in(own_key, 6)
    for axis_at, parts in split:
        draws = jnp.exp(jax.random.uniform(jax.random.fold_in(own, axis_at), (parts,), jnp.float32, least / len(split), top_value / len(split)))
        gain = gain * jnp.repeat(draws, shape[axis_at] // parts).reshape([-1 if axis == axis_at else 1 for axis in range(len(shape))])
    return gain


def gaussian(key, extent, deviation, limit, cuts=(), kind=jnp.bfloat16):
    result = deviation * jax.random.normal(key, extent, jnp.float32)
    if cuts:
        result = result * shard_levels(key, extent, cuts, -0.22, 0.18)
    return jnp.clip(result, -limit, limit).astype(kind)


def setup_inputs(seed: int = 0) -> dict:
    seeds = jax.random.split(jax.random.key(seed), 7)
    return {
        "spikes": jnp.clip(2.0 * jax.random.uniform(seeds[0], (IMAGES, TIMESTEPS, SIDE, SIDE, C), jnp.float32) ** shard_levels(seeds[0], (IMAGES, TIMESTEPS, SIDE, SIDE, C), ((0, 8),), -0.2, 0.2), 0.0, 2.0).astype(jnp.bfloat16),
        "labels": with_ends(jax.random.randint(seeds[1], (IMAGES,), 0, CLASSES), jax.random.fold_in(seeds[1], 1), 0, CLASSES - 1).astype(jnp.int32),
        "readout": gaussian(seeds[2], (C, CLASSES), C ** -0.5, 0.1875, (), jnp.float32),
        "weights": gaussian(seeds[3], (BLOCKS, 9 * C, C), 1.0, 6.0, ((0, 4), (1, 8)), jnp.float32),
        "first_moment": gaussian(seeds[4], (BLOCKS, 9 * C, C), 0.3, 4.0, ((0, 4), (1, 8)), jnp.float32),
        "second_moment": jnp.clip(jnp.exp(math.log(16.0) - 2.7725887 * jax.random.uniform(seeds[5], (BLOCKS, 9 * C, C), jnp.float32) ** shard_levels(seeds[5], (BLOCKS, 9 * C, C), ((0, 4), (1, 8)), -0.2, 0.2)), 1.0, 16.0),
    }


leak_rate = 0.5
spike_slope = 4.0
threshold = 1.0
loss_scale = 4096.0
beta_first = 0.8
beta_second = 0.95
learn_rate = 0.5
adam_eps = 1e-08

def unfold(field_in):
    height_cells = field_in.shape[2]
    width_cells = field_in.shape[3]
    padded = jnp.pad(field_in, ((0, 0), (0, 0), (1, 1), (1, 1), (0, 0)))
    pieces = [padded[:, :, row_shift:row_shift + height_cells, col_shift:col_shift + width_cells, :] for row_shift in range(3) for col_shift in range(3)]
    stacked = jnp.stack(pieces, axis=4)
    return stacked.reshape(-1, 9 * field_in.shape[4])

def leaky(current):
    membrane = jnp.zeros_like(current[:, 0])
    fired_list = []
    for step_index in range(current.shape[1]):
        membrane = leak_rate * membrane + current[:, step_index]
        fired = jax.nn.sigmoid(spike_slope * (membrane - threshold))
        membrane = membrane - threshold * fired
        fired_list.append(fired)
    return jnp.stack(fired_list, axis=1)

def block_forward(field_in, kernel):
    rows_all = unfold(field_in)
    conv_scale = float(kernel.shape[0]) ** (-0.5)
    current = jnp.dot(rows_all, kernel, preferred_element_type=jnp.float32) * conv_scale
    shaped = current.reshape(field_in.shape[0], field_in.shape[1], -1)
    fired = leaky(shaped)
    output = (field_in.astype(jnp.float32) + fired.reshape(field_in.shape)).astype(jnp.bfloat16)
    return (output, shaped)

def block_backward(field_shape, shaped, kernel, upstream):
    up_float = upstream.astype(jnp.float32)
    unused, pull_back = jax.vjp(leaky, shaped)
    current_grad = pull_back(up_float.reshape(shaped.shape))[0]
    conv_scale = float(kernel.shape[0]) ** (-0.5)
    raw_grad = (current_grad * conv_scale).astype(jnp.bfloat16).reshape(-1, kernel.shape[1])
    row_grads = jnp.einsum('rc,kc->rk', raw_grad, kernel, preferred_element_type=jnp.float32)
    unused_two, unfold_back = jax.vjp(unfold, jnp.zeros(field_shape, jnp.float32))
    field_grad = unfold_back(row_grads)[0]
    back_grad = (up_float + field_grad).astype(jnp.bfloat16)
    return (back_grad, raw_grad)

def head_grads(final, group_labels, readout):
    pooled = lax.optimization_barrier(jnp.mean(final.astype(jnp.float32), axis=(1, 2, 3)))
    logits = jnp.dot(pooled, readout, precision=lax.Precision.HIGHEST)
    largest = lax.optimization_barrier(jnp.max(logits, axis=-1, keepdims=True))
    exponent = jnp.exp(logits - largest)
    probability = exponent / lax.optimization_barrier(jnp.sum(exponent, axis=-1, keepdims=True))
    classes = jnp.arange(readout.shape[1], dtype=jnp.int32)
    onehot = (group_labels[:, None] == classes[None, :]).astype(jnp.float32)
    dlogits = loss_scale * (probability - onehot)
    dpooled = jnp.dot(dlogits, readout.T, precision=lax.Precision.HIGHEST)
    cell_count = final.shape[1] * final.shape[2] * final.shape[3]
    spread = jnp.broadcast_to((dpooled / cell_count)[:, None, None, None, :], final.shape)
    return spread.astype(jnp.bfloat16)

def adam_update(weights, first_moment, second_moment, grad_total):
    new_first = beta_first * first_moment + (1.0 - beta_first) * grad_total
    new_second = beta_second * second_moment + (1.0 - beta_second) * grad_total * grad_total
    new_weights = weights - learn_rate * new_first / (jnp.sqrt(new_second) + adam_eps)
    return (new_weights, new_first, new_second)

def reference(spikes, labels, readout, weights, first_moment, second_moment):
    kernels = weights.astype(jnp.bfloat16)

    def one_group(grad_total, group_index):
        first_row = (group_index * IMG_DEV).astype(jnp.int32)
        field_in = lax.dynamic_slice_in_dim(spikes, first_row, IMG_DEV, 0)
        group_labels = lax.dynamic_slice_in_dim(labels, first_row, IMG_DEV, 0)
        inputs = []
        states = []
        for section_index in range(N_SECTION):
            inputs.append(field_in)
            field_in, shaped = block_forward(field_in, kernels[section_index])
            states.append(shaped)
        upstream = head_grads(field_in, group_labels, readout)
        grads = [None] * N_SECTION
        for section_index in reversed(range(N_SECTION)):
            upstream, raw_grad = block_backward(inputs[section_index].shape, states[section_index], kernels[section_index], upstream)
            rows_all = unfold(inputs[section_index])
            group_grad = jnp.einsum('rk,rc->kc', rows_all, raw_grad, preferred_element_type=jnp.float32)
            rounded = lax.optimization_barrier(group_grad.astype(jnp.bfloat16))
            grads[section_index] = rounded.astype(jnp.float32)
        return (grad_total + jnp.stack(grads), None)
    grad_total, unused = lax.scan(one_group, jnp.zeros(weights.shape, jnp.float32), jnp.arange(N_DP, dtype=jnp.int32))
    return adam_update(weights, first_moment, second_moment, grad_total)
```

```python
import functools
import jax
import jax.numpy as jnp
from jax import lax
from jax.experimental import pallas as pl
from jax.experimental.pallas import tpu as pltpu
from jax.sharding import PartitionSpec as P

leak_rate = 0.5
spike_slope = 4.0
threshold = 1.0
loss_scale = 4096.0
beta_first = 0.8
beta_second = 0.95
learn_rate = 0.5
adam_eps = 1e-08
HIGH = lax.Precision.HIGHEST
VMEM = pltpu.VMEM
LIMIT = 56 * 2**20


def fetch_weights(scal, sources, weights, sems):
    z, core = scal[1], scal[2]
    ring, depth = sources[0].shape[0], sources[0].shape[1]
    copies = []
    for which, source in enumerate(sources):
        owner_core = core if which == 0 else 1 - core
        for j in range(ring):
            place = lax.rem(z + j, ring)
            row = pl.multiple_of((place * 2 + owner_core) * depth, depth)
            copies.append(
                pltpu.make_async_copy(
                    source.at[j], weights.at[pl.ds(row, depth), :], sems.at[which, j]
                )
            )
    for copy in copies:
        copy.start()
    return copies


def forward_kernel(dims, last, scal, *refs):
    sections, height, width, images, steps = dims
    slices = refs[:sections]
    refs = refs[sections:]
    sources = refs[:2]
    refs = refs[2:]
    if last:
        readout, out, fired_out, logits_out, weights, padded, work, sems = refs
    else:
        out, fired_out, weights, padded, work, sems = refs
    copies = fetch_weights(scal, sources, weights, sems)
    rows, lanes = slices[0].shape
    group = images * steps
    channels = sections * lanes
    padded[...] = jnp.zeros_like(padded)
    for k in range(sections):
        padded[scal[0] ^ k, 1 : height + 1, 1 : width + 1] = slices[k][...].reshape(
            height, width, group, lanes
        )
    for copy in copies:
        copy.wait()
    total = jnp.zeros((rows, lanes), jnp.float32)
    for offset in range(9):
        r, c = divmod(offset, 3)
        lhs = jnp.concatenate(
            [
                padded[j, r : r + height, c : c + width].reshape(rows, lanes)
                for j in range(sections)
            ],
            axis=1,
        )
        total += jnp.dot(
            lhs,
            weights[offset * channels : (offset + 1) * channels, :],
            preferred_element_type=jnp.float32,
        )
    scale = float(9 * channels) ** (-0.5)
    current = total * scale
    count = rows // steps
    tiles = lanes // 128
    for tile in range(tiles):
        here, there = work.at[tile], fired_out.at[tile]
        here[...] = current[:, tile * 128 : (tile + 1) * 128]
        membrane = jnp.zeros((count, 128), jnp.float32)
        for t in range(steps):
            spot = pl.ds(t, count, stride=steps)
            h = leak_rate * membrane + here[spot, :]
            fired = jax.nn.sigmoid(spike_slope * (h - threshold))
            membrane = h - threshold * fired
            there[spot, :] = fired
    fired = jnp.concatenate([fired_out[tile] for tile in range(tiles)], axis=1)
    result = (slices[0][...].astype(jnp.float32) + fired).astype(jnp.bfloat16)
    out[...] = result
    if last:
        summed = jnp.sum(
            result.astype(jnp.float32).reshape(height * width, group, lanes), axis=0
        )
        pooled = jnp.sum(summed.reshape(images, steps, lanes), axis=1) / float(
            height * width * steps
        )
        logits_out[...] = jnp.dot(
            pooled, readout[...], precision=HIGH, preferred_element_type=jnp.float32
        )


def backward_kernel(dims, stage, classes, scal, *refs):
    sections, height, width, images, steps = dims
    if stage == 0:
        logit_parts = refs[:sections]
        labels, readout = refs[sections : sections + 2]
        refs = refs[sections + 2 :]
    else:
        own_part = refs[0]
        arrived = refs[1:sections]
        refs = refs[sections:]
    fired = refs[0]
    refs = refs[1:]
    if stage < 2:
        sources = refs[:2]
        refs = refs[2:]
        raw_out, own_out = refs[:2]
        sends = refs[2 : 1 + sections]
        weights, padded, upstream, work, sems = refs[1 + sections :]
        copies = fetch_weights(scal, sources, weights, sems)
        padded[...] = jnp.zeros_like(padded)
    else:
        raw_out, upstream, work = refs
    tiles, rows = fired.shape[:2]
    lanes = tiles * 128
    group = images * steps
    channels = sections * lanes
    cells = height * width
    count = rows // steps
    if stage == 0:
        logits = logit_parts[0][...]
        for part in logit_parts[1:]:
            logits = logits + part[...]
        lane = lax.broadcasted_iota(jnp.int32, logits.shape, 1)
        logits = jnp.where(lane < classes, logits, -jnp.inf)
        exponent = jnp.exp(logits - jnp.max(logits, axis=-1, keepdims=True))
        probability = exponent / jnp.sum(exponent, axis=-1, keepdims=True)
        onehot = (labels[...] == lane).astype(jnp.float32)
        dlogits = loss_scale * (probability - onehot)
        dpooled = lax.dot_general(
            dlogits,
            readout[...],
            (((1,), (1,)), ((), ())),
            precision=HIGH,
            preferred_element_type=jnp.float32,
        )
        spread = (dpooled / float(cells * steps)).astype(jnp.bfloat16).astype(jnp.float32)
        arriving = jnp.broadcast_to(
            spread[None, :, None, :], (cells, images, steps, lanes)
        ).reshape(rows, lanes)
    else:
        arriving = own_part[...]
        for part in arrived:
            arriving = arriving + part[...].astype(jnp.float32)
        arriving = arriving.astype(jnp.bfloat16).astype(jnp.float32)
    scale = float(9 * channels) ** (-0.5)
    for tile in range(tiles):
        upstream[tile] = arriving[:, tile * 128 : (tile + 1) * 128]
        here, there, fired_here = upstream.at[tile], work.at[tile], fired.at[tile]
        dmembrane = jnp.zeros((count, 128), jnp.float32)
        for t in reversed(range(steps)):
            spot = pl.ds(t, count, stride=steps)
            f = fired_here[spot, :]
            slope = spike_slope * (f * (1.0 - f))
            dh = dmembrane + (here[spot, :] - threshold * dmembrane) * slope
            there[spot, :] = dh * scale
            dmembrane = leak_rate * dh
    raw = jnp.concatenate([work[tile] for tile in range(tiles)], axis=1).astype(jnp.bfloat16)
    raw_out[...] = raw
    if stage == 2:
        return
    padded[1 : height + 1, 1 : width + 1] = raw.reshape(height, width, group, lanes)
    for copy in copies:
        copy.wait()
    for k in list(range(1, sections)) + [0]:
        total = jnp.zeros((rows, lanes), jnp.float32)
        for offset in range(9):
            r, c = divmod(offset, 3)
            lhs = padded[2 - r : 2 - r + height, 2 - c : 2 - c + width].reshape(rows, lanes)
            row = pl.multiple_of(offset * channels + (scal[0] ^ k) * lanes, lanes)
            total += lax.dot_general(
                lhs,
                weights[pl.ds(row, lanes), :],
                (((1,), (1,)), ((), ())),
                preferred_element_type=jnp.float32,
            )
        if k == 0:
            own_out[...] = total + jnp.concatenate([upstream[tile] for tile in range(tiles)], axis=1)
        else:
            sends[k - 1][...] = total.astype(jnp.bfloat16)


def vmem(count):
    return [pl.BlockSpec(memory_space=VMEM)] * count


def run_forward(dims, last, scal, slices, sources, readout):
    sections, height, width, images, steps = dims
    rows, lanes = slices[0].shape
    depth = sources[0].shape[1]
    ring = sources[0].shape[0]
    shapes = [
        jax.ShapeDtypeStruct((rows, lanes), jnp.bfloat16),
        jax.ShapeDtypeStruct((lanes // 128, rows, 128), jnp.float32),
    ]
    operands = [scal, *slices, *sources]
    extra = []
    if last:
        shapes.append(jax.ShapeDtypeStruct((images, readout.shape[1]), jnp.float32))
        operands.append(readout)
        extra = vmem(1)
    return pl.pallas_call(
        functools.partial(forward_kernel, dims, last),
        out_shape=shapes,
        in_specs=[pl.BlockSpec(memory_space=pltpu.SMEM)]
        + vmem(sections)
        + [pl.BlockSpec(memory_space=pl.ANY)] * 2
        + extra,
        out_specs=vmem(len(shapes)),
        scratch_shapes=[
            VMEM((2 * ring * depth, lanes), jnp.bfloat16),
            VMEM((sections, height + 2, width + 2, images * steps, lanes), jnp.bfloat16),
            VMEM((lanes // 128, rows, 128), jnp.float32),
            pltpu.SemaphoreType.DMA((2, ring)),
        ],
        compiler_params=pltpu.CompilerParams(vmem_limit_bytes=LIMIT),
        cost_estimate=pl.CostEstimate(
            flops=2 * rows * lanes * 2 * ring * depth,
            bytes_accessed=4 * ring * depth * lanes,
            transcendentals=rows * lanes,
        ),
        name="forward_block",
    )(*operands)


def run_backward(dims, stage, classes, scal, heads, fired, sources):
    sections, height, width, images, steps = dims
    tiles, rows = fired.shape[:2]
    lanes = tiles * 128
    half = jax.ShapeDtypeStruct((rows, lanes), jnp.bfloat16)
    full = jax.ShapeDtypeStruct((rows, lanes), jnp.float32)
    operands = [scal, *heads, fired]
    specs = [pl.BlockSpec(memory_space=pltpu.SMEM)] + vmem(len(heads) + 1)
    work = [VMEM(fired.shape, jnp.float32), VMEM(fired.shape, jnp.float32)]
    cost = 0
    if stage < 2:
        ring, depth = sources[0].shape[:2]
        operands += list(sources)
        specs += [pl.BlockSpec(memory_space=pl.ANY)] * 2
        shapes = [half, full] + [half] * (sections - 1)
        work = (
            [
                VMEM((2 * ring * depth, lanes), jnp.bfloat16),
                VMEM((height + 2, width + 2, images * steps, lanes), jnp.bfloat16),
            ]
            + work
            + [pltpu.SemaphoreType.DMA((2, ring))]
        )
        cost = 2 * ring * depth
    else:
        shapes = [half]
    return pl.pallas_call(
        functools.partial(backward_kernel, dims, stage, classes),
        out_shape=shapes,
        in_specs=specs,
        out_specs=vmem(len(shapes)),
        scratch_shapes=work,
        compiler_params=pltpu.CompilerParams(vmem_limit_bytes=LIMIT),
        cost_estimate=pl.CostEstimate(
            flops=2 * rows * lanes * cost + rows * lanes * 100,
            bytes_accessed=2 * cost * lanes + 8 * rows * lanes,
            transcendentals=0,
        ),
        name="backward_block",
    )(*operands)


def after(value, earlier):
    if earlier is None:
        return value
    return lax.optimization_barrier((value, earlier))[0]


def ring_steps(piece, z, ring, gate):
    def pairs(step, way):
        if way > 0:
            hops = [(i, i + 1) for i in range(step - 1, ring - 1)]
        else:
            hops = [(i, i - 1) for i in range(1, ring - step + 1)]
        return [(2 * a + core, 2 * b + core) for a, b in hops for core in range(2)]

    low, high = {}, {}
    up, down = piece, piece
    for step in range(1, ring):
        up, down = gate(up), gate(down)
        up = lax.ppermute(up, "dp", pairs(step, 1))
        down = lax.ppermute(down, "dp", pairs(step, -1))
        low[step], high[step] = up, down
        yield up
    result = [piece]
    for j in range(1, ring):
        result.append(jnp.where(z + j < ring, high[j], low[ring - j]))
    yield result


def swap_core(value, count):
    return lax.ppermute(value, "dp", [(i, i ^ 1) for i in range(count)])


def gather_ring(piece, z, ring):
    for result in ring_steps(piece, z, ring, lambda value: value):
        pass
    own = jnp.stack(result)
    return own, swap_core(own, 2 * ring)


def adam_update(weights, first_moment, second_moment, grad_total):
    new_first = beta_first * first_moment + (1.0 - beta_first) * grad_total
    new_second = beta_second * second_moment + (1.0 - beta_second) * grad_total * grad_total
    new_weights = weights - learn_rate * new_first / (jnp.sqrt(new_second) + adam_eps)
    return (new_weights, new_first, new_second)


def shards(spikes, labels, readout, weights, first_moment, second_moment):
    sections = lax.axis_size("section")
    devices = lax.axis_size("dp")
    ring = devices // 2
    s = lax.axis_index("section")
    d = lax.axis_index("dp")
    z, core = d // 2, d % 2
    images, steps, height, width, channels = spikes.shape
    group = images * steps
    rows = height * width * group
    lanes = channels // sections
    depth = weights.shape[1]
    classes = readout.shape[1]
    dims = (sections, height, width, images, steps)
    scal = jnp.stack([s, z, core]).astype(jnp.int32)

    def exchange(values):
        return [
            lax.ppermute(values[k], "section", [(i, i ^ (k + 1)) for i in range(sections)])
            for k in range(sections - 1)
        ]

    def columns(array, k):
        return lax.dynamic_slice_in_dim(array, (s ^ k) * lanes, lanes, 1)

    def pick(options, index):
        return lax.dynamic_index_in_dim(jnp.stack(options), index, 0, keepdims=False)

    pieces = [columns(weights[0], k).astype(jnp.bfloat16) for k in range(sections)]
    pieces = [pieces[0]] + exchange(pieces[1:])
    field = spikes.transpose(2, 3, 0, 1, 4).reshape(rows, channels)
    slices = [columns(field, k) for k in range(sections)]
    padded_classes = -(-classes // 128) * 128
    readout_own = lax.dynamic_slice_in_dim(readout, s * lanes, lanes, 0)
    readout_own = jnp.pad(readout_own, ((0, 0), (0, padded_classes - classes)))

    history = []

    def gate(value):
        if len(history) >= 4:
            value = after(value, history[-4])
        return value

    sources = [None] * sections
    for first in range(0, sections, 2):
        blocks = [b for b in (first, first + 1) if b < sections]
        walks = {b: ring_steps(pick(pieces, s ^ b), z, ring, gate) for b in blocks}
        for step in range(ring):
            for b in blocks:
                sources[b] = next(walks[b])
                if step < ring - 1:
                    history.extend([sources[b], sources[b]])
        for b in blocks:
            own = jnp.stack(sources[b])
            sources[b] = (own, swap_core(own, devices))

    inputs, fired_all = [], []
    for b in range(sections):
        inputs.append(slices)
        last = b == sections - 1
        result = run_forward(dims, last, scal, slices, sources[b], readout_own)
        fired_all.append(result[1])
        if not last:
            slices = [result[0]] + exchange([result[0]] * (sections - 1))
    logits = result[2]
    heads = [logits] + exchange([logits] * (sections - 1))
    heads += [labels[:, None], readout_own]

    def ordered(parts):
        return jnp.concatenate([pick(parts, s ^ j) for j in range(sections)], axis=1)

    own_inputs = [pick([inputs[b][k] for b in range(sections)], s) for k in range(sections)]
    x_all = gather_ring(ordered(own_inputs), z, ring)

    raws = [None] * sections
    for b in reversed(range(sections)):
        stage = 0 if b == sections - 1 else (2 if b == 0 else 1)
        result = run_backward(dims, stage, classes, scal, heads, fired_all[b], sources[b])
        raws[b] = result[0]
        if b > 0:
            heads = [result[1]] + exchange(result[2:])

    sent = [pick(raws, s ^ k) for k in range(sections)]
    own_raw = ordered([sent[0]] + exchange(sent[1:]))
    raw_all = gather_ring(own_raw, z, ring)

    x_all = jnp.concatenate(x_all).reshape(devices, height, width, group, channels)
    x_all = jnp.pad(x_all, ((0, 0), (1, 1), (1, 1), (0, 0), (0, 0)))
    start = d * depth
    channel = start % channels
    step = 1
    while channels % (2 * step) == 0 and depth % (2 * step) == 0:
        step *= 2
    spans = -(-(channels - step + depth) // channels)
    shifted = []
    for i in range(spans):
        offset = jnp.minimum(start // channels + i, 8)
        shifted.append(
            lax.dynamic_slice(
                x_all,
                (0, offset // 3, offset % 3, 0, 0),
                (devices, height, width, group, channels),
            ).reshape(devices * rows, channels)
        )
    cols = lax.dynamic_slice_in_dim(jnp.concatenate(shifted, axis=1), channel, depth, 1)
    raw_all = jnp.concatenate(raw_all).reshape(devices * rows, channels)
    grad = lax.dot_general(
        cols, raw_all, (((0,), (0,)), ((), ())), preferred_element_type=jnp.float32
    )
    return adam_update(weights, first_moment, second_moment, grad[None])


def solution(mesh):
    return jax.shard_map(
        shards,
        mesh=mesh,
        in_specs=(
            P("dp", None, None, None, None),
            P("dp"),
            P(),
            P("section", "dp", None),
            P("section", "dp", None),
            P("section", "dp", None),
        ),
        out_specs=(P("section", "dp", None), P("section", "dp", None), P("section", "dp", None)),
        check_vma=False,
    )
```

```python
import functools
import jax
import jax.numpy as jnp
from jax import lax
from jax.experimental import pallas as pl
from jax.experimental.pallas import tpu as pltpu
from jax.sharding import PartitionSpec as P

leak_rate = 0.5
spike_slope = 4.0
threshold = 1.0
loss_scale = 4096.0
beta_first = 0.8
beta_second = 0.95
learn_rate = 0.5
adam_eps = 1e-08
HIGH = lax.Precision.HIGHEST
VMEM = pltpu.VMEM
LIMIT = 24 * 2**20
parts = 2


def fetch_weights(scal, sources, weights, sems):
    z, core = scal[1], scal[2]
    ring, part_rows = sources[0].shape[0], sources[0].shape[1]
    depth = part_rows * (len(sources) // 2)
    copies = []
    for index, source in enumerate(sources):
        part, which = divmod(index, 2)
        owner_core = core if which == 0 else 1 - core
        for j in range(ring):
            place = lax.rem(z + j, ring)
            row = (place * 2 + owner_core) * depth + part * part_rows
            row = pl.multiple_of(row, part_rows)
            copies.append(
                pltpu.make_async_copy(
                    source.at[j], weights.at[pl.ds(row, part_rows), :], sems.at[index, j]
                )
            )
    for copy in copies:
        copy.start()
    return copies


def forward_kernel(dims, last, scal, *refs):
    sections, height, width, images, steps = dims
    slices = refs[:sections]
    refs = refs[sections:]
    sources = refs[: 2 * parts]
    refs = refs[2 * parts :]
    if last:
        readout, out, fired_out, logits_out, weights, padded, work, sems = refs
    else:
        out, fired_out, weights, padded, work, sems = refs
    copies = fetch_weights(scal, sources, weights, sems)
    rows, lanes = slices[0].shape
    group = images * steps
    channels = sections * lanes
    padded[...] = jnp.zeros_like(padded)
    for k in range(sections):
        padded[scal[0] ^ k, 1 : height + 1, 1 : width + 1] = slices[k][...].reshape(
            height, width, group, lanes
        )
    for copy in copies:
        copy.wait()
    total = jnp.zeros((rows, lanes), jnp.float32)
    for offset in range(9):
        r, c = divmod(offset, 3)
        lhs = jnp.concatenate(
            [
                padded[j, r : r + height, c : c + width].reshape(rows, lanes)
                for j in range(sections)
            ],
            axis=1,
        )
        total += jnp.dot(
            lhs,
            weights[offset * channels : (offset + 1) * channels, :],
            preferred_element_type=jnp.float32,
        )
    scale = float(9 * channels) ** (-0.5)
    current = total * scale
    count = rows // steps
    tiles = lanes // 128
    for tile in range(tiles):
        here, there = work.at[tile], fired_out.at[tile]
        here[...] = current[:, tile * 128 : (tile + 1) * 128]
        membrane = jnp.zeros((count, 128), jnp.float32)
        for t in range(steps):
            spot = pl.ds(t, count, stride=steps)
            h = leak_rate * membrane + here[spot, :]
            fired = jax.nn.sigmoid(spike_slope * (h - threshold))
            membrane = h - threshold * fired
            there[spot, :] = fired
    fired = jnp.concatenate([fired_out[tile] for tile in range(tiles)], axis=1)
    result = (slices[0][...].astype(jnp.float32) + fired).astype(jnp.bfloat16)
    out[...] = result
    if last:
        summed = jnp.sum(
            result.astype(jnp.float32).reshape(height * width, group, lanes), axis=0
        )
        pooled = jnp.sum(summed.reshape(images, steps, lanes), axis=1) / float(
            height * width * steps
        )
        logits_out[...] = jnp.dot(
            pooled, readout[...], precision=HIGH, preferred_element_type=jnp.float32
        )


def backward_kernel(dims, stage, classes, scal, *refs):
    sections, height, width, images, steps = dims
    if stage == 0:
        logit_parts = refs[:sections]
        labels, readout = refs[sections : sections + 2]
        refs = refs[sections + 2 :]
    else:
        own_part = refs[0]
        arrived = refs[1:sections]
        refs = refs[sections:]
    fired = refs[0]
    refs = refs[1:]
    if stage < 2:
        sources = refs[: 2 * parts]
        refs = refs[2 * parts :]
        raw_out, own_out = refs[:2]
        sends = refs[2 : 1 + sections]
        weights, padded, upstream, work, sems = refs[1 + sections :]
        copies = fetch_weights(scal, sources, weights, sems)
        padded[...] = jnp.zeros_like(padded)
    else:
        raw_out, upstream, work = refs
    tiles, rows = fired.shape[:2]
    lanes = tiles * 128
    group = images * steps
    channels = sections * lanes
    cells = height * width
    count = rows // steps
    if stage == 0:
        logits = logit_parts[0][...]
        for part in logit_parts[1:]:
            logits = logits + part[...]
        lane = lax.broadcasted_iota(jnp.int32, logits.shape, 1)
        logits = jnp.where(lane < classes, logits, -jnp.inf)
        exponent = jnp.exp(logits - jnp.max(logits, axis=-1, keepdims=True))
        probability = exponent / jnp.sum(exponent, axis=-1, keepdims=True)
        onehot = (labels[...] == lane).astype(jnp.float32)
        dlogits = loss_scale * (probability - onehot)
        dpooled = lax.dot_general(
            dlogits,
            readout[...],
            (((1,), (1,)), ((), ())),
            precision=HIGH,
            preferred_element_type=jnp.float32,
        )
        spread = (dpooled / float(cells * steps)).astype(jnp.bfloat16).astype(jnp.float32)
        arriving = jnp.broadcast_to(
            spread[None, :, None, :], (cells, images, steps, lanes)
        ).reshape(rows, lanes)
    else:
        arriving = own_part[...]
        for part in arrived:
            arriving = arriving + part[...].astype(jnp.float32)
        arriving = arriving.astype(jnp.bfloat16).astype(jnp.float32)
    scale = float(9 * channels) ** (-0.5)
    for tile in range(tiles):
        upstream[tile] = arriving[:, tile * 128 : (tile + 1) * 128]
        here, there, fired_here = upstream.at[tile], work.at[tile], fired.at[tile]
        dmembrane = jnp.zeros((count, 128), jnp.float32)
        for t in reversed(range(steps)):
            spot = pl.ds(t, count, stride=steps)
            f = fired_here[spot, :]
            slope = spike_slope * (f * (1.0 - f))
            dh = dmembrane + (here[spot, :] - threshold * dmembrane) * slope
            there[spot, :] = dh * scale
            dmembrane = leak_rate * dh
    raw = jnp.concatenate([work[tile] for tile in range(tiles)], axis=1).astype(jnp.bfloat16)
    raw_out[...] = raw
    if stage == 2:
        return
    padded[1 : height + 1, 1 : width + 1] = raw.reshape(height, width, group, lanes)
    for copy in copies:
        copy.wait()
    for k in list(range(1, sections)) + [0]:
        total = jnp.zeros((rows, lanes), jnp.float32)
        for offset in range(9):
            r, c = divmod(offset, 3)
            lhs = padded[2 - r : 2 - r + height, 2 - c : 2 - c + width].reshape(rows, lanes)
            row = pl.multiple_of(offset * channels + (scal[0] ^ k) * lanes, lanes)
            total += lax.dot_general(
                lhs,
                weights[pl.ds(row, lanes), :],
                (((1,), (1,)), ((), ())),
                preferred_element_type=jnp.float32,
            )
        if k == 0:
            own_out[...] = total + jnp.concatenate([upstream[tile] for tile in range(tiles)], axis=1)
        else:
            sends[k - 1][...] = total.astype(jnp.bfloat16)


def vmem(count):
    return [pl.BlockSpec(memory_space=VMEM)] * count


def run_forward(dims, last, scal, slices, sources, readout):
    sections, height, width, images, steps = dims
    rows, lanes = slices[0].shape
    ring, part_rows = sources[0].shape[:2]
    depth = parts * part_rows
    shapes = [
        jax.ShapeDtypeStruct((rows, lanes), jnp.bfloat16),
        jax.ShapeDtypeStruct((lanes // 128, rows, 128), jnp.float32),
    ]
    operands = [scal, *slices, *sources]
    extra = []
    if last:
        shapes.append(jax.ShapeDtypeStruct((images, readout.shape[1]), jnp.float32))
        operands.append(readout)
        extra = vmem(1)
    return pl.pallas_call(
        functools.partial(forward_kernel, dims, last),
        out_shape=shapes,
        in_specs=[pl.BlockSpec(memory_space=pltpu.SMEM)]
        + vmem(sections)
        + [pl.BlockSpec(memory_space=pl.ANY)] * len(sources)
        + extra,
        out_specs=vmem(len(shapes)),
        scratch_shapes=[
            VMEM((2 * ring * depth, lanes), jnp.bfloat16),
            VMEM((sections, height + 2, width + 2, images * steps, lanes), jnp.bfloat16),
            VMEM((lanes // 128, rows, 128), jnp.float32),
            pltpu.SemaphoreType.DMA((2 * parts, ring)),
        ],
        compiler_params=pltpu.CompilerParams(vmem_limit_bytes=LIMIT),
        cost_estimate=pl.CostEstimate(
            flops=2 * rows * lanes * 2 * ring * depth,
            bytes_accessed=4 * ring * depth * lanes,
            transcendentals=rows * lanes,
        ),
        name="forward_block",
    )(*operands)


def run_backward(dims, stage, classes, scal, heads, fired, sources):
    sections, height, width, images, steps = dims
    tiles, rows = fired.shape[:2]
    lanes = tiles * 128
    half = jax.ShapeDtypeStruct((rows, lanes), jnp.bfloat16)
    full = jax.ShapeDtypeStruct((rows, lanes), jnp.float32)
    operands = [scal, *heads, fired]
    specs = [pl.BlockSpec(memory_space=pltpu.SMEM)] + vmem(len(heads) + 1)
    work = [VMEM(fired.shape, jnp.float32), VMEM(fired.shape, jnp.float32)]
    cost = 0
    if stage < 2:
        ring, part_rows = sources[0].shape[:2]
        depth = parts * part_rows
        operands += list(sources)
        specs += [pl.BlockSpec(memory_space=pl.ANY)] * len(sources)
        shapes = [half, full] + [half] * (sections - 1)
        work = (
            [
                VMEM((2 * ring * depth, lanes), jnp.bfloat16),
                VMEM((height + 2, width + 2, images * steps, lanes), jnp.bfloat16),
            ]
            + work
            + [pltpu.SemaphoreType.DMA((2 * parts, ring))]
        )
        cost = 2 * ring * depth
    else:
        shapes = [half]
    return pl.pallas_call(
        functools.partial(backward_kernel, dims, stage, classes),
        out_shape=shapes,
        in_specs=specs,
        out_specs=vmem(len(shapes)),
        scratch_shapes=work,
        compiler_params=pltpu.CompilerParams(vmem_limit_bytes=LIMIT),
        cost_estimate=pl.CostEstimate(
            flops=2 * rows * lanes * cost + rows * lanes * 100,
            bytes_accessed=2 * cost * lanes + 8 * rows * lanes,
            transcendentals=0,
        ),
        name="backward_block",
    )(*operands)


def after(value, *earlier):
    return lax.optimization_barrier((value, *earlier))[0]


def hops(step, way, ring):
    if way > 0:
        pairs = [(i, i + 1) for i in range(step - 1, ring - 1)]
    else:
        pairs = [(i, i - 1) for i in range(1, ring - step + 1)]
    return [(2 * a + core, 2 * b + core) for a, b in pairs for core in range(2)]


def ring_gather(pieces, ring, gates=()):
    low = [[] for _ in pieces]
    high = [[] for _ in pieces]
    for step in range(1, ring):
        for h, piece in enumerate(pieces):
            up = low[h][-1] if step > 1 else piece
            down = high[h][-1] if step > 1 else piece
            if step == 1 and gates:
                up = down = after(piece, *gates[h])
            low[h].append(lax.ppermute(up, "dp", hops(step, 1, ring)))
            high[h].append(lax.ppermute(down, "dp", hops(step, -1, ring)))
    return low, high


def swap_core(value):
    count = lax.axis_size("dp")
    return lax.ppermute(value, "dp", [(i, i ^ 1) for i in range(count)])


def by_step(piece, low, high, z, ring):
    result = [[piece]]
    for step in range(1, ring):
        up, down = low[step - 1], high[step - 1]
        if 2 * step < ring:
            result.append([down, up])
        else:
            result.append([jnp.where(z + step < ring, down, up)])
    return result


def adam_update(weights, first_moment, second_moment, grad_total):
    new_first = beta_first * first_moment + (1.0 - beta_first) * grad_total
    new_second = beta_second * second_moment + (1.0 - beta_second) * grad_total * grad_total
    new_weights = weights - learn_rate * new_first / (jnp.sqrt(new_second) + adam_eps)
    return (new_weights, new_first, new_second)


def shards(spikes, labels, readout, weights, first_moment, second_moment):
    sections = lax.axis_size("section")
    devices = lax.axis_size("dp")
    ring = devices // 2
    s = lax.axis_index("section")
    d = lax.axis_index("dp")
    z, core = d // 2, d % 2
    images, steps, height, width, channels = spikes.shape
    group = images * steps
    rows = height * width * group
    lanes = channels // sections
    depth = weights.shape[1]
    classes = readout.shape[1]
    dims = (sections, height, width, images, steps)
    scal = jnp.stack([s, z, core]).astype(jnp.int32)

    def exchange(values):
        return [
            lax.ppermute(values[k], "section", [(i, i ^ (k + 1)) for i in range(sections)])
            for k in range(sections - 1)
        ]

    def columns(array, k):
        return lax.dynamic_slice_in_dim(array, (s ^ k) * lanes, lanes, 1)

    def pick(options, index):
        return lax.dynamic_index_in_dim(jnp.stack(options), index, 0, keepdims=False)

    part_rows = depth // parts
    pieces = []
    for h in range(parts):
        own = [
            columns(weights[0, h * part_rows : (h + 1) * part_rows], k).astype(jnp.bfloat16)
            for k in range(sections)
        ]
        if h:
            own = [own[0]] + [after(own[k], pieces[-1][k]) for k in range(1, sections)]
        pieces.append([own[0]] + exchange(own[1:]))
    field = spikes.transpose(2, 3, 0, 1, 4).reshape(rows, channels)
    slices = [columns(field, k) for k in range(sections)]
    padded_classes = -(-classes // 128) * 128
    readout_own = lax.dynamic_slice_in_dim(readout, s * lanes, lanes, 0)
    readout_own = jnp.pad(readout_own, ((0, 0), (0, padded_classes - classes)))

    inputs, results, chains, sources = [slices], [], [], []

    def gather_block(b):
        gates = ()
        if b > 0:
            low, high = chains[b - 1]
            near = max(ring - 3, 0)
            gates = [(low[h][near], high[h][near]) for h in range(parts)]
            if b > 1:
                gates = [gate + (results[b - 2][0],) for gate in gates]
        own = [pick(pieces[h], s ^ b) for h in range(parts)]
        low, high = ring_gather(own, ring, gates)
        chains.append((low, high))
        flat = []
        for h in range(parts):
            held = [own[h]]
            for j in range(1, ring):
                held.append(jnp.where(z + j < ring, high[h][j - 1], low[h][ring - j - 1]))
            held = jnp.stack(held)
            flat += [held, swap_core(held)]
        sources.append(flat)

    gather_block(0)
    for b in range(sections):
        if b + 1 < sections:
            gather_block(b + 1)
        last = b == sections - 1
        result = run_forward(dims, last, scal, inputs[b], sources[b], readout_own)
        results.append(result)
        if not last:
            inputs.append([result[0]] + exchange([result[0]] * (sections - 1)))
    logits = result[2]
    heads = [logits] + exchange([logits] * (sections - 1))
    heads += [labels[:, None], readout_own]

    def ordered(parts):
        return jnp.concatenate([pick(parts, s ^ j) for j in range(sections)], axis=1)

    own_inputs = [pick([inputs[b][k] for b in range(sections)], s) for k in range(sections)]
    own_x = ordered(own_inputs)
    x_low, x_high = ring_gather([own_x], ring)
    x_low, x_high = x_low[0], x_high[0]

    raws = [None] * sections
    for b in reversed(range(sections)):
        stage = 0 if b == sections - 1 else (2 if b == 0 else 1)
        step = sections - 1 - b
        if 0 < step < ring:
            heads[0] = after(heads[0], x_low[step - 1], x_high[step - 1])
        result = run_backward(dims, stage, classes, scal, heads, results[b][1], sources[b])
        raws[b] = result[0]
        if b > 0:
            heads = [result[1]] + exchange(result[2:])

    sent = [pick(raws, s ^ k) for k in range(sections)]
    own_raw = ordered([sent[0]] + exchange(sent[1:]))
    raw_parts = [own_raw[h * rows // parts : (h + 1) * rows // parts] for h in range(parts)]
    raw_low, raw_high = ring_gather(raw_parts, ring)
    raw_steps = [by_step(raw_parts[h], raw_low[h], raw_high[h], z, ring) for h in range(parts)]
    x_steps = by_step(own_x, x_low, x_high, z, ring)

    def both_cores(values):
        return [array for value in values for array in (value, swap_core(value))]

    def raw_of(step, *earlier):
        count = len(raw_steps[0][step])
        values = [raw_steps[h][step] for h in range(parts)]
        if earlier:
            values = [[after(value, *earlier) for value in part] for part in values]
        swapped = [both_cores(part) for part in values]
        return [swapped[h][i] for i in range(2 * count) for h in range(parts)]

    start = d * depth
    channel = start % channels
    step = 1
    while channels % (2 * step) == 0 and depth % (2 * step) == 0:
        step *= 2
    spans = -(-(channels - step + depth) // channels)

    def cols_of(pieces):
        count = len(pieces)
        fields = jnp.stack(pieces).reshape(count, height, width, group, channels)
        fields = jnp.pad(fields, ((0, 0), (1, 1), (1, 1), (0, 0), (0, 0)))
        shifted = []
        for i in range(spans):
            offset = jnp.minimum(start // channels + i, 8)
            shifted.append(
                lax.dynamic_slice(
                    fields,
                    (0, offset // 3, offset % 3, 0, 0),
                    (count, height, width, group, channels),
                ).reshape(count * rows, channels)
            )
        return lax.dynamic_slice_in_dim(jnp.concatenate(shifted, axis=1), channel, depth, 1)

    def product(x_pieces, raw_pieces):
        return lax.dot_general(
            cols_of(x_pieces),
            jnp.concatenate(raw_pieces),
            (((0,), (0,)), ((), ())),
            preferred_element_type=jnp.float32,
        )

    early_x = both_cores([piece for pieces in x_steps[:-1] for piece in pieces])
    early_raw = [piece for step in range(ring - 1) for piece in raw_of(step)]
    late_x = both_cores(x_steps[-1])
    early = product(early_x, early_raw)
    grad = early + product(late_x, raw_of(ring - 1, early))
    return adam_update(weights, first_moment, second_moment, grad[None])


def solution(mesh):
    return jax.shard_map(
        shards,
        mesh=mesh,
        in_specs=(
            P("dp", None, None, None, None),
            P("dp"),
            P(),
            P("section", "dp", None),
            P("section", "dp", None),
            P("section", "dp", None),
        ),
        out_specs=(P("section", "dp", None), P("section", "dp", None), P("section", "dp", None)),
        check_vma=False,
    )
```

```python
import functools
import jax
import jax.numpy as jnp
from jax import lax
from jax.experimental import pallas as pl
from jax.experimental.pallas import tpu as pltpu
from jax.sharding import PartitionSpec as P

leak_rate = 0.5
spike_slope = 4.0
threshold = 1.0
loss_scale = 4096.0
beta_first = 0.8
beta_second = 0.95
learn_rate = 0.5
adam_eps = 1e-08
HIGH = lax.Precision.HIGHEST
VMEM = pltpu.VMEM
LIMIT = 24 * 2**20
parts = 1


def fetch_weights(scal, sources, weights, sems):
    z, core = scal[1], scal[2]
    ring, part_rows = sources[0].shape[0], sources[0].shape[1]
    depth = part_rows * (len(sources) // 2)
    copies = []
    for index, source in enumerate(sources):
        part, which = divmod(index, 2)
        owner_core = core if which == 0 else 1 - core
        for j in range(ring):
            place = lax.rem(z + j, ring)
            row = (place * 2 + owner_core) * depth + part * part_rows
            row = pl.multiple_of(row, part_rows)
            copies.append(
                pltpu.make_async_copy(
                    source.at[j], weights.at[pl.ds(row, part_rows), :], sems.at[index, j]
                )
            )
    for copy in copies:
        copy.start()
    return copies


def forward_kernel(dims, last, scal, *refs):
    sections, height, width, images, steps = dims
    slices = refs[:sections]
    refs = refs[sections:]
    sources = refs[: 2 * parts]
    refs = refs[2 * parts :]
    if last:
        readout, out, fired_out, logits_out, weights, padded, work, sems = refs
    else:
        out, fired_out, weights, padded, work, sems = refs
    copies = fetch_weights(scal, sources, weights, sems)
    rows, lanes = slices[0].shape
    group = images * steps
    channels = sections * lanes
    padded[...] = jnp.zeros_like(padded)
    for k in range(sections):
        padded[scal[0] ^ k, 1 : height + 1, 1 : width + 1] = slices[k][...].reshape(
            height, width, group, lanes
        )
    for copy in copies:
        copy.wait()
    total = jnp.zeros((rows, lanes), jnp.float32)
    for offset in range(9):
        r, c = divmod(offset, 3)
        lhs = jnp.concatenate(
            [
                padded[j, r : r + height, c : c + width].reshape(rows, lanes)
                for j in range(sections)
            ],
            axis=1,
        )
        total += jnp.dot(
            lhs,
            weights[offset * channels : (offset + 1) * channels, :],
            preferred_element_type=jnp.float32,
        )
    scale = float(9 * channels) ** (-0.5)
    current = total * scale
    count = rows // steps
    tiles = lanes // 128
    for tile in range(tiles):
        here, there = work.at[tile], fired_out.at[tile]
        here[...] = current[:, tile * 128 : (tile + 1) * 128]
        membrane = jnp.zeros((count, 128), jnp.float32)
        for t in range(steps):
            spot = pl.ds(t, count, stride=steps)
            h = leak_rate * membrane + here[spot, :]
            fired = jax.nn.sigmoid(spike_slope * (h - threshold))
            membrane = h - threshold * fired
            there[spot, :] = fired
    fired = jnp.concatenate([fired_out[tile] for tile in range(tiles)], axis=1)
    result = (slices[0][...].astype(jnp.float32) + fired).astype(jnp.bfloat16)
    out[...] = result
    if last:
        summed = jnp.sum(
            result.astype(jnp.float32).reshape(height * width, group, lanes), axis=0
        )
        pooled = jnp.sum(summed.reshape(images, steps, lanes), axis=1) / float(
            height * width * steps
        )
        logits_out[...] = jnp.dot(
            pooled, readout[...], precision=HIGH, preferred_element_type=jnp.float32
        )


def backward_kernel(dims, stage, classes, scal, *refs):
    sections, height, width, images, steps = dims
    if stage == 0:
        logit_parts = refs[:sections]
        labels, readout = refs[sections : sections + 2]
        refs = refs[sections + 2 :]
    else:
        own_part = refs[0]
        arrived = refs[1:sections]
        refs = refs[sections:]
    fired = refs[0]
    refs = refs[1:]
    if stage < 2:
        sources = refs[: 2 * parts]
        refs = refs[2 * parts :]
        raw_out, own_out = refs[:2]
        sends = refs[2 : 1 + sections]
        weights, padded, upstream, work, sems = refs[1 + sections :]
        copies = fetch_weights(scal, sources, weights, sems)
        padded[...] = jnp.zeros_like(padded)
    else:
        raw_out, upstream, work = refs
    tiles, rows = fired.shape[:2]
    lanes = tiles * 128
    group = images * steps
    channels = sections * lanes
    cells = height * width
    count = rows // steps
    if stage == 0:
        logits = logit_parts[0][...]
        for part in logit_parts[1:]:
            logits = logits + part[...]
        lane = lax.broadcasted_iota(jnp.int32, logits.shape, 1)
        logits = jnp.where(lane < classes, logits, -jnp.inf)
        exponent = jnp.exp(logits - jnp.max(logits, axis=-1, keepdims=True))
        probability = exponent / jnp.sum(exponent, axis=-1, keepdims=True)
        onehot = (labels[...] == lane).astype(jnp.float32)
        dlogits = loss_scale * (probability - onehot)
        dpooled = lax.dot_general(
            dlogits,
            readout[...],
            (((1,), (1,)), ((), ())),
            precision=HIGH,
            preferred_element_type=jnp.float32,
        )
        spread = (dpooled / float(cells * steps)).astype(jnp.bfloat16).astype(jnp.float32)
        arriving = jnp.broadcast_to(
            spread[None, :, None, :], (cells, images, steps, lanes)
        ).reshape(rows, lanes)
    else:
        arriving = own_part[...]
        for part in arrived:
            arriving = arriving + part[...].astype(jnp.float32)
        arriving = arriving.astype(jnp.bfloat16).astype(jnp.float32)
    scale = float(9 * channels) ** (-0.5)
    for tile in range(tiles):
        upstream[tile] = arriving[:, tile * 128 : (tile + 1) * 128]
        here, there, fired_here = upstream.at[tile], work.at[tile], fired.at[tile]
        dmembrane = jnp.zeros((count, 128), jnp.float32)
        for t in reversed(range(steps)):
            spot = pl.ds(t, count, stride=steps)
            f = fired_here[spot, :]
            slope = spike_slope * (f * (1.0 - f))
            dh = dmembrane + (here[spot, :] - threshold * dmembrane) * slope
            there[spot, :] = dh * scale
            dmembrane = leak_rate * dh
    raw = jnp.concatenate([work[tile] for tile in range(tiles)], axis=1).astype(jnp.bfloat16)
    raw_out[...] = raw
    if stage == 2:
        return
    padded[1 : height + 1, 1 : width + 1] = raw.reshape(height, width, group, lanes)
    for copy in copies:
        copy.wait()
    for k in list(range(1, sections)) + [0]:
        total = jnp.zeros((rows, lanes), jnp.float32)
        for offset in range(9):
            r, c = divmod(offset, 3)
            lhs = padded[2 - r : 2 - r + height, 2 - c : 2 - c + width].reshape(rows, lanes)
            row = pl.multiple_of(offset * channels + (scal[0] ^ k) * lanes, lanes)
            total += lax.dot_general(
                lhs,
                weights[pl.ds(row, lanes), :],
                (((1,), (1,)), ((), ())),
                preferred_element_type=jnp.float32,
            )
        if k == 0:
            own_out[...] = total + jnp.concatenate([upstream[tile] for tile in range(tiles)], axis=1)
        else:
            sends[k - 1][...] = total.astype(jnp.bfloat16)


def vmem(count):
    return [pl.BlockSpec(memory_space=VMEM)] * count


def run_forward(dims, last, scal, slices, sources, readout):
    sections, height, width, images, steps = dims
    rows, lanes = slices[0].shape
    ring, part_rows = sources[0].shape[:2]
    depth = parts * part_rows
    shapes = [
        jax.ShapeDtypeStruct((rows, lanes), jnp.bfloat16),
        jax.ShapeDtypeStruct((lanes // 128, rows, 128), jnp.float32),
    ]
    operands = [scal, *slices, *sources]
    extra = []
    if last:
        shapes.append(jax.ShapeDtypeStruct((images, readout.shape[1]), jnp.float32))
        operands.append(readout)
        extra = vmem(1)
    return pl.pallas_call(
        functools.partial(forward_kernel, dims, last),
        out_shape=shapes,
        in_specs=[pl.BlockSpec(memory_space=pltpu.SMEM)]
        + vmem(sections)
        + [pl.BlockSpec(memory_space=pltpu.HBM)] * len(sources)
        + extra,
        out_specs=vmem(len(shapes)),
        scratch_shapes=[
            VMEM((2 * ring * depth, lanes), jnp.bfloat16),
            VMEM((sections, height + 2, width + 2, images * steps, lanes), jnp.bfloat16),
            VMEM((lanes // 128, rows, 128), jnp.float32),
            pltpu.SemaphoreType.DMA((2 * parts, ring)),
        ],
        compiler_params=pltpu.CompilerParams(vmem_limit_bytes=LIMIT),
        cost_estimate=pl.CostEstimate(
            flops=2 * rows * lanes * 2 * ring * depth,
            bytes_accessed=4 * ring * depth * lanes,
            transcendentals=rows * lanes,
        ),
        name="forward_block",
    )(*operands)


def run_backward(dims, stage, classes, scal, heads, fired, sources):
    sections, height, width, images, steps = dims
    tiles, rows = fired.shape[:2]
    lanes = tiles * 128
    half = jax.ShapeDtypeStruct((rows, lanes), jnp.bfloat16)
    full = jax.ShapeDtypeStruct((rows, lanes), jnp.float32)
    operands = [scal, *heads, fired]
    specs = [pl.BlockSpec(memory_space=pltpu.SMEM)] + vmem(len(heads) + 1)
    work = [VMEM(fired.shape, jnp.float32), VMEM(fired.shape, jnp.float32)]
    cost = 0
    if stage < 2:
        ring, part_rows = sources[0].shape[:2]
        depth = parts * part_rows
        operands += list(sources)
        specs += [pl.BlockSpec(memory_space=pltpu.HBM)] * len(sources)
        shapes = [half, full] + [half] * (sections - 1)
        work = (
            [
                VMEM((2 * ring * depth, lanes), jnp.bfloat16),
                VMEM((height + 2, width + 2, images * steps, lanes), jnp.bfloat16),
            ]
            + work
            + [pltpu.SemaphoreType.DMA((2 * parts, ring))]
        )
        cost = 2 * ring * depth
    else:
        shapes = [half]
    return pl.pallas_call(
        functools.partial(backward_kernel, dims, stage, classes),
        out_shape=shapes,
        in_specs=specs,
        out_specs=vmem(len(shapes)),
        scratch_shapes=work,
        compiler_params=pltpu.CompilerParams(vmem_limit_bytes=LIMIT),
        cost_estimate=pl.CostEstimate(
            flops=2 * rows * lanes * cost + rows * lanes * 100,
            bytes_accessed=2 * cost * lanes + 8 * rows * lanes,
            transcendentals=0,
        ),
        name="backward_block",
    )(*operands)


def after(value, *earlier):
    return lax.optimization_barrier((value, *earlier))[0]


def hops(step, way, ring):
    if way > 0:
        pairs = [(i, i + 1) for i in range(step - 1, ring - 1)]
    else:
        pairs = [(i, i - 1) for i in range(1, ring - step + 1)]
    return [(2 * a + core, 2 * b + core) for a, b in pairs for core in range(2)]


def swap_core(value):
    count = lax.axis_size("dp")
    return lax.ppermute(value, "dp", [(i, i ^ 1) for i in range(count)])


def adam_update(weights, first_moment, second_moment, grad_total):
    new_first = beta_first * first_moment + (1.0 - beta_first) * grad_total
    new_second = beta_second * second_moment + (1.0 - beta_second) * grad_total * grad_total
    new_weights = weights - learn_rate * new_first / (jnp.sqrt(new_second) + adam_eps)
    return (new_weights, new_first, new_second)


def shards(spikes, labels, readout, weights, first_moment, second_moment):
    sections = lax.axis_size("section")
    devices = lax.axis_size("dp")
    ring = devices // 2
    s = lax.axis_index("section")
    d = lax.axis_index("dp")
    z, core = d // 2, d % 2
    images, steps, height, width, channels = spikes.shape
    group = images * steps
    rows = height * width * group
    lanes = channels // sections
    depth = weights.shape[1]
    classes = readout.shape[1]
    dims = (sections, height, width, images, steps)
    scal = jnp.stack([s, z, core]).astype(jnp.int32)

    def exchange(values):
        return [
            lax.ppermute(values[k], "section", [(i, i ^ (k + 1)) for i in range(sections)])
            for k in range(sections - 1)
        ]

    def columns(array, k):
        return lax.dynamic_slice_in_dim(array, (s ^ k) * lanes, lanes, 1)

    def pick(options, index):
        return lax.dynamic_index_in_dim(jnp.stack(options), index, 0, keepdims=False)

    part_rows = depth // parts
    pieces = []
    for h in range(parts):
        own = [
            columns(weights[0, h * part_rows : (h + 1) * part_rows], k).astype(jnp.bfloat16)
            for k in range(sections)
        ]
        if h:
            own = [own[0]] + [after(own[k], pieces[-1][k]) for k in range(1, sections)]
        pieces.append([own[0]] + exchange(own[1:]))
    field = spikes.transpose(2, 3, 0, 1, 4).reshape(rows, channels)
    slices = [columns(field, k) for k in range(sections)]
    padded_classes = -(-classes // 128) * 128
    readout_own = lax.dynamic_slice_in_dim(readout, s * lanes, lanes, 0)
    readout_own = jnp.pad(readout_own, ((0, 0), (0, padded_classes - classes)))

    inputs, results, sources = [slices], [], []

    def forward(b, *earlier):
        last = b == sections - 1
        slices = list(inputs[b])
        if earlier:
            slices[0] = after(slices[0], *earlier)
        results.append(run_forward(dims, last, scal, slices, sources[b], readout_own))
        if not last:
            out = results[b][0]
            inputs.append([out] + exchange([out] * (sections - 1)))

    done = {}
    for first in range(0, sections, 2):
        blocks = [b for b in (first, first + 1) if b < sections]
        for step in range(1, ring):
            for b in blocks:
                if first and step == 2 and b == blocks[-1]:
                    forward(first - 2, *done[first, 1])
                gates = []
                if step == 1 and len(done) >= 2:
                    gates += list(done.values())[-2]
                if (b, step) == (0, 1):
                    gates += [readout_own, *slices]
                if first and step == 2 and b == blocks[-1]:
                    gates += [results[first - 2][0]]
                up, down = done[b, step - 1] if step > 1 else [pick(pieces[0], s ^ b)] * 2
                if gates:
                    up, down = after(up, *gates), after(down, *gates)
                done[b, step] = (
                    lax.ppermute(up, "dp", hops(step, 1, ring)),
                    lax.ppermute(down, "dp", hops(step, -1, ring)),
                )
        for b in blocks:
            held = [pick(pieces[0], s ^ b)]
            for j in range(1, ring):
                held.append(jnp.where(z + j < ring, done[b, j][1], done[b, ring - j][0]))
            held = jnp.stack(held)
            sources.append([held, swap_core(held)])
        if first and len(results) == first - 1:
            forward(first - 1, *done[blocks[-1], max(1, ring - 2)])
    while len(results) < sections:
        b = len(results)
        forward(b, *(done[sections - 1, ring - 1] if b < sections - 1 else ()))
    result = results[-1]
    logits = result[2]
    heads = [logits] + exchange([logits] * (sections - 1))
    heads += [labels[:, None], readout_own]

    def ordered(parts):
        return jnp.concatenate([pick(parts, s ^ j) for j in range(sections)], axis=1)

    own_inputs = [
        pick([after(inputs[b][k], logits) for b in range(sections)], s) for k in range(sections)
    ]
    own_x = ordered(own_inputs)
    x_all = lax.all_gather(own_x, "dp")

    raws = [None] * sections
    for b in reversed(range(sections)):
        stage = 0 if b == sections - 1 else (2 if b == 0 else 1)
        result = run_backward(dims, stage, classes, scal, heads, results[b][1], sources[b])
        raws[b] = result[0]
        if b > 0:
            heads = [result[1]] + exchange(result[2:])

    sent = [pick(raws, s ^ k) for k in range(sections)]
    own_raw = ordered([sent[0]] + exchange(sent[1:]))
    start = d * depth
    channel = start % channels
    step = 1
    while channels % (2 * step) == 0 and depth % (2 * step) == 0:
        step *= 2
    spans = -(-(channels - step + depth) // channels)

    def cols_of(distances):
        pieces = [
            lax.dynamic_index_in_dim(
                x_all, lax.rem(z + j, ring) * 2 + place, 0, keepdims=False
            )
            for j in distances
            for place in (core, 1 - core)
        ]
        count = len(pieces)
        fields = jnp.stack(pieces).reshape(count, height, width, group, channels)
        fields = jnp.pad(fields, ((0, 0), (1, 1), (1, 1), (0, 0), (0, 0)))
        shifted = []
        for i in range(spans):
            offset = jnp.minimum(start // channels + i, 8)
            shifted.append(
                lax.dynamic_slice(
                    fields,
                    (0, offset // 3, offset % 3, 0, 0),
                    (count, height, width, group, channels),
                ).reshape(count * rows, channels)
            )
        return lax.dynamic_slice_in_dim(jnp.concatenate(shifted, axis=1), channel, depth, 1)

    def product(cols, raw_pieces):
        return lax.dot_general(
            cols,
            jnp.concatenate(raw_pieces),
            (((0,), (0,)), ((), ())),
            preferred_element_type=jnp.float32,
        )

    arrivals = [[0]]
    for step in range(1, ring):
        arrivals.append([step, ring - step] if 2 * step < ring else [None])

    def origins(step):
        if arrivals[step] == [None]:
            return [jnp.where(z + step < ring, step, ring - step)]
        return arrivals[step]

    early_cols = cols_of([j for step in range(ring - 1) for j in origins(step)])
    late_cols = cols_of(origins(ring - 1))
    up = down = own_raw
    early_raw = [own_raw, swap_core(own_raw)]
    for step in range(1, ring):
        if step == 2:
            up, down = after(up, early_cols, late_cols), after(down, early_cols, late_cols)
        up = lax.ppermute(up, "dp", hops(step, 1, ring))
        down = lax.ppermute(down, "dp", hops(step, -1, ring))
        if 2 * step < ring:
            landed = [down, up]
        else:
            landed = [jnp.where(z + step < ring, down, up)]
        if step < ring - 1:
            early_raw += [array for value in landed for array in (value, swap_core(value))]
    early = product(early_cols, early_raw)
    late = [array for value in landed for array in (value, swap_core(after(value, early)))]
    grad = early + product(late_cols, late)
    return adam_update(weights, first_moment, second_moment, grad[None])


def solution(mesh):
    return jax.shard_map(
        shards,
        mesh=mesh,
        in_specs=(
            P("dp", None, None, None, None),
            P("dp"),
            P(),
            P("section", "dp", None),
            P("section", "dp", None),
            P("section", "dp", None),
        ),
        out_specs=(P("section", "dp", None), P("section", "dp", None), P("section", "dp", None)),
        check_vma=False,
    )
```

```python
import functools
import jax
import jax.numpy as jnp
from jax import lax
from jax.experimental import pallas as pl
from jax.experimental.pallas import tpu as pltpu
from jax.sharding import PartitionSpec as P

leak_rate = 0.5
spike_slope = 4.0
threshold = 1.0
loss_scale = 4096.0
beta_first = 0.8
beta_second = 0.95
learn_rate = 0.5
adam_eps = 1e-08
HIGH = lax.Precision.HIGHEST
VMEM = pltpu.VMEM
LIMIT = 24 * 2**20


def slots_of(block, sections):
    return sorted({0, block, min(block + 1, sections - 1)})


def fetch_weights(block, sections, scal, sources, weights, sems):
    s, z, core = scal[0], scal[1], scal[2]
    slot = jnp.where(block == s, 0, jnp.where(block < s, block + 1, block))
    ring, depth = sources[0].shape[0], sources[0].shape[1]

    def copies(which_slot):
        result = []
        for which in range(2):
            source = sources[2 * which_slot + which]
            owner_core = core if which == 0 else 1 - core
            for j in range(ring):
                place = lax.rem(z + j, ring)
                row = pl.multiple_of((place * 2 + owner_core) * depth, depth)
                result.append(
                    pltpu.make_async_copy(
                        source.at[j], weights.at[pl.ds(row, depth), :], sems.at[which, j]
                    )
                )
        return result

    for index, candidate in enumerate(slots_of(block, sections)):

        @pl.when(slot == candidate)
        def _():
            for copy in copies(index):
                copy.start()

    return copies(0)


def forward_kernel(dims, block, scal, *refs):
    last = block == dims[0] - 1
    sections, height, width, images, steps = dims
    slices = refs[:sections]
    refs = refs[sections:]
    count = 2 * len(slots_of(block, sections))
    sources = refs[:count]
    refs = refs[count:]
    if last:
        readout, out, fired_out, logits_out, weights, padded, work, sems = refs
    else:
        out, fired_out, weights, padded, work, sems = refs
    copies = fetch_weights(block, sections, scal, sources, weights, sems)
    rows, lanes = slices[0].shape
    group = images * steps
    channels = sections * lanes
    padded[...] = jnp.zeros_like(padded)
    for k in range(sections):
        padded[scal[0] ^ k, 1 : height + 1, 1 : width + 1] = slices[k][...].reshape(
            height, width, group, lanes
        )
    for copy in copies:
        copy.wait()
    total = jnp.zeros((rows, lanes), jnp.float32)
    for offset in range(9):
        r, c = divmod(offset, 3)
        lhs = jnp.concatenate(
            [
                padded[j, r : r + height, c : c + width].reshape(rows, lanes)
                for j in range(sections)
            ],
            axis=1,
        )
        total += jnp.dot(
            lhs,
            weights[offset * channels : (offset + 1) * channels, :],
            preferred_element_type=jnp.float32,
        )
    scale = float(9 * channels) ** (-0.5)
    current = total * scale
    count = rows // steps
    tiles = lanes // 128
    for tile in range(tiles):
        here, there = work.at[tile], fired_out.at[tile]
        here[...] = current[:, tile * 128 : (tile + 1) * 128]
        membrane = jnp.zeros((count, 128), jnp.float32)
        for t in range(steps):
            spot = pl.ds(t, count, stride=steps)
            h = leak_rate * membrane + here[spot, :]
            fired = jax.nn.sigmoid(spike_slope * (h - threshold))
            membrane = h - threshold * fired
            there[spot, :] = fired
    fired = jnp.concatenate([fired_out[tile] for tile in range(tiles)], axis=1)
    result = (slices[0][...].astype(jnp.float32) + fired).astype(jnp.bfloat16)
    out[...] = result
    if last:
        summed = jnp.sum(
            result.astype(jnp.float32).reshape(height * width, group, lanes), axis=0
        )
        pooled = jnp.sum(summed.reshape(images, steps, lanes), axis=1) / float(
            height * width * steps
        )
        logits_out[...] = jnp.dot(
            pooled, readout[...], precision=HIGH, preferred_element_type=jnp.float32
        )


def backward_kernel(dims, block, classes, scal, *refs):
    stage = 0 if block == dims[0] - 1 else (2 if block == 0 else 1)
    sections, height, width, images, steps = dims
    if stage == 0:
        logit_parts = refs[:sections]
        labels, readout = refs[sections : sections + 2]
        refs = refs[sections + 2 :]
    else:
        own_part = refs[0]
        arrived = refs[1:sections]
        refs = refs[sections:]
    fired = refs[0]
    refs = refs[1:]
    if stage < 2:
        count = 2 * len(slots_of(block, sections))
        sources = refs[:count]
        refs = refs[count:]
        raw_out, own_out = refs[:2]
        sends = refs[2 : 1 + sections]
        weights, padded, upstream, work, sems = refs[1 + sections :]
        copies = fetch_weights(block, sections, scal, sources, weights, sems)
        padded[...] = jnp.zeros_like(padded)
    else:
        raw_out, upstream, work = refs
    tiles, rows = fired.shape[:2]
    lanes = tiles * 128
    group = images * steps
    channels = sections * lanes
    cells = height * width
    count = rows // steps
    if stage == 0:
        logits = logit_parts[0][...]
        for part in logit_parts[1:]:
            logits = logits + part[...]
        lane = lax.broadcasted_iota(jnp.int32, logits.shape, 1)
        logits = jnp.where(lane < classes, logits, -jnp.inf)
        exponent = jnp.exp(logits - jnp.max(logits, axis=-1, keepdims=True))
        probability = exponent / jnp.sum(exponent, axis=-1, keepdims=True)
        onehot = (labels[...] == lane).astype(jnp.float32)
        dlogits = loss_scale * (probability - onehot)
        dpooled = lax.dot_general(
            dlogits,
            readout[...],
            (((1,), (1,)), ((), ())),
            precision=HIGH,
            preferred_element_type=jnp.float32,
        )
        spread = (dpooled / float(cells * steps)).astype(jnp.bfloat16).astype(jnp.float32)
        arriving = jnp.broadcast_to(
            spread[None, :, None, :], (cells, images, steps, lanes)
        ).reshape(rows, lanes)
    else:
        arriving = own_part[...]
        for part in arrived:
            arriving = arriving + part[...].astype(jnp.float32)
        arriving = arriving.astype(jnp.bfloat16).astype(jnp.float32)
    scale = float(9 * channels) ** (-0.5)
    for tile in range(tiles):
        upstream[tile] = arriving[:, tile * 128 : (tile + 1) * 128]
        here, there, fired_here = upstream.at[tile], work.at[tile], fired.at[tile]
        dmembrane = jnp.zeros((count, 128), jnp.float32)
        for t in reversed(range(steps)):
            spot = pl.ds(t, count, stride=steps)
            f = fired_here[spot, :]
            slope = spike_slope * (f * (1.0 - f))
            dh = dmembrane + (here[spot, :] - threshold * dmembrane) * slope
            there[spot, :] = dh * scale
            dmembrane = leak_rate * dh
    raw = jnp.concatenate([work[tile] for tile in range(tiles)], axis=1).astype(jnp.bfloat16)
    raw_out[...] = raw
    if stage == 2:
        return
    padded[1 : height + 1, 1 : width + 1] = raw.reshape(height, width, group, lanes)
    for copy in copies:
        copy.wait()
    for k in list(range(1, sections)) + [0]:
        total = jnp.zeros((rows, lanes), jnp.float32)
        for offset in range(9):
            r, c = divmod(offset, 3)
            lhs = padded[2 - r : 2 - r + height, 2 - c : 2 - c + width].reshape(rows, lanes)
            row = pl.multiple_of(offset * channels + (scal[0] ^ k) * lanes, lanes)
            total += lax.dot_general(
                lhs,
                weights[pl.ds(row, lanes), :],
                (((1,), (1,)), ((), ())),
                preferred_element_type=jnp.float32,
            )
        if k == 0:
            own_out[...] = total + jnp.concatenate([upstream[tile] for tile in range(tiles)], axis=1)
        else:
            sends[k - 1][...] = total.astype(jnp.bfloat16)


def vmem(count):
    return [pl.BlockSpec(memory_space=VMEM)] * count


def run_forward(dims, block, scal, slices, sources, readout):
    sections, height, width, images, steps = dims
    rows, lanes = slices[0].shape
    ring, depth = sources[0].shape[:2]
    last = block == sections - 1
    shapes = [
        jax.ShapeDtypeStruct((rows, lanes), jnp.bfloat16),
        jax.ShapeDtypeStruct((lanes // 128, rows, 128), jnp.float32),
    ]
    operands = [scal, *slices, *sources]
    extra = []
    if last:
        shapes.append(jax.ShapeDtypeStruct((images, readout.shape[1]), jnp.float32))
        operands.append(readout)
        extra = vmem(1)
    return pl.pallas_call(
        functools.partial(forward_kernel, dims, block),
        out_shape=shapes,
        in_specs=[pl.BlockSpec(memory_space=pltpu.SMEM)]
        + vmem(sections)
        + [pl.BlockSpec(memory_space=pltpu.HBM)] * len(sources)
        + extra,
        out_specs=vmem(len(shapes)),
        scratch_shapes=[
            VMEM((2 * ring * depth, lanes), jnp.bfloat16),
            VMEM((sections, height + 2, width + 2, images * steps, lanes), jnp.bfloat16),
            VMEM((lanes // 128, rows, 128), jnp.float32),
            pltpu.SemaphoreType.DMA((2, ring)),
        ],
        compiler_params=pltpu.CompilerParams(vmem_limit_bytes=LIMIT),
        cost_estimate=pl.CostEstimate(
            flops=2 * rows * lanes * 2 * ring * depth,
            bytes_accessed=4 * ring * depth * lanes,
            transcendentals=rows * lanes,
        ),
        name="forward_block",
    )(*operands)


def run_backward(dims, block, classes, scal, heads, fired, sources):
    sections, height, width, images, steps = dims
    stage = 0 if block == sections - 1 else (2 if block == 0 else 1)
    tiles, rows = fired.shape[:2]
    lanes = tiles * 128
    half = jax.ShapeDtypeStruct((rows, lanes), jnp.bfloat16)
    full = jax.ShapeDtypeStruct((rows, lanes), jnp.float32)
    operands = [scal, *heads, fired]
    specs = [pl.BlockSpec(memory_space=pltpu.SMEM)] + vmem(len(heads) + 1)
    work = [VMEM(fired.shape, jnp.float32), VMEM(fired.shape, jnp.float32)]
    cost = 0
    if stage < 2:
        ring, depth = sources[0].shape[:2]
        operands += list(sources)
        specs += [pl.BlockSpec(memory_space=pltpu.HBM)] * len(sources)
        shapes = [half, full] + [half] * (sections - 1)
        work = (
            [
                VMEM((2 * ring * depth, lanes), jnp.bfloat16),
                VMEM((height + 2, width + 2, images * steps, lanes), jnp.bfloat16),
            ]
            + work
            + [pltpu.SemaphoreType.DMA((2, ring))]
        )
        cost = 2 * ring * depth
    else:
        shapes = [half]
    return pl.pallas_call(
        functools.partial(backward_kernel, dims, block, classes),
        out_shape=shapes,
        in_specs=specs,
        out_specs=vmem(len(shapes)),
        scratch_shapes=work,
        compiler_params=pltpu.CompilerParams(vmem_limit_bytes=LIMIT),
        cost_estimate=pl.CostEstimate(
            flops=2 * rows * lanes * cost + rows * lanes * 100,
            bytes_accessed=2 * cost * lanes + 8 * rows * lanes,
            transcendentals=0,
        ),
        name="backward_block",
    )(*operands)


def after(value, *earlier):
    return lax.optimization_barrier((value, *earlier))[0]


def hops(step, way, ring):
    if way > 0:
        pairs = [(i, i + 1) for i in range(step - 1, ring - 1)]
    else:
        pairs = [(i, i - 1) for i in range(1, ring - step + 1)]
    return [(2 * a + core, 2 * b + core) for a, b in pairs for core in range(2)]


def swap_core(value):
    count = lax.axis_size("dp")
    return lax.ppermute(value, "dp", [(i, i ^ 1) for i in range(count)])


def adam_update(weights, first_moment, second_moment, grad_total):
    new_first = beta_first * first_moment + (1.0 - beta_first) * grad_total
    new_second = beta_second * second_moment + (1.0 - beta_second) * grad_total * grad_total
    new_weights = weights - learn_rate * new_first / (jnp.sqrt(new_second) + adam_eps)
    return (new_weights, new_first, new_second)


def shards(spikes, labels, readout, weights, first_moment, second_moment):
    sections = lax.axis_size("section")
    devices = lax.axis_size("dp")
    ring = devices // 2
    s = lax.axis_index("section")
    d = lax.axis_index("dp")
    z, core = d // 2, d % 2
    images, steps, height, width, channels = spikes.shape
    group = images * steps
    rows = height * width * group
    lanes = channels // sections
    depth = weights.shape[1]
    classes = readout.shape[1]
    dims = (sections, height, width, images, steps)
    scal = jnp.stack([s, z, core]).astype(jnp.int32)

    def exchange(values):
        return [
            lax.ppermute(values[k], "section", [(i, i ^ (k + 1)) for i in range(sections)])
            for k in range(sections - 1)
        ]

    def columns(array, k):
        return lax.dynamic_slice_in_dim(array, (s ^ k) * lanes, lanes, 1)

    def pick(options, index):
        return lax.dynamic_index_in_dim(jnp.stack(options), index, 0, keepdims=False)

    pieces = [columns(weights[0], k).astype(jnp.bfloat16) for k in range(sections)]
    pieces = [pieces[0]] + exchange(pieces[1:])
    field = spikes.transpose(2, 3, 0, 1, 4).reshape(rows, channels)
    slices = [columns(field, k) for k in range(sections)]
    padded_classes = -(-classes // 128) * 128
    readout_own = lax.dynamic_slice_in_dim(readout, s * lanes, lanes, 0)
    readout_own = jnp.pad(readout_own, ((0, 0), (0, padded_classes - classes)))

    inputs, results, slots, done = [slices], [], {}, {}
    own_inputs = jnp.stack(slices)

    def holding(b):
        return [array for slot in slots_of(b, sections) for array in slots[slot]]

    def forward(b, *earlier):
        nonlocal own_inputs
        slices = list(inputs[b])
        if earlier:
            slices[0] = after(slices[0], *earlier)
        results.append(run_forward(dims, b, scal, slices, holding(b), readout_own))
        if b < sections - 1:
            out = results[b][0]
            inputs.append([out] + exchange([out] * (sections - 1)))
            own_inputs = jnp.where(s == b + 1, jnp.stack(inputs[b + 1]), own_inputs)

    def piece_of(slot):
        if slot == 0:
            return pieces[0]
        return pick(pieces, jnp.where(slot - 1 < s, slot - 1, slot) ^ s)

    groups = [[0]] + [[g, g + 1][: sections - g] for g in range(1, sections, 2)]
    order = []
    for number, members in enumerate(groups):
        units = [(slot, step) for step in range(1, ring) for slot in members]
        if number > 1 and len(order) > 1:
            order[-1:] = [units[0], order[-1]]
            units = units[1:]
        order += units
    for index, (slot, step) in enumerate(order):
        up, down = done[slot, step - 1] if step > 1 else [piece_of(slot)] * 2
        gates = []
        if index == 1:
            gates += [pieces[sections // 2]]
        if index == 2:
            gates += [readout_own, *slices, *pieces[1:]]
        if index > 2:
            gates += done[order[index - 2]]
        if slot > 2 and slot % 2 == 1 and step in (2, ring - 1):
            for b in range(len(results), slot - 3 + (1 if step == 2 else 2)):
                forward(b)
            gates += [results[-1][0]]
        if gates:
            up, down = after(up, *gates), after(down, *gates)
        done[slot, step] = [
            lax.ppermute(up, "dp", hops(step, 1, ring)),
            lax.ppermute(down, "dp", hops(step, -1, ring)),
        ]
        if step == ring - 1:
            held = [piece_of(slot)]
            for j in range(1, ring):
                held.append(
                    jnp.where(z + j < ring, done[slot, j][1], done[slot, ring - j][0])
                )
            held = jnp.stack(held)
            slots[slot] = [held, swap_core(held)]
    while len(results) < sections:
        b = len(results)
        forward(b, *(done[order[-1]] if b < sections - 1 else ()))
    result = results[-1]
    logits = result[2]
    heads = [logits] + exchange([logits] * (sections - 1))
    heads += [labels[:, None], readout_own]

    def ordered(parts):
        return jnp.concatenate([pick(parts, s ^ j) for j in range(sections)], axis=1)

    own_x = jnp.concatenate(
        [
            lax.dynamic_index_in_dim(own_inputs, s ^ j, 0, keepdims=False)
            for j in range(sections)
        ],
        axis=1,
    )
    x_all = lax.all_gather(own_x, "dp")

    raws = [None] * sections
    for b in reversed(range(sections)):
        held = holding(b) if b > 0 else None
        result = run_backward(dims, b, classes, scal, heads, results[b][1], held)
        raws[b] = result[0]
        if b > 0:
            heads = [result[1]] + exchange(result[2:])

    sent = [pick(raws, s ^ k) for k in range(sections)]
    own_raw = ordered([sent[0]] + exchange(sent[1:]))
    start = d * depth
    channel = start % channels
    step = 1
    while channels % (2 * step) == 0 and depth % (2 * step) == 0:
        step *= 2
    spans = -(-(channels - step + depth) // channels)

    fields = x_all.reshape(devices, height, width, group, channels)
    fields = jnp.pad(fields, ((0, 0), (1, 1), (1, 1), (0, 0), (0, 0)))
    shifted = []
    for i in range(spans):
        offset = jnp.minimum(start // channels + i, 8)
        shifted.append(
            lax.dynamic_slice(
                fields,
                (0, offset // 3, offset % 3, 0, 0),
                (devices, height, width, group, channels),
            ).reshape(devices * rows, channels)
        )
    cols = lax.dynamic_slice_in_dim(jnp.concatenate(shifted, axis=1), channel, depth, 1)

    def product(cols, raw):
        return lax.dot_general(
            cols,
            raw.reshape(-1, channels),
            (((0,), (0,)), ((), ())),
            preferred_element_type=jnp.float32,
        )

    def store(buffer, origin, value, valid=None):
        for place, piece in ((core, value), (1 - core, swap_core(value))):
            spot = lax.rem(origin + ring, ring) * 2 + place
            if valid is not None:
                piece = jnp.where(valid, piece, lax.dynamic_index_in_dim(buffer, spot, 0, False))
            buffer = lax.dynamic_update_index_in_dim(buffer, piece, spot, 0)
        return buffer

    up = down = own_raw
    early_raw = jnp.zeros((devices, rows, channels), jnp.bfloat16)
    early_raw = store(early_raw, z, own_raw)
    for step in range(1, ring):
        if step == 2:
            up, down = after(up, cols), after(down, cols)
        up = lax.ppermute(up, "dp", hops(step, 1, ring))
        down = lax.ppermute(down, "dp", hops(step, -1, ring))
        landed = jnp.where(z + step < ring, down, up)
        origin = jnp.where(z + step < ring, z + step, z - step)
        if step == ring - 1:
            continue
        if 2 * step < ring:
            early_raw = store(early_raw, z + step, down)
            early_raw = store(early_raw, z - step, up)
        elif 2 * step == ring:
            early_raw = store(early_raw, origin, landed)
        else:
            early_raw = store(early_raw, origin, landed, (z + step < ring) | (z >= step))
    early = product(cols, early_raw)
    late_raw = jnp.stack([landed, swap_core(after(landed, early))])
    late_cols = jnp.concatenate(
        [
            lax.dynamic_slice_in_dim(
                cols, (lax.rem(origin + ring, ring) * 2 + place) * rows, rows, 0
            )
            for place in (core, 1 - core)
        ]
    )
    grad = early + product(late_cols, late_raw)
    return adam_update(weights, first_moment, second_moment, grad[None])


def solution(mesh):
    return jax.shard_map(
        shards,
        mesh=mesh,
        in_specs=(
            P("dp", None, None, None, None),
            P("dp"),
            P(),
            P("section", "dp", None),
            P("section", "dp", None),
            P("section", "dp", None),
        ),
        out_specs=(P("section", "dp", None), P("section", "dp", None), P("section", "dp", None)),
        check_vma=False,
    )
```

```python
import functools
import jax
import jax.numpy as jnp
from jax import lax
from jax.experimental import pallas as pl
from jax.experimental.pallas import tpu as pltpu
from jax.sharding import PartitionSpec as P

leak_rate = 0.5
spike_slope = 4.0
threshold = 1.0
loss_scale = 4096.0
beta_first = 0.8
beta_second = 0.95
learn_rate = 0.5
adam_eps = 1e-08
HIGH = lax.Precision.HIGHEST
VMEM = pltpu.VMEM
LIMIT = 24 * 2**20


def slots_of(block, sections):
    return sorted({0, block, min(block + 1, sections - 1)})


def by_ring(slot):
    return slot > 0 and slot % 2 == 0


def fetch_weights(block, sections, scal, sources, weights, sems):
    s, z, core = scal[0], scal[1], scal[2]
    slot = jnp.where(block == s, 0, jnp.where(block < s, block + 1, block))
    slots = slots_of(block, sections)
    sources = list(sources)

    def copies(arrays):
        if len(arrays) == 1:
            return [pltpu.make_async_copy(arrays[0], weights, sems.at[0])]
        result = []
        for which, source in enumerate(arrays):
            ring, depth = source.shape[:2]
            owner_core = core if which == 0 else 1 - core
            for j in range(ring):
                place = lax.rem(z + j, ring)
                row = pl.multiple_of((place * 2 + owner_core) * depth, depth)
                result.append(
                    pltpu.make_async_copy(
                        source.at[j],
                        weights.at[pl.ds(row, depth), :],
                        sems.at[1 + which * ring + j],
                    )
                )
        return result

    choices = []
    for candidate in slots:
        count = 2 if by_ring(candidate) else 1
        choices.append((slot == candidate, sources[:count]))
        sources = sources[count:]

    for chosen, arrays in choices:

        @pl.when(chosen)
        def _():
            for copy in copies(arrays):
                copy.start()

    def wait():
        for chosen, arrays in choices:

            @pl.when(chosen)
            def _():
                for copy in copies(arrays):
                    copy.wait()

    return wait


def forward_kernel(dims, block, scal, *refs):
    last = block == dims[0] - 1
    sections, height, width, images, steps = dims
    slices = refs[:sections]
    refs = refs[sections:]
    count = sum(2 if by_ring(slot) else 1 for slot in slots_of(block, sections))
    sources = refs[:count]
    refs = refs[count:]
    if last:
        readout, out, fired_out, logits_out, weights, padded, work, sems = refs
    else:
        out, fired_out, weights, padded, work, sems = refs
    wait = fetch_weights(block, sections, scal, sources, weights, sems)
    rows, lanes = slices[0].shape
    group = images * steps
    channels = sections * lanes
    padded[...] = jnp.zeros_like(padded)
    for k in range(sections):
        padded[scal[0] ^ k, 1 : height + 1, 1 : width + 1] = slices[k][...].reshape(
            height, width, group, lanes
        )
    wait()
    total = jnp.zeros((rows, lanes), jnp.float32)
    for offset in range(9):
        r, c = divmod(offset, 3)
        lhs = jnp.concatenate(
            [
                padded[j, r : r + height, c : c + width].reshape(rows, lanes)
                for j in range(sections)
            ],
            axis=1,
        )
        total += jnp.dot(
            lhs,
            weights[offset * channels : (offset + 1) * channels, :],
            preferred_element_type=jnp.float32,
        )
    scale = float(9 * channels) ** (-0.5)
    current = total * scale
    count = rows // steps
    tiles = lanes // 128
    for tile in range(tiles):
        here, there = work.at[tile], fired_out.at[tile]
        here[...] = current[:, tile * 128 : (tile + 1) * 128]
        membrane = jnp.zeros((count, 128), jnp.float32)
        for t in range(steps):
            spot = pl.ds(t, count, stride=steps)
            h = leak_rate * membrane + here[spot, :]
            fired = jax.nn.sigmoid(spike_slope * (h - threshold))
            membrane = h - threshold * fired
            there[spot, :] = fired
    fired = jnp.concatenate([fired_out[tile] for tile in range(tiles)], axis=1)
    result = (slices[0][...].astype(jnp.float32) + fired).astype(jnp.bfloat16)
    out[...] = result
    if last:
        summed = jnp.sum(
            result.astype(jnp.float32).reshape(height * width, group, lanes), axis=0
        )
        pooled = jnp.sum(summed.reshape(images, steps, lanes), axis=1) / float(
            height * width * steps
        )
        logits_out[...] = jnp.dot(
            pooled, readout[...], precision=HIGH, preferred_element_type=jnp.float32
        )


def backward_kernel(dims, block, classes, scal, *refs):
    stage = 0 if block == dims[0] - 1 else (2 if block == 0 else 1)
    sections, height, width, images, steps = dims
    if stage == 0:
        logit_parts = refs[:sections]
        labels, readout = refs[sections : sections + 2]
        refs = refs[sections + 2 :]
    else:
        own_part = refs[0]
        arrived = refs[1:sections]
        refs = refs[sections:]
    fired = refs[0]
    refs = refs[1:]
    if stage < 2:
        count = sum(2 if by_ring(slot) else 1 for slot in slots_of(block, sections))
        sources = refs[:count]
        refs = refs[count:]
        raw_out, own_out = refs[:2]
        sends = refs[2 : 1 + sections]
        weights, padded, upstream, work, sems = refs[1 + sections :]
        wait = fetch_weights(block, sections, scal, sources, weights, sems)
        padded[...] = jnp.zeros_like(padded)
    else:
        raw_out, upstream, work = refs
    tiles, rows = fired.shape[:2]
    lanes = tiles * 128
    group = images * steps
    channels = sections * lanes
    cells = height * width
    count = rows // steps
    if stage == 0:
        logits = logit_parts[0][...]
        for part in logit_parts[1:]:
            logits = logits + part[...]
        lane = lax.broadcasted_iota(jnp.int32, logits.shape, 1)
        logits = jnp.where(lane < classes, logits, -jnp.inf)
        exponent = jnp.exp(logits - jnp.max(logits, axis=-1, keepdims=True))
        probability = exponent / jnp.sum(exponent, axis=-1, keepdims=True)
        onehot = (labels[...] == lane).astype(jnp.float32)
        dlogits = loss_scale * (probability - onehot)
        dpooled = lax.dot_general(
            dlogits,
            readout[...],
            (((1,), (1,)), ((), ())),
            precision=HIGH,
            preferred_element_type=jnp.float32,
        )
        spread = (dpooled / float(cells * steps)).astype(jnp.bfloat16).astype(jnp.float32)
        arriving = jnp.broadcast_to(
            spread[None, :, None, :], (cells, images, steps, lanes)
        ).reshape(rows, lanes)
    else:
        arriving = own_part[...]
        for part in arrived:
            arriving = arriving + part[...].astype(jnp.float32)
        arriving = arriving.astype(jnp.bfloat16).astype(jnp.float32)
    scale = float(9 * channels) ** (-0.5)
    for tile in range(tiles):
        upstream[tile] = arriving[:, tile * 128 : (tile + 1) * 128]
        here, there, fired_here = upstream.at[tile], work.at[tile], fired.at[tile]
        dmembrane = jnp.zeros((count, 128), jnp.float32)
        for t in reversed(range(steps)):
            spot = pl.ds(t, count, stride=steps)
            f = fired_here[spot, :]
            slope = spike_slope * (f * (1.0 - f))
            dh = dmembrane + (here[spot, :] - threshold * dmembrane) * slope
            there[spot, :] = dh * scale
            dmembrane = leak_rate * dh
    raw = jnp.concatenate([work[tile] for tile in range(tiles)], axis=1).astype(jnp.bfloat16)
    raw_out[...] = raw
    if stage == 2:
        return
    padded[1 : height + 1, 1 : width + 1] = raw.reshape(height, width, group, lanes)
    wait()
    for k in list(range(1, sections)) + [0]:
        total = jnp.zeros((rows, lanes), jnp.float32)
        for offset in range(9):
            r, c = divmod(offset, 3)
            lhs = padded[2 - r : 2 - r + height, 2 - c : 2 - c + width].reshape(rows, lanes)
            row = pl.multiple_of(offset * channels + (scal[0] ^ k) * lanes, lanes)
            total += lax.dot_general(
                lhs,
                weights[pl.ds(row, lanes), :],
                (((1,), (1,)), ((), ())),
                preferred_element_type=jnp.float32,
            )
        if k == 0:
            own_out[...] = total + jnp.concatenate([upstream[tile] for tile in range(tiles)], axis=1)
        else:
            sends[k - 1][...] = total.astype(jnp.bfloat16)


def vmem(count):
    return [pl.BlockSpec(memory_space=VMEM)] * count


def run_forward(dims, block, devices, scal, slices, sources, readout):
    sections, height, width, images, steps = dims
    rows, lanes = slices[0].shape
    depth = 9 * sections * lanes
    last = block == sections - 1
    shapes = [
        jax.ShapeDtypeStruct((rows, lanes), jnp.bfloat16),
        jax.ShapeDtypeStruct((lanes // 128, rows, 128), jnp.float32),
    ]
    operands = [scal, *slices, *sources]
    extra = []
    if last:
        shapes.append(jax.ShapeDtypeStruct((images, readout.shape[1]), jnp.float32))
        operands.append(readout)
        extra = vmem(1)
    return pl.pallas_call(
        functools.partial(forward_kernel, dims, block),
        out_shape=shapes,
        in_specs=[pl.BlockSpec(memory_space=pltpu.SMEM)]
        + vmem(sections)
        + [pl.BlockSpec(memory_space=pltpu.HBM)] * len(sources)
        + extra,
        out_specs=vmem(len(shapes)),
        scratch_shapes=[
            VMEM((depth, lanes), jnp.bfloat16),
            VMEM((sections, height + 2, width + 2, images * steps, lanes), jnp.bfloat16),
            VMEM((lanes // 128, rows, 128), jnp.float32),
            pltpu.SemaphoreType.DMA((1 + devices,)),
        ],
        compiler_params=pltpu.CompilerParams(vmem_limit_bytes=LIMIT),
        cost_estimate=pl.CostEstimate(
            flops=2 * rows * lanes * depth,
            bytes_accessed=2 * depth * lanes,
            transcendentals=rows * lanes,
        ),
        name="forward_block",
    )(*operands)


def run_backward(dims, block, devices, classes, scal, heads, fired, sources):
    sections, height, width, images, steps = dims
    stage = 0 if block == sections - 1 else (2 if block == 0 else 1)
    tiles, rows = fired.shape[:2]
    lanes = tiles * 128
    half = jax.ShapeDtypeStruct((rows, lanes), jnp.bfloat16)
    full = jax.ShapeDtypeStruct((rows, lanes), jnp.float32)
    operands = [scal, *heads, fired]
    specs = [pl.BlockSpec(memory_space=pltpu.SMEM)] + vmem(len(heads) + 1)
    work = [VMEM(fired.shape, jnp.float32), VMEM(fired.shape, jnp.float32)]
    cost = 0
    if stage < 2:
        depth = 9 * sections * lanes
        operands += list(sources)
        specs += [pl.BlockSpec(memory_space=pltpu.HBM)] * len(sources)
        shapes = [half, full] + [half] * (sections - 1)
        work = (
            [
                VMEM((depth, lanes), jnp.bfloat16),
                VMEM((height + 2, width + 2, images * steps, lanes), jnp.bfloat16),
            ]
            + work
            + [pltpu.SemaphoreType.DMA((1 + devices,))]
        )
        cost = depth
    else:
        shapes = [half]
    return pl.pallas_call(
        functools.partial(backward_kernel, dims, block, classes),
        out_shape=shapes,
        in_specs=specs,
        out_specs=vmem(len(shapes)),
        scratch_shapes=work,
        compiler_params=pltpu.CompilerParams(vmem_limit_bytes=LIMIT),
        cost_estimate=pl.CostEstimate(
            flops=2 * rows * lanes * cost + rows * lanes * 100,
            bytes_accessed=2 * cost * lanes + 8 * rows * lanes,
            transcendentals=0,
        ),
        name="backward_block",
    )(*operands)


def after(value, *earlier):
    return lax.optimization_barrier((value, *earlier))[0]


def hops(step, way, ring):
    if way > 0:
        pairs = [(i, i + 1) for i in range(step - 1, ring - 1)]
    else:
        pairs = [(i, i - 1) for i in range(1, ring - step + 1)]
    return [(2 * a + core, 2 * b + core) for a, b in pairs for core in range(2)]


def swap_core(value):
    count = lax.axis_size("dp")
    return lax.ppermute(value, "dp", [(i, i ^ 1) for i in range(count)])


def adam_update(weights, first_moment, second_moment, grad_total):
    new_first = beta_first * first_moment + (1.0 - beta_first) * grad_total
    new_second = beta_second * second_moment + (1.0 - beta_second) * grad_total * grad_total
    new_weights = weights - learn_rate * new_first / (jnp.sqrt(new_second) + adam_eps)
    return (new_weights, new_first, new_second)


def shards(spikes, labels, readout, weights, first_moment, second_moment):
    sections = lax.axis_size("section")
    devices = lax.axis_size("dp")
    ring = devices // 2
    s = lax.axis_index("section")
    d = lax.axis_index("dp")
    z, core = d // 2, d % 2
    images, steps, height, width, channels = spikes.shape
    group = images * steps
    rows = height * width * group
    lanes = channels // sections
    depth = weights.shape[1]
    classes = readout.shape[1]
    dims = (sections, height, width, images, steps)
    scal = jnp.stack([s, z, core]).astype(jnp.int32)

    def exchange(values):
        return [
            lax.ppermute(values[k], "section", [(i, i ^ (k + 1)) for i in range(sections)])
            for k in range(sections - 1)
        ]

    def columns(array, k):
        return lax.dynamic_slice_in_dim(array, (s ^ k) * lanes, lanes, 1)

    def pick(options, index):
        return lax.dynamic_index_in_dim(jnp.stack(options), index, 0, keepdims=False)

    pieces = [columns(weights[0], k).astype(jnp.bfloat16) for k in range(sections)]
    pieces = [pieces[0]] + exchange(pieces[1:])
    field = spikes.transpose(2, 3, 0, 1, 4).reshape(rows, channels)
    slices = [columns(field, k) for k in range(sections)]
    padded_classes = -(-classes // 128) * 128
    readout_own = lax.dynamic_slice_in_dim(readout, s * lanes, lanes, 0)
    readout_own = jnp.pad(readout_own, ((0, 0), (0, padded_classes - classes)))

    inputs, results, slots, done = [slices], [], {}, {}
    own_inputs = jnp.stack(slices)

    def holding(b):
        return [array for slot in slots_of(b, sections) for array in slots[slot]]

    def forward(b):
        nonlocal own_inputs
        results.append(run_forward(dims, b, devices, scal, inputs[b], holding(b), readout_own))
        if b < sections - 1:
            out = results[b][0]
            inputs.append([out] + exchange([out] * (sections - 1)))
            own_inputs = jnp.where(s == b + 1, jnp.stack(inputs[b + 1]), own_inputs)

    def piece_of(slot):
        if slot == 0:
            return pieces[0]
        return pick(pieces, jnp.where(slot - 1 < s, slot - 1, slot) ^ s)

    for slot in range(2, sections, 2):
        piece = piece_of(slot)
        gates = [readout_own, *slices] if slot == 2 else done[slot - 2, ring - 1]
        up = down = after(piece, *gates)
        for step in range(1, ring):
            up = lax.ppermute(up, "dp", hops(step, 1, ring))
            down = lax.ppermute(down, "dp", hops(step, -1, ring))
            done[slot, step] = [up, down]
        held = [piece]
        for j in range(1, ring):
            held.append(jnp.where(z + j < ring, done[slot, j][1], done[slot, ring - j][0]))
        held = jnp.stack(held)
        slots[slot] = [held, swap_core(held)]
    gates = []
    for slot in [0] + list(range(1, sections, 2)):
        piece = after(piece_of(slot), *gates) if gates else piece_of(slot)
        gathered = lax.all_gather(piece, "dp", axis=0, tiled=True)
        slots[slot] = [gathered]
        gates = [gathered] + done.get((2, 1) if slot == 0 else (slot + 1, ring - 1), [])
    for b in range(sections):
        forward(b)
    result = results[-1]
    logits = result[2]
    heads = [logits] + exchange([logits] * (sections - 1))
    heads += [labels[:, None], readout_own]

    def ordered(parts):
        return jnp.concatenate([pick(parts, s ^ j) for j in range(sections)], axis=1)

    own_x = jnp.concatenate(
        [
            lax.dynamic_index_in_dim(own_inputs, s ^ j, 0, keepdims=False)
            for j in range(sections)
        ],
        axis=1,
    )
    x_all = lax.all_gather(own_x, "dp")

    raws = [None] * sections
    for b in reversed(range(sections)):
        held = holding(b) if b > 0 else None
        result = run_backward(dims, b, devices, classes, scal, heads, results[b][1], held)
        raws[b] = result[0]
        if b > 0:
            heads = [result[1]] + exchange(result[2:])

    sent = [pick(raws, s ^ k) for k in range(sections)]
    own_raw = ordered([sent[0]] + exchange(sent[1:]))
    start = d * depth
    channel = start % channels
    step = 1
    while channels % (2 * step) == 0 and depth % (2 * step) == 0:
        step *= 2
    spans = -(-(channels - step + depth) // channels)

    fields = x_all.reshape(devices, height, width, group, channels)
    fields = jnp.pad(fields, ((0, 0), (1, 1), (1, 1), (0, 0), (0, 0)))
    shifted = []
    for i in range(spans):
        offset = jnp.minimum(start // channels + i, 8)
        shifted.append(
            lax.dynamic_slice(
                fields,
                (0, offset // 3, offset % 3, 0, 0),
                (devices, height, width, group, channels),
            ).reshape(devices * rows, channels)
        )
    cols = lax.dynamic_slice_in_dim(jnp.concatenate(shifted, axis=1), channel, depth, 1)

    raw_all = lax.all_gather(own_raw, "dp", axis=0, tiled=True)
    raw_all, cols = lax.optimization_barrier((raw_all, cols))
    grad = lax.dot_general(
        cols, raw_all, (((0,), (0,)), ((), ())), preferred_element_type=jnp.float32
    )
    return adam_update(weights, first_moment, second_moment, grad[None])


def solution(mesh):
    return jax.shard_map(
        shards,
        mesh=mesh,
        in_specs=(
            P("dp", None, None, None, None),
            P("dp"),
            P(),
            P("section", "dp", None),
            P("section", "dp", None),
            P("section", "dp", None),
        ),
        out_specs=(P("section", "dp", None), P("section", "dp", None), P("section", "dp", None)),
        check_vma=False,
    )
```

```python
import functools
import jax
import jax.numpy as jnp
from jax import lax
from jax.experimental import pallas as pl
from jax.experimental.pallas import tpu as pltpu
from jax.sharding import PartitionSpec as P

leak_rate = 0.5
spike_slope = 4.0
threshold = 1.0
loss_scale = 4096.0
beta_first = 0.8
beta_second = 0.95
learn_rate = 0.5
adam_eps = 1e-08
HIGH = lax.Precision.HIGHEST
VMEM = pltpu.VMEM
LIMIT = 24 * 2**20


def slots_of(block, sections):
    return sorted({0, block, min(block + 1, sections - 1)})


def by_ring(slot):
    return slot > 0 and slot % 2 == 0


def fetch_weights(block, sections, scal, sources, weights, sems):
    s, z, core = scal[0], scal[1], scal[2]
    slot = jnp.where(block == s, 0, jnp.where(block < s, block + 1, block))
    slots = slots_of(block, sections)
    sources = list(sources)

    def copies(arrays, only=None):
        result = []
        if len(arrays) == 1:
            rows = weights.shape[0] // 9
            for offset in range(9) if only is None else [only]:
                part = pl.ds(offset * rows, rows)
                result.append(
                    pltpu.make_async_copy(
                        arrays[0].at[part, :], weights.at[part, :], sems.at[offset]
                    )
                )
            return result
        for which, source in enumerate(arrays):
            ring, depth = source.shape[:2]
            owner_core = core if which == 0 else 1 - core
            for j in range(ring):
                place = lax.rem(z + j, ring)
                row = pl.multiple_of((place * 2 + owner_core) * depth, depth)
                result.append(
                    pltpu.make_async_copy(
                        source.at[j],
                        weights.at[pl.ds(row, depth), :],
                        sems.at[9 + which * ring + j],
                    )
                )
        return result

    choices = []
    for candidate in slots:
        count = 2 if by_ring(candidate) else 1
        choices.append((slot == candidate, sources[:count]))
        sources = sources[count:]

    for chosen, arrays in choices:

        @pl.when(chosen)
        def _():
            for copy in copies(arrays):
                copy.start()

    def wait(offset):
        for chosen, arrays in choices:
            if len(arrays) == 1 or offset == 0:

                @pl.when(chosen)
                def _():
                    for copy in copies(arrays, offset if len(arrays) == 1 else None):
                        copy.wait()

    return wait


def forward_kernel(dims, block, scal, *refs):
    last = block == dims[0] - 1
    sections, height, width, images, steps = dims
    slices = refs[:sections]
    refs = refs[sections:]
    count = sum(2 if by_ring(slot) else 1 for slot in slots_of(block, sections))
    sources = refs[:count]
    refs = refs[count:]
    if last:
        readout, out, fired_out, logits_out, weights, padded, work, sems = refs
    else:
        out, fired_out, weights, padded, work, sems = refs
    wait = fetch_weights(block, sections, scal, sources, weights, sems)
    rows, lanes = slices[0].shape
    group = images * steps
    channels = sections * lanes
    padded[...] = jnp.zeros_like(padded)
    for k in range(sections):
        padded[scal[0] ^ k, 1 : height + 1, 1 : width + 1] = slices[k][...].reshape(
            height, width, group, lanes
        )
    total = jnp.zeros((rows, lanes), jnp.float32)
    for offset in range(9):
        r, c = divmod(offset, 3)
        wait(offset)
        lhs = jnp.concatenate(
            [
                padded[j, r : r + height, c : c + width].reshape(rows, lanes)
                for j in range(sections)
            ],
            axis=1,
        )
        total += jnp.dot(
            lhs,
            weights[offset * channels : (offset + 1) * channels, :],
            preferred_element_type=jnp.float32,
        )
    scale = float(9 * channels) ** (-0.5)
    current = total * scale
    count = rows // steps
    tiles = lanes // 128
    for tile in range(tiles):
        here, there = work.at[tile], fired_out.at[tile]
        here[...] = current[:, tile * 128 : (tile + 1) * 128]
        membrane = jnp.zeros((count, 128), jnp.float32)
        for t in range(steps):
            spot = pl.ds(t, count, stride=steps)
            h = leak_rate * membrane + here[spot, :]
            fired = jax.nn.sigmoid(spike_slope * (h - threshold))
            membrane = h - threshold * fired
            there[spot, :] = fired
    fired = jnp.concatenate([fired_out[tile] for tile in range(tiles)], axis=1)
    result = (slices[0][...].astype(jnp.float32) + fired).astype(jnp.bfloat16)
    out[...] = result
    if last:
        summed = jnp.sum(
            result.astype(jnp.float32).reshape(height * width, group, lanes), axis=0
        )
        pooled = jnp.sum(summed.reshape(images, steps, lanes), axis=1) / float(
            height * width * steps
        )
        logits_out[...] = jnp.dot(
            pooled, readout[...], precision=HIGH, preferred_element_type=jnp.float32
        )


def backward_kernel(dims, block, classes, scal, *refs):
    stage = 0 if block == dims[0] - 1 else (2 if block == 0 else 1)
    sections, height, width, images, steps = dims
    if stage == 0:
        logit_parts = refs[:sections]
        labels, readout = refs[sections : sections + 2]
        refs = refs[sections + 2 :]
    else:
        own_part = refs[0]
        arrived = refs[1:sections]
        refs = refs[sections:]
    fired = refs[0]
    refs = refs[1:]
    if stage < 2:
        count = sum(2 if by_ring(slot) else 1 for slot in slots_of(block, sections))
        sources = refs[:count]
        refs = refs[count:]
        raw_out, own_out = refs[:2]
        sends = refs[2 : 1 + sections]
        weights, padded, upstream, work, sems = refs[1 + sections :]
        wait = fetch_weights(block, sections, scal, sources, weights, sems)
        padded[...] = jnp.zeros_like(padded)
    else:
        raw_out, upstream, work = refs
    tiles, rows = fired.shape[:2]
    lanes = tiles * 128
    group = images * steps
    channels = sections * lanes
    cells = height * width
    count = rows // steps
    if stage == 0:
        logits = logit_parts[0][...]
        for part in logit_parts[1:]:
            logits = logits + part[...]
        lane = lax.broadcasted_iota(jnp.int32, logits.shape, 1)
        logits = jnp.where(lane < classes, logits, -jnp.inf)
        exponent = jnp.exp(logits - jnp.max(logits, axis=-1, keepdims=True))
        probability = exponent / jnp.sum(exponent, axis=-1, keepdims=True)
        onehot = (labels[...] == lane).astype(jnp.float32)
        dlogits = loss_scale * (probability - onehot)
        dpooled = lax.dot_general(
            dlogits,
            readout[...],
            (((1,), (1,)), ((), ())),
            precision=HIGH,
            preferred_element_type=jnp.float32,
        )
        spread = (dpooled / float(cells * steps)).astype(jnp.bfloat16).astype(jnp.float32)
        arriving = jnp.broadcast_to(
            spread[None, :, None, :], (cells, images, steps, lanes)
        ).reshape(rows, lanes)
    else:
        arriving = own_part[...]
        for part in arrived:
            arriving = arriving + part[...].astype(jnp.float32)
        arriving = arriving.astype(jnp.bfloat16).astype(jnp.float32)
    scale = float(9 * channels) ** (-0.5)
    for tile in range(tiles):
        upstream[tile] = arriving[:, tile * 128 : (tile + 1) * 128]
        here, there, fired_here = upstream.at[tile], work.at[tile], fired.at[tile]
        dmembrane = jnp.zeros((count, 128), jnp.float32)
        for t in reversed(range(steps)):
            spot = pl.ds(t, count, stride=steps)
            f = fired_here[spot, :]
            slope = spike_slope * (f * (1.0 - f))
            dh = dmembrane + (here[spot, :] - threshold * dmembrane) * slope
            there[spot, :] = dh * scale
            dmembrane = leak_rate * dh
    raw = jnp.concatenate([work[tile] for tile in range(tiles)], axis=1).astype(jnp.bfloat16)
    raw_out[...] = raw
    if stage == 2:
        return
    padded[1 : height + 1, 1 : width + 1] = raw.reshape(height, width, group, lanes)
    for k in list(range(1, sections)) + [0]:
        total = jnp.zeros((rows, lanes), jnp.float32)
        for offset in range(9):
            r, c = divmod(offset, 3)
            if k == 1:
                wait(offset)
            lhs = padded[2 - r : 2 - r + height, 2 - c : 2 - c + width].reshape(rows, lanes)
            row = pl.multiple_of(offset * channels + (scal[0] ^ k) * lanes, lanes)
            total += lax.dot_general(
                lhs,
                weights[pl.ds(row, lanes), :],
                (((1,), (1,)), ((), ())),
                preferred_element_type=jnp.float32,
            )
        if k == 0:
            own_out[...] = total + jnp.concatenate([upstream[tile] for tile in range(tiles)], axis=1)
        else:
            sends[k - 1][...] = total.astype(jnp.bfloat16)


def stay(arrays):
    return [pltpu.with_memory_space_constraint(array, pltpu.HBM) for array in arrays]


def vmem(count):
    return [pl.BlockSpec(memory_space=VMEM)] * count


def run_forward(dims, block, devices, scal, slices, sources, readout):
    sections, height, width, images, steps = dims
    rows, lanes = slices[0].shape
    depth = 9 * sections * lanes
    last = block == sections - 1
    shapes = [
        jax.ShapeDtypeStruct((rows, lanes), jnp.bfloat16),
        jax.ShapeDtypeStruct((lanes // 128, rows, 128), jnp.float32),
    ]
    operands = [scal, *slices, *stay(sources)]
    extra = []
    if last:
        shapes.append(jax.ShapeDtypeStruct((images, readout.shape[1]), jnp.float32))
        operands.append(readout)
        extra = vmem(1)
    return pl.pallas_call(
        functools.partial(forward_kernel, dims, block),
        out_shape=shapes,
        in_specs=[pl.BlockSpec(memory_space=pltpu.SMEM)]
        + vmem(sections)
        + [pl.BlockSpec(memory_space=pltpu.HBM)] * len(sources)
        + extra,
        out_specs=vmem(len(shapes)),
        scratch_shapes=[
            VMEM((depth, lanes), jnp.bfloat16),
            VMEM((sections, height + 2, width + 2, images * steps, lanes), jnp.bfloat16),
            VMEM((lanes // 128, rows, 128), jnp.float32),
            pltpu.SemaphoreType.DMA((9 + devices,)),
        ],
        compiler_params=pltpu.CompilerParams(vmem_limit_bytes=LIMIT),
        cost_estimate=pl.CostEstimate(
            flops=2 * rows * lanes * depth,
            bytes_accessed=2 * depth * lanes,
            transcendentals=rows * lanes,
        ),
        name="forward_block",
    )(*operands)


def run_backward(dims, block, devices, classes, scal, heads, fired, sources):
    sections, height, width, images, steps = dims
    stage = 0 if block == sections - 1 else (2 if block == 0 else 1)
    tiles, rows = fired.shape[:2]
    lanes = tiles * 128
    half = jax.ShapeDtypeStruct((rows, lanes), jnp.bfloat16)
    full = jax.ShapeDtypeStruct((rows, lanes), jnp.float32)
    operands = [scal, *heads, fired]
    specs = [pl.BlockSpec(memory_space=pltpu.SMEM)] + vmem(len(heads) + 1)
    work = [VMEM(fired.shape, jnp.float32), VMEM(fired.shape, jnp.float32)]
    cost = 0
    if stage < 2:
        depth = 9 * sections * lanes
        operands += stay(sources)
        specs += [pl.BlockSpec(memory_space=pltpu.HBM)] * len(sources)
        shapes = [half, full] + [half] * (sections - 1)
        work = (
            [
                VMEM((depth, lanes), jnp.bfloat16),
                VMEM((height + 2, width + 2, images * steps, lanes), jnp.bfloat16),
            ]
            + work
            + [pltpu.SemaphoreType.DMA((9 + devices,))]
        )
        cost = depth
    else:
        shapes = [half]
    return pl.pallas_call(
        functools.partial(backward_kernel, dims, block, classes),
        out_shape=shapes,
        in_specs=specs,
        out_specs=vmem(len(shapes)),
        scratch_shapes=work,
        compiler_params=pltpu.CompilerParams(vmem_limit_bytes=LIMIT),
        cost_estimate=pl.CostEstimate(
            flops=2 * rows * lanes * cost + rows * lanes * 100,
            bytes_accessed=2 * cost * lanes + 8 * rows * lanes,
            transcendentals=0,
        ),
        name="backward_block",
    )(*operands)


def after(value, *earlier):
    return lax.optimization_barrier((value, *earlier))[0]


def hops(step, way, ring):
    if way > 0:
        pairs = [(i, i + 1) for i in range(step - 1, ring - 1)]
    else:
        pairs = [(i, i - 1) for i in range(1, ring - step + 1)]
    return [(2 * a + core, 2 * b + core) for a, b in pairs for core in range(2)]


def swap_core(value):
    count = lax.axis_size("dp")
    return lax.ppermute(value, "dp", [(i, i ^ 1) for i in range(count)])


def adam_update(weights, first_moment, second_moment, grad_total):
    new_first = beta_first * first_moment + (1.0 - beta_first) * grad_total
    new_second = beta_second * second_moment + (1.0 - beta_second) * grad_total * grad_total
    new_weights = weights - learn_rate * new_first / (jnp.sqrt(new_second) + adam_eps)
    return (new_weights, new_first, new_second)


def shards(spikes, labels, readout, weights, first_moment, second_moment):
    sections = lax.axis_size("section")
    devices = lax.axis_size("dp")
    ring = devices // 2
    s = lax.axis_index("section")
    d = lax.axis_index("dp")
    z, core = d // 2, d % 2
    images, steps, height, width, channels = spikes.shape
    group = images * steps
    rows = height * width * group
    lanes = channels // sections
    depth = weights.shape[1]
    classes = readout.shape[1]
    dims = (sections, height, width, images, steps)
    scal = jnp.stack([s, z, core]).astype(jnp.int32)

    def exchange(values):
        return [
            lax.ppermute(values[k], "section", [(i, i ^ (k + 1)) for i in range(sections)])
            for k in range(sections - 1)
        ]

    def columns(array, k):
        return lax.dynamic_slice_in_dim(array, (s ^ k) * lanes, lanes, 1)

    def pick(options, index):
        return lax.dynamic_index_in_dim(jnp.stack(options), index, 0, keepdims=False)

    pieces = [columns(weights[0], k).astype(jnp.bfloat16) for k in range(sections)]
    pieces = [pieces[0]] + exchange(pieces[1:])
    field = spikes.transpose(2, 3, 0, 1, 4).reshape(rows, channels)
    slices = [columns(field, k) for k in range(sections)]
    padded_classes = -(-classes // 128) * 128
    readout_own = lax.dynamic_slice_in_dim(readout, s * lanes, lanes, 0)
    readout_own = jnp.pad(readout_own, ((0, 0), (0, padded_classes - classes)))

    inputs, results, slots, done = [slices], [], {}, {}
    own_inputs = jnp.stack(slices)

    def holding(b):
        return [array for slot in slots_of(b, sections) for array in slots[slot]]

    def forward(b):
        nonlocal own_inputs
        results.append(run_forward(dims, b, devices, scal, inputs[b], holding(b), readout_own))
        if b < sections - 1:
            out = results[b][0]
            inputs.append([out] + exchange([out] * (sections - 1)))
            own_inputs = jnp.where(s == b + 1, jnp.stack(inputs[b + 1]), own_inputs)

    def piece_of(slot):
        if slot == 0:
            return pieces[0]
        return pick(pieces, jnp.where(slot - 1 < s, slot - 1, slot) ^ s)

    for slot in range(2, sections, 2):
        piece = piece_of(slot)
        gates = [readout_own, *slices] if slot == 2 else done[slot - 2, ring - 1]
        up = down = after(piece, *gates)
        for step in range(1, ring):
            up = lax.ppermute(up, "dp", hops(step, 1, ring))
            down = lax.ppermute(down, "dp", hops(step, -1, ring))
            done[slot, step] = [up, down]
        held = [piece]
        for j in range(1, ring):
            held.append(jnp.where(z + j < ring, done[slot, j][1], done[slot, ring - j][0]))
        held = jnp.stack(held)
        slots[slot] = [held, swap_core(held)]
    gates = []
    for slot in [0] + list(range(1, sections, 2)):
        piece = after(piece_of(slot), *gates) if gates else piece_of(slot)
        gathered = lax.all_gather(piece, "dp", axis=0, tiled=True)
        slots[slot] = [gathered]
        gates = [gathered] + done.get((2, 1) if slot == 0 else (slot + 1, max(1, ring - 2)), [])
    for b in range(sections):
        forward(b)
    result = results[-1]
    logits = result[2]
    heads = [logits] + exchange([logits] * (sections - 1))
    heads += [labels[:, None], readout_own]

    def ordered(parts):
        return jnp.concatenate([pick(parts, s ^ j) for j in range(sections)], axis=1)

    own_x = jnp.concatenate(
        [
            lax.dynamic_index_in_dim(own_inputs, s ^ j, 0, keepdims=False)
            for j in range(sections)
        ],
        axis=1,
    )
    x_all = lax.all_gather(own_x, "dp")

    raws = [None] * sections
    for b in reversed(range(sections)):
        held = holding(b) if b > 0 else None
        result = run_backward(dims, b, devices, classes, scal, heads, results[b][1], held)
        raws[b] = result[0]
        if b > 0:
            heads = [result[1]] + exchange(result[2:])

    sent = [pick(raws, s ^ k) for k in range(sections)]
    own_raw = ordered([sent[0]] + exchange(sent[1:]))
    start = d * depth
    channel = start % channels
    step = 1
    while channels % (2 * step) == 0 and depth % (2 * step) == 0:
        step *= 2
    spans = -(-(channels - step + depth) // channels)

    fields = x_all.reshape(devices, height, width, group, channels)
    fields = jnp.pad(fields, ((0, 0), (1, 1), (1, 1), (0, 0), (0, 0)))
    shifted = []
    for i in range(spans):
        offset = jnp.minimum(start // channels + i, 8)
        shifted.append(
            lax.dynamic_slice(
                fields,
                (0, offset // 3, offset % 3, 0, 0),
                (devices, height, width, group, channels),
            ).reshape(devices * rows, channels)
        )
    cols = lax.dynamic_slice_in_dim(jnp.concatenate(shifted, axis=1), channel, depth, 1)

    raw_all = lax.all_gather(own_raw, "dp", axis=0, tiled=True)
    raw_all, cols = lax.optimization_barrier((raw_all, cols))
    grad = lax.dot_general(
        cols, raw_all, (((0,), (0,)), ((), ())), preferred_element_type=jnp.float32
    )
    return adam_update(weights, first_moment, second_moment, grad[None])


def solution(mesh):
    return jax.shard_map(
        shards,
        mesh=mesh,
        in_specs=(
            P("dp", None, None, None, None),
            P("dp"),
            P(),
            P("section", "dp", None),
            P("section", "dp", None),
            P("section", "dp", None),
        ),
        out_specs=(P("section", "dp", None), P("section", "dp", None), P("section", "dp", None)),
        check_vma=False,
    )
```

```python
import functools
import jax
import jax.numpy as jnp
from jax import lax
from jax.experimental import pallas as pl
from jax.experimental.pallas import tpu as pltpu
from jax.sharding import PartitionSpec as P

leak_rate = 0.5
spike_slope = 4.0
threshold = 1.0
loss_scale = 4096.0
beta_first = 0.8
beta_second = 0.95
learn_rate = 0.5
adam_eps = 1e-08
HIGH = lax.Precision.HIGHEST
VMEM = pltpu.VMEM
LIMIT = 24 * 2**20


def slots_of(block, sections):
    return sorted({0, block, min(block + 1, sections - 1)})


def by_ring(slot):
    return slot > 0 and slot % 2 == 0


def fetch_weights(block, sections, scal, sources, weights, sem):
    s, z, core = scal[0], scal[1], scal[2]
    slot = jnp.where(block == s, 0, jnp.where(block < s, block + 1, block))
    slots = slots_of(block, sections)
    sources = list(sources)

    def start(arrays):
        if len(arrays) == 1:
            pltpu.make_async_copy(arrays[0], weights, sem).start()
            return
        for which, source in enumerate(arrays):
            ring, depth = source.shape[:2]
            owner_core = core if which == 0 else 1 - core
            for j in range(ring):
                place = lax.rem(z + j, ring)
                row = pl.multiple_of((place * 2 + owner_core) * depth, depth)
                pltpu.make_async_copy(
                    source.at[j], weights.at[pl.ds(row, depth), :], sem
                ).start()

    for candidate in slots:
        count = 2 if by_ring(candidate) else 1
        arrays, sources = sources[:count], sources[count:]

        @pl.when(slot == candidate)
        def _():
            start(arrays)

    return lambda: pltpu.make_async_copy(weights, weights, sem).wait()


def forward_kernel(dims, block, scal, *refs):
    last = block == dims[0] - 1
    sections, height, width, images, steps = dims
    slices = refs[:sections]
    refs = refs[sections:]
    count = sum(2 if by_ring(slot) else 1 for slot in slots_of(block, sections))
    sources = refs[:count]
    refs = refs[count:]
    if last:
        readout, out, fired_out, logits_out, weights, padded, work, sem = refs
    else:
        out, fired_out, weights, padded, work, sem = refs
    wait = fetch_weights(block, sections, scal, sources, weights, sem)
    rows, lanes = slices[0].shape
    group = images * steps
    channels = sections * lanes
    padded[...] = jnp.zeros_like(padded)
    for k in range(sections):
        padded[scal[0] ^ k, 1 : height + 1, 1 : width + 1] = slices[k][...].reshape(
            height, width, group, lanes
        )
    wait()
    total = jnp.zeros((rows, lanes), jnp.float32)
    for offset in range(9):
        r, c = divmod(offset, 3)
        lhs = jnp.concatenate(
            [
                padded[j, r : r + height, c : c + width].reshape(rows, lanes)
                for j in range(sections)
            ],
            axis=1,
        )
        total += jnp.dot(
            lhs,
            weights[offset * channels : (offset + 1) * channels, :],
            preferred_element_type=jnp.float32,
        )
    scale = float(9 * channels) ** (-0.5)
    current = total * scale
    count = rows // steps
    tiles = lanes // 128
    for tile in range(tiles):
        here, there = work.at[tile], fired_out.at[tile]
        here[...] = current[:, tile * 128 : (tile + 1) * 128]
        membrane = jnp.zeros((count, 128), jnp.float32)
        for t in range(steps):
            spot = pl.ds(t, count, stride=steps)
            h = leak_rate * membrane + here[spot, :]
            fired = jax.nn.sigmoid(spike_slope * (h - threshold))
            membrane = h - threshold * fired
            there[spot, :] = fired
    fired = jnp.concatenate([fired_out[tile] for tile in range(tiles)], axis=1)
    result = (slices[0][...].astype(jnp.float32) + fired).astype(jnp.bfloat16)
    out[...] = result
    if last:
        summed = jnp.sum(
            result.astype(jnp.float32).reshape(height * width, group, lanes), axis=0
        )
        pooled = jnp.sum(summed.reshape(images, steps, lanes), axis=1) / float(
            height * width * steps
        )
        logits_out[...] = jnp.dot(
            pooled, readout[...], precision=HIGH, preferred_element_type=jnp.float32
        )


def backward_kernel(dims, block, classes, scal, *refs):
    stage = 0 if block == dims[0] - 1 else (2 if block == 0 else 1)
    sections, height, width, images, steps = dims
    if stage == 0:
        logit_parts = refs[:sections]
        labels, readout = refs[sections : sections + 2]
        refs = refs[sections + 2 :]
    else:
        own_part = refs[0]
        arrived = refs[1:sections]
        refs = refs[sections:]
    fired = refs[0]
    refs = refs[1:]
    if stage < 2:
        count = sum(2 if by_ring(slot) else 1 for slot in slots_of(block, sections))
        sources = refs[:count]
        refs = refs[count:]
        raw_out, own_out = refs[:2]
        sends = refs[2 : 1 + sections]
        weights, padded, upstream, work, sem = refs[1 + sections :]
        wait = fetch_weights(block, sections, scal, sources, weights, sem)
        padded[...] = jnp.zeros_like(padded)
    else:
        raw_out, upstream, work = refs
    tiles, rows = fired.shape[:2]
    lanes = tiles * 128
    group = images * steps
    channels = sections * lanes
    cells = height * width
    count = rows // steps
    if stage == 0:
        logits = logit_parts[0][...]
        for part in logit_parts[1:]:
            logits = logits + part[...]
        lane = lax.broadcasted_iota(jnp.int32, logits.shape, 1)
        logits = jnp.where(lane < classes, logits, -jnp.inf)
        exponent = jnp.exp(logits - jnp.max(logits, axis=-1, keepdims=True))
        probability = exponent / jnp.sum(exponent, axis=-1, keepdims=True)
        onehot = (labels[...] == lane).astype(jnp.float32)
        dlogits = loss_scale * (probability - onehot)
        dpooled = lax.dot_general(
            dlogits,
            readout[...],
            (((1,), (1,)), ((), ())),
            precision=HIGH,
            preferred_element_type=jnp.float32,
        )
        spread = (dpooled / float(cells * steps)).astype(jnp.bfloat16).astype(jnp.float32)
        arriving = jnp.broadcast_to(
            spread[None, :, None, :], (cells, images, steps, lanes)
        ).reshape(rows, lanes)
    else:
        arriving = own_part[...]
        for part in arrived:
            arriving = arriving + part[...].astype(jnp.float32)
        arriving = arriving.astype(jnp.bfloat16).astype(jnp.float32)
    scale = float(9 * channels) ** (-0.5)
    for tile in range(tiles):
        upstream[tile] = arriving[:, tile * 128 : (tile + 1) * 128]
        here, there, fired_here = upstream.at[tile], work.at[tile], fired.at[tile]
        dmembrane = jnp.zeros((count, 128), jnp.float32)
        for t in reversed(range(steps)):
            spot = pl.ds(t, count, stride=steps)
            f = fired_here[spot, :]
            slope = spike_slope * (f * (1.0 - f))
            dh = dmembrane + (here[spot, :] - threshold * dmembrane) * slope
            there[spot, :] = dh * scale
            dmembrane = leak_rate * dh
    raw = jnp.concatenate([work[tile] for tile in range(tiles)], axis=1).astype(jnp.bfloat16)
    raw_out[...] = raw
    if stage == 2:
        return
    padded[1 : height + 1, 1 : width + 1] = raw.reshape(height, width, group, lanes)
    wait()
    for k in list(range(1, sections)) + [0]:
        total = jnp.zeros((rows, lanes), jnp.float32)
        for offset in range(9):
            r, c = divmod(offset, 3)
            lhs = padded[2 - r : 2 - r + height, 2 - c : 2 - c + width].reshape(rows, lanes)
            row = pl.multiple_of(offset * channels + (scal[0] ^ k) * lanes, lanes)
            total += lax.dot_general(
                lhs,
                weights[pl.ds(row, lanes), :],
                (((1,), (1,)), ((), ())),
                preferred_element_type=jnp.float32,
            )
        if k == 0:
            own_out[...] = total + jnp.concatenate([upstream[tile] for tile in range(tiles)], axis=1)
        else:
            sends[k - 1][...] = total.astype(jnp.bfloat16)


def stay(arrays):
    return [pltpu.with_memory_space_constraint(array, pltpu.HBM) for array in arrays]


def vmem(count):
    return [pl.BlockSpec(memory_space=VMEM)] * count


def run_forward(dims, block, scal, slices, sources, readout):
    sections, height, width, images, steps = dims
    rows, lanes = slices[0].shape
    depth = 9 * sections * lanes
    last = block == sections - 1
    shapes = [
        jax.ShapeDtypeStruct((rows, lanes), jnp.bfloat16),
        jax.ShapeDtypeStruct((lanes // 128, rows, 128), jnp.float32),
    ]
    operands = [scal, *(slices if last else stay(slices)), *stay(sources)]
    extra = []
    if last:
        shapes.append(jax.ShapeDtypeStruct((images, readout.shape[1]), jnp.float32))
        operands.append(readout)
        extra = vmem(1)
    return pl.pallas_call(
        functools.partial(forward_kernel, dims, block),
        out_shape=shapes,
        in_specs=[pl.BlockSpec(memory_space=pltpu.SMEM)]
        + vmem(sections)
        + [pl.BlockSpec(memory_space=pltpu.HBM)] * len(sources)
        + extra,
        out_specs=vmem(len(shapes)),
        scratch_shapes=[
            VMEM((depth, lanes), jnp.bfloat16),
            VMEM((sections, height + 2, width + 2, images * steps, lanes), jnp.bfloat16),
            VMEM((lanes // 128, rows, 128), jnp.float32),
            pltpu.SemaphoreType.DMA,
        ],
        compiler_params=pltpu.CompilerParams(vmem_limit_bytes=LIMIT),
        cost_estimate=pl.CostEstimate(
            flops=2 * rows * lanes * depth,
            bytes_accessed=2 * depth * lanes,
            transcendentals=rows * lanes,
        ),
        name="forward_block",
    )(*operands)


def run_backward(dims, block, classes, scal, heads, fired, sources):
    sections, height, width, images, steps = dims
    stage = 0 if block == sections - 1 else (2 if block == 0 else 1)
    tiles, rows = fired.shape[:2]
    lanes = tiles * 128
    half = jax.ShapeDtypeStruct((rows, lanes), jnp.bfloat16)
    full = jax.ShapeDtypeStruct((rows, lanes), jnp.float32)
    operands = [scal, *heads, *stay([fired])]
    specs = [pl.BlockSpec(memory_space=pltpu.SMEM)] + vmem(len(heads) + 1)
    work = [VMEM(fired.shape, jnp.float32), VMEM(fired.shape, jnp.float32)]
    cost = 0
    if stage < 2:
        depth = 9 * sections * lanes
        operands += stay(sources)
        specs += [pl.BlockSpec(memory_space=pltpu.HBM)] * len(sources)
        shapes = [half, full] + [half] * (sections - 1)
        work = (
            [
                VMEM((depth, lanes), jnp.bfloat16),
                VMEM((height + 2, width + 2, images * steps, lanes), jnp.bfloat16),
            ]
            + work
            + [pltpu.SemaphoreType.DMA]
        )
        cost = depth
    else:
        shapes = [half]
    return pl.pallas_call(
        functools.partial(backward_kernel, dims, block, classes),
        out_shape=shapes,
        in_specs=specs,
        out_specs=vmem(len(shapes)),
        scratch_shapes=work,
        compiler_params=pltpu.CompilerParams(vmem_limit_bytes=LIMIT),
        cost_estimate=pl.CostEstimate(
            flops=2 * rows * lanes * cost + rows * lanes * 100,
            bytes_accessed=2 * cost * lanes + 8 * rows * lanes,
            transcendentals=0,
        ),
        name="backward_block",
    )(*operands)


def after(value, *earlier):
    return lax.optimization_barrier((value, *earlier))[0]


def hops(step, way, ring):
    if way > 0:
        pairs = [(i, i + 1) for i in range(step - 1, ring - 1)]
    else:
        pairs = [(i, i - 1) for i in range(1, ring - step + 1)]
    return [(2 * a + core, 2 * b + core) for a, b in pairs for core in range(2)]


def swap_core(value):
    count = lax.axis_size("dp")
    return lax.ppermute(value, "dp", [(i, i ^ 1) for i in range(count)])


def adam_update(weights, first_moment, second_moment, grad_total):
    new_first = beta_first * first_moment + (1.0 - beta_first) * grad_total
    new_second = beta_second * second_moment + (1.0 - beta_second) * grad_total * grad_total
    new_weights = weights - learn_rate * new_first / (jnp.sqrt(new_second) + adam_eps)
    return (new_weights, new_first, new_second)


def shards(spikes, labels, readout, weights, first_moment, second_moment):
    sections = lax.axis_size("section")
    devices = lax.axis_size("dp")
    ring = devices // 2
    s = lax.axis_index("section")
    d = lax.axis_index("dp")
    z, core = d // 2, d % 2
    images, steps, height, width, channels = spikes.shape
    group = images * steps
    rows = height * width * group
    lanes = channels // sections
    depth = weights.shape[1]
    classes = readout.shape[1]
    dims = (sections, height, width, images, steps)
    scal = jnp.stack([s, z, core]).astype(jnp.int32)

    def exchange(values):
        return [
            lax.ppermute(values[k], "section", [(i, i ^ (k + 1)) for i in range(sections)])
            for k in range(sections - 1)
        ]

    def columns(array, k):
        return lax.dynamic_slice_in_dim(array, (s ^ k) * lanes, lanes, 1)

    def pick(options, index):
        return lax.dynamic_index_in_dim(jnp.stack(options), index, 0, keepdims=False)

    pieces = [columns(weights[0], k).astype(jnp.bfloat16) for k in range(sections)]
    pieces = [pieces[0]] + exchange(pieces[1:])
    field = spikes.transpose(2, 3, 0, 1, 4).reshape(rows, channels)
    slices = [columns(field, k) for k in range(sections)]
    padded_classes = -(-classes // 128) * 128
    readout_own = lax.dynamic_slice_in_dim(readout, s * lanes, lanes, 0)
    readout_own = jnp.pad(readout_own, ((0, 0), (0, padded_classes - classes)))

    inputs, results, slots, done = [slices], [], {}, {}
    own_inputs = jnp.stack(slices)

    def holding(b):
        return [array for slot in slots_of(b, sections) for array in slots[slot]]

    def forward(b):
        nonlocal own_inputs
        results.append(run_forward(dims, b, scal, inputs[b], holding(b), readout_own))
        if b < sections - 1:
            out = results[b][0]
            inputs.append([out] + exchange([out] * (sections - 1)))
            own_inputs = jnp.where(s == b + 1, jnp.stack(inputs[b + 1]), own_inputs)

    def piece_of(slot):
        if slot == 0:
            return pieces[0]
        return pick(pieces, jnp.where(slot - 1 < s, slot - 1, slot) ^ s)

    for slot in range(2, sections, 2):
        piece = piece_of(slot)
        gates = [readout_own, *slices] if slot == 2 else done[slot - 2, ring - 1]
        up = down = after(piece, *gates)
        for step in range(1, ring):
            up = lax.ppermute(up, "dp", hops(step, 1, ring))
            down = lax.ppermute(down, "dp", hops(step, -1, ring))
            done[slot, step] = [up, down]
        held = [piece]
        for j in range(1, ring):
            held.append(jnp.where(z + j < ring, done[slot, j][1], done[slot, ring - j][0]))
        held = jnp.stack(held)
        slots[slot] = [held, swap_core(held)]
    gates = []
    for slot in [0] + list(range(1, sections, 2)):
        piece = after(piece_of(slot), *gates) if gates else piece_of(slot)
        gathered = lax.all_gather(piece, "dp", axis=0, tiled=True)
        slots[slot] = [gathered]
        gates = [gathered] + done.get((2, 1) if slot == 0 else (slot + 1, ring - 1), [])
    for b in range(sections):
        forward(b)
    result = results[-1]
    logits = result[2]
    heads = [logits] + exchange([logits] * (sections - 1))
    heads += [labels[:, None], readout_own]

    def ordered(parts):
        return jnp.concatenate([pick(parts, s ^ j) for j in range(sections)], axis=1)

    own_x = jnp.concatenate(
        [
            lax.dynamic_index_in_dim(own_inputs, s ^ j, 0, keepdims=False)
            for j in range(sections)
        ],
        axis=1,
    )
    x_all = lax.all_gather(own_x, "dp")

    raws = [None] * sections
    for b in reversed(range(sections)):
        held = holding(b) if b > 0 else None
        result = run_backward(dims, b, classes, scal, heads, results[b][1], held)
        raws[b] = result[0]
        if b > 0:
            heads = [result[1]] + exchange(result[2:])

    sent = [pick(raws, s ^ k) for k in range(sections)]
    own_raw = ordered([sent[0]] + exchange(sent[1:]))
    start = d * depth
    channel = start % channels
    step = 1
    while channels % (2 * step) == 0 and depth % (2 * step) == 0:
        step *= 2
    spans = -(-(channels - step + depth) // channels)

    fields = x_all.reshape(devices, height, width, group, channels)
    fields = jnp.pad(fields, ((0, 0), (1, 1), (1, 1), (0, 0), (0, 0)))
    shifted = []
    for i in range(spans):
        offset = jnp.minimum(start // channels + i, 8)
        shifted.append(
            lax.dynamic_slice(
                fields,
                (0, offset // 3, offset % 3, 0, 0),
                (devices, height, width, group, channels),
            ).reshape(devices * rows, channels)
        )
    cols = lax.dynamic_slice_in_dim(jnp.concatenate(shifted, axis=1), channel, depth, 1)

    raw_all = lax.all_gather(own_raw, "dp", axis=0, tiled=True)
    raw_all, cols = lax.optimization_barrier((raw_all, cols))
    grad = lax.dot_general(
        cols, raw_all, (((0,), (0,)), ((), ())), preferred_element_type=jnp.float32
    )
    return adam_update(weights, first_moment, second_moment, grad[None])


def solution(mesh):
    return jax.shard_map(
        shards,
        mesh=mesh,
        in_specs=(
            P("dp", None, None, None, None),
            P("dp"),
            P(),
            P("section", "dp", None),
            P("section", "dp", None),
            P("section", "dp", None),
        ),
        out_specs=(P("section", "dp", None), P("section", "dp", None), P("section", "dp", None)),
        check_vma=False,
    )
```

```python
import functools
import jax
import jax.numpy as jnp
from jax import lax
from jax.experimental import pallas as pl
from jax.experimental.pallas import tpu as pltpu
from jax.sharding import PartitionSpec as P

leak_rate = 0.5
spike_slope = 4.0
threshold = 1.0
loss_scale = 4096.0
beta_first = 0.8
beta_second = 0.95
learn_rate = 0.5
adam_eps = 1e-08
HIGH = lax.Precision.HIGHEST
VMEM = pltpu.VMEM
LIMIT = 24 * 2**20


def slots_of(block, sections):
    return sorted({0, block, min(block + 1, sections - 1)})


offsets = (4, 0, 1, 2, 3, 5, 6, 7, 8)


def overlap(offset, height, width):
    r, c = divmod(offset, 3)
    cells = slice(max(0, 1 - r), min(height, height + 1 - r)), slice(
        max(0, 1 - c), min(width, width + 1 - c)
    )
    neighbours = slice(max(0, r - 1), min(height, height + r - 1)), slice(
        max(0, c - 1), min(width, width + c - 1)
    )
    return cells, neighbours


def fetch_weights(block, sections, scal, sources, weights, sems):
    s = scal[0]
    slot = jnp.where(block == s, 0, jnp.where(block < s, block + 1, block))
    rows = weights.shape[0] // 9

    def copy(source, offset):
        part = pl.ds(offset * rows, rows)
        return pltpu.make_async_copy(source.at[part, :], weights.at[part, :], sems.at[offset])

    for candidate, source in zip(slots_of(block, sections), sources):

        @pl.when(slot == candidate)
        def _():
            for offset in offsets:
                copy(source, offset).start()

    return lambda offset: copy(weights, offset).wait()


def forward_kernel(dims, block, scal, *refs):
    last = block == dims[0] - 1
    sections, height, width, images, steps = dims
    slices = refs[:sections]
    refs = refs[sections:]
    count = len(slots_of(block, sections))
    sources = refs[:count]
    refs = refs[count:]
    if last:
        readout, out, fired_out, logits_out, weights, held, work, total, sems = refs
    else:
        out, fired_out, weights, held, work, total, sems = refs
    wait = fetch_weights(block, sections, scal, sources, weights, sems)
    rows, lanes = slices[0].shape
    group = images * steps
    channels = sections * lanes
    for k in range(sections):
        held[scal[0] ^ k] = slices[k][...].reshape(height, width, group, lanes)
    for offset in offsets:
        cells, neighbours = overlap(offset, height, width)
        wait(offset)
        lhs = jnp.concatenate(
            [held[(j, *neighbours)].reshape(-1, lanes) for j in range(sections)], axis=1
        )
        part = jnp.dot(
            lhs,
            weights[offset * channels : (offset + 1) * channels, :],
            preferred_element_type=jnp.float32,
        ).reshape(*total[cells].shape)
        total[cells] = part if offset == offsets[0] else total[cells] + part
    scale = float(9 * channels) ** (-0.5)
    current = total[...].reshape(rows, lanes) * scale
    count = rows // steps
    tiles = lanes // 128
    for tile in range(tiles):
        here, there = work.at[tile], fired_out.at[tile]
        here[...] = current[:, tile * 128 : (tile + 1) * 128]
        membrane = jnp.zeros((count, 128), jnp.float32)
        for t in range(steps):
            spot = pl.ds(t, count, stride=steps)
            h = leak_rate * membrane + here[spot, :]
            fired = jax.nn.sigmoid(spike_slope * (h - threshold))
            membrane = h - threshold * fired
            there[spot, :] = fired
    fired = jnp.concatenate([fired_out[tile] for tile in range(tiles)], axis=1)
    result = (slices[0][...].astype(jnp.float32) + fired).astype(jnp.bfloat16)
    out[...] = result
    if last:
        summed = jnp.sum(
            result.astype(jnp.float32).reshape(height * width, group, lanes), axis=0
        )
        pooled = jnp.sum(summed.reshape(images, steps, lanes), axis=1) / float(
            height * width * steps
        )
        logits_out[...] = jnp.dot(
            pooled, readout[...], precision=HIGH, preferred_element_type=jnp.float32
        )


def backward_kernel(dims, block, classes, scal, *refs):
    stage = 0 if block == dims[0] - 1 else (2 if block == 0 else 1)
    sections, height, width, images, steps = dims
    if stage == 0:
        logit_parts = refs[:sections]
        labels, readout = refs[sections : sections + 2]
        refs = refs[sections + 2 :]
    else:
        own_part = refs[0]
        arrived = refs[1:sections]
        refs = refs[sections:]
    fired = refs[0]
    refs = refs[1:]
    if stage < 2:
        count = len(slots_of(block, sections))
        sources = refs[:count]
        refs = refs[count:]
        raw_out, own_out = refs[:2]
        sends = refs[2 : 1 + sections]
        weights, held, upstream, work, total, sems = refs[1 + sections :]
        wait = fetch_weights(block, sections, scal, sources, weights, sems)
    else:
        raw_out, upstream, work = refs
    tiles, rows = fired.shape[:2]
    lanes = tiles * 128
    group = images * steps
    channels = sections * lanes
    cells = height * width
    count = rows // steps
    if stage == 0:
        logits = logit_parts[0][...]
        for part in logit_parts[1:]:
            logits = logits + part[...]
        lane = lax.broadcasted_iota(jnp.int32, logits.shape, 1)
        logits = jnp.where(lane < classes, logits, -jnp.inf)
        exponent = jnp.exp(logits - jnp.max(logits, axis=-1, keepdims=True))
        probability = exponent / jnp.sum(exponent, axis=-1, keepdims=True)
        onehot = (labels[...] == lane).astype(jnp.float32)
        dlogits = loss_scale * (probability - onehot)
        dpooled = lax.dot_general(
            dlogits,
            readout[...],
            (((1,), (1,)), ((), ())),
            precision=HIGH,
            preferred_element_type=jnp.float32,
        )
        spread = (dpooled / float(cells * steps)).astype(jnp.bfloat16).astype(jnp.float32)
        arriving = jnp.broadcast_to(
            spread[None, :, None, :], (cells, images, steps, lanes)
        ).reshape(rows, lanes)
    else:
        arriving = own_part[...]
        for part in arrived:
            arriving = arriving + part[...].astype(jnp.float32)
        arriving = arriving.astype(jnp.bfloat16).astype(jnp.float32)
    scale = float(9 * channels) ** (-0.5)
    for tile in range(tiles):
        upstream[tile] = arriving[:, tile * 128 : (tile + 1) * 128]
        here, there, fired_here = upstream.at[tile], work.at[tile], fired.at[tile]
        dmembrane = jnp.zeros((count, 128), jnp.float32)
        for t in reversed(range(steps)):
            spot = pl.ds(t, count, stride=steps)
            f = fired_here[spot, :]
            slope = spike_slope * (f * (1.0 - f))
            dh = dmembrane + (here[spot, :] - threshold * dmembrane) * slope
            there[spot, :] = dh * scale
            dmembrane = leak_rate * dh
    raw = jnp.concatenate([work[tile] for tile in range(tiles)], axis=1).astype(jnp.bfloat16)
    raw_out[...] = raw
    if stage == 2:
        return
    held[...] = raw.reshape(height, width, group, lanes)
    for k in list(range(1, sections)) + [0]:
        for offset in offsets:
            cells, neighbours = overlap(offset, height, width)
            if k == 1 or sections == 1:
                wait(offset)
            row = pl.multiple_of(offset * channels + (scal[0] ^ k) * lanes, lanes)
            part = lax.dot_general(
                held[cells].reshape(-1, lanes),
                weights[pl.ds(row, lanes), :],
                (((1,), (1,)), ((), ())),
                preferred_element_type=jnp.float32,
            ).reshape(*total[neighbours].shape)
            total[neighbours] = part if offset == offsets[0] else total[neighbours] + part
        whole = total[...].reshape(rows, lanes)
        if k == 0:
            own_out[...] = whole + jnp.concatenate([upstream[tile] for tile in range(tiles)], axis=1)
        else:
            sends[k - 1][...] = whole.astype(jnp.bfloat16)


def stay(arrays):
    return [pltpu.with_memory_space_constraint(array, pltpu.HBM) for array in arrays]


def vmem(count):
    return [pl.BlockSpec(memory_space=VMEM)] * count


def run_forward(dims, block, scal, slices, sources, readout):
    sections, height, width, images, steps = dims
    rows, lanes = slices[0].shape
    depth = 9 * sections * lanes
    last = block == sections - 1
    shapes = [
        jax.ShapeDtypeStruct((rows, lanes), jnp.bfloat16),
        jax.ShapeDtypeStruct((lanes // 128, rows, 128), jnp.float32),
    ]
    operands = [scal, *(slices if last else stay(slices)), *stay(sources)]
    extra = []
    if last:
        shapes.append(jax.ShapeDtypeStruct((images, readout.shape[1]), jnp.float32))
        operands.append(readout)
        extra = vmem(1)
    return pl.pallas_call(
        functools.partial(forward_kernel, dims, block),
        out_shape=shapes,
        in_specs=[pl.BlockSpec(memory_space=pltpu.SMEM)]
        + vmem(sections)
        + [pl.BlockSpec(memory_space=pltpu.HBM)] * len(sources)
        + extra,
        out_specs=vmem(len(shapes)),
        scratch_shapes=[
            VMEM((depth, lanes), jnp.bfloat16),
            VMEM((sections, height, width, images * steps, lanes), jnp.bfloat16),
            VMEM((lanes // 128, rows, 128), jnp.float32),
            VMEM((height, width, images * steps, lanes), jnp.float32),
            pltpu.SemaphoreType.DMA((9,)),
        ],
        compiler_params=pltpu.CompilerParams(vmem_limit_bytes=LIMIT),
        cost_estimate=pl.CostEstimate(
            flops=2 * rows * lanes * depth,
            bytes_accessed=2 * depth * lanes,
            transcendentals=rows * lanes,
        ),
        name="forward_block",
    )(*operands)


def run_backward(dims, block, classes, scal, heads, fired, sources):
    sections, height, width, images, steps = dims
    stage = 0 if block == sections - 1 else (2 if block == 0 else 1)
    tiles, rows = fired.shape[:2]
    lanes = tiles * 128
    half = jax.ShapeDtypeStruct((rows, lanes), jnp.bfloat16)
    full = jax.ShapeDtypeStruct((rows, lanes), jnp.float32)
    operands = [scal, *heads, *stay([fired])]
    specs = [pl.BlockSpec(memory_space=pltpu.SMEM)] + vmem(len(heads) + 1)
    work = [VMEM(fired.shape, jnp.float32), VMEM(fired.shape, jnp.float32)]
    cost = 0
    if stage < 2:
        depth = 9 * sections * lanes
        operands += stay(sources)
        specs += [pl.BlockSpec(memory_space=pltpu.HBM)] * len(sources)
        shapes = [half, full] + [half] * (sections - 1)
        work = (
            [
                VMEM((depth, lanes), jnp.bfloat16),
                VMEM((height, width, images * steps, lanes), jnp.bfloat16),
            ]
            + work
            + [
                VMEM((height, width, images * steps, lanes), jnp.float32),
                pltpu.SemaphoreType.DMA((9,)),
            ]
        )
        cost = depth
    else:
        shapes = [half]
    return pl.pallas_call(
        functools.partial(backward_kernel, dims, block, classes),
        out_shape=shapes,
        in_specs=specs,
        out_specs=vmem(len(shapes)),
        scratch_shapes=work,
        compiler_params=pltpu.CompilerParams(vmem_limit_bytes=LIMIT),
        cost_estimate=pl.CostEstimate(
            flops=2 * rows * lanes * cost + rows * lanes * 100,
            bytes_accessed=2 * cost * lanes + 8 * rows * lanes,
            transcendentals=0,
        ),
        name="backward_block",
    )(*operands)


def after(value, *earlier):
    return lax.optimization_barrier((value, *earlier))[0]


def hops(step, way, ring):
    if way > 0:
        pairs = [(i, i + 1) for i in range(step - 1, ring - 1)]
    else:
        pairs = [(i, i - 1) for i in range(1, ring - step + 1)]
    return [(2 * a + core, 2 * b + core) for a, b in pairs for core in range(2)]


def swap_core(value):
    count = lax.axis_size("dp")
    return lax.ppermute(value, "dp", [(i, i ^ 1) for i in range(count)])


def update_kernel(cols, raw, weights, first_moment, second_moment, *outs):
    grad = jnp.dot(cols[...], raw[...], preferred_element_type=jnp.float32)
    new_first = beta_first * first_moment[...] + (1.0 - beta_first) * grad
    new_second = beta_second * second_moment[...] + (1.0 - beta_second) * grad * grad
    outs[0][...] = weights[...] - learn_rate * new_first / (jnp.sqrt(new_second) + adam_eps)
    outs[1][...] = new_first
    outs[2][...] = new_second


def run_update(cols, raw, weights, first_moment, second_moment):
    depth, channels = weights.shape
    rows = raw.shape[0]
    tile = min(256, channels)
    state = pl.BlockSpec((depth, tile), lambda i: (0, i))
    return pl.pallas_call(
        update_kernel,
        grid=(channels // tile,),
        out_shape=[jax.ShapeDtypeStruct(weights.shape, jnp.float32)] * 3,
        in_specs=[
            pl.BlockSpec(memory_space=VMEM),
            pl.BlockSpec((rows, tile), lambda i: (0, i)),
            state,
            state,
            state,
        ],
        out_specs=[state] * 3,
        compiler_params=pltpu.CompilerParams(vmem_limit_bytes=40 * 2**20),
        cost_estimate=pl.CostEstimate(
            flops=2 * rows * depth * channels,
            bytes_accessed=24 * depth * channels + 2 * rows * channels,
            transcendentals=0,
        ),
        name="update",
    )(
        pltpu.with_memory_space_constraint(cols, VMEM),
        raw,
        weights,
        first_moment,
        second_moment,
    )


def shards(spikes, labels, readout, weights, first_moment, second_moment):
    sections = lax.axis_size("section")
    devices = lax.axis_size("dp")
    ring = devices // 2
    s = lax.axis_index("section")
    d = lax.axis_index("dp")
    z, core = d // 2, d % 2
    images, steps, height, width, channels = spikes.shape
    group = images * steps
    rows = height * width * group
    lanes = channels // sections
    depth = weights.shape[1]
    classes = readout.shape[1]
    dims = (sections, height, width, images, steps)
    scal = jnp.stack([s, z, core]).astype(jnp.int32)

    def exchange(values):
        return [
            lax.ppermute(values[k], "section", [(i, i ^ (k + 1)) for i in range(sections)])
            for k in range(sections - 1)
        ]

    def columns(array, k):
        return lax.dynamic_slice_in_dim(array, (s ^ k) * lanes, lanes, 1)

    def pick(options, index):
        return lax.dynamic_index_in_dim(jnp.stack(options), index, 0, keepdims=False)

    pieces = [columns(weights[0], k).astype(jnp.bfloat16) for k in range(sections)]
    pieces = [pieces[0]] + exchange(pieces[1:])
    field = spikes.transpose(2, 3, 0, 1, 4).reshape(rows, channels)
    slices = [columns(field, k) for k in range(sections)]
    padded_classes = -(-classes // 128) * 128
    readout_own = lax.dynamic_slice_in_dim(readout, s * lanes, lanes, 0)
    readout_own = jnp.pad(readout_own, ((0, 0), (0, padded_classes - classes)))

    inputs, results, slots, rings, done = [slices], [], {}, {}, {}
    own_inputs = jnp.stack(slices)

    def holding(b):
        return [slots[slot] for slot in slots_of(b, sections)]

    def lay_out(slot, earlier):
        whole = jnp.zeros((devices, depth, lanes), jnp.bfloat16)
        for place, pieces_held in zip((core, 1 - core), rings[slot]):
            pieces_held = after(pieces_held, earlier)
            for j in range(ring):
                spot = lax.rem(z + j, ring) * 2 + place
                whole = lax.dynamic_update_index_in_dim(whole, pieces_held[j], spot, 0)
        return whole.reshape(devices * depth, lanes)

    def forward(b):
        nonlocal own_inputs
        if b + 1 in rings:
            slots[b + 1] = lay_out(b + 1, results[b - 1][0])
        results.append(run_forward(dims, b, scal, inputs[b], holding(b), readout_own))
        if b < sections - 1:
            out = results[b][0]
            inputs.append([out] + exchange([out] * (sections - 1)))
            own_inputs = jnp.where(s == b + 1, jnp.stack(inputs[b + 1]), own_inputs)

    def piece_of(slot):
        if slot == 0:
            return pieces[0]
        return pick(pieces, jnp.where(slot - 1 < s, slot - 1, slot) ^ s)

    for slot in range(2, sections, 2):
        piece = piece_of(slot)
        gates = [readout_own, *slices] if slot == 2 else done[slot - 2, ring - 1]
        up = down = after(piece, *gates)
        for step in range(1, ring):
            up = lax.ppermute(up, "dp", hops(step, 1, ring))
            down = lax.ppermute(down, "dp", hops(step, -1, ring))
            done[slot, step] = [up, down]
        held = [piece]
        for j in range(1, ring):
            held.append(jnp.where(z + j < ring, done[slot, j][1], done[slot, ring - j][0]))
        held = jnp.stack(held)
        rings[slot] = (held, swap_core(held))
    gates = []
    for slot in [0] + list(range(1, sections, 2)):
        piece = after(piece_of(slot), *gates) if gates else piece_of(slot)
        gathered = lax.all_gather(piece, "dp", axis=0, tiled=True)
        slots[slot] = gathered
        gates = [gathered] + done.get((2, 1) if slot == 0 else (slot + 1, ring - 1), [])
    for b in range(sections):
        forward(b)
    result = results[-1]
    logits = result[2]
    heads = [logits] + exchange([logits] * (sections - 1))
    heads += [labels[:, None], readout_own]

    def ordered(parts):
        return jnp.concatenate([pick(parts, s ^ j) for j in range(sections)], axis=1)

    own_x = jnp.concatenate(
        [
            lax.dynamic_index_in_dim(own_inputs, s ^ j, 0, keepdims=False)
            for j in range(sections)
        ],
        axis=1,
    )
    x_all = lax.all_gather(own_x, "dp")

    raws = [None] * sections
    for b in reversed(range(sections)):
        held = holding(b) if b > 0 else None
        result = run_backward(dims, b, classes, scal, heads, results[b][1], held)
        raws[b] = result[0]
        if b > 0:
            heads = [result[1]] + exchange(result[2:])

    sent = [pick(raws, s ^ k) for k in range(sections)]
    own_raw = ordered([sent[0]] + exchange(sent[1:]))
    start = d * depth
    channel = start % channels
    step = 1
    while channels % (2 * step) == 0 and depth % (2 * step) == 0:
        step *= 2
    spans = -(-(channels - step + depth) // channels)

    fields = x_all.reshape(devices, height, width, group, channels)
    fields = jnp.pad(fields, ((0, 0), (1, 1), (1, 1), (0, 0), (0, 0)))
    shifted = []
    for i in range(spans):
        offset = jnp.minimum(start // channels + i, 8)
        shifted.append(
            lax.dynamic_slice(
                fields,
                (0, offset // 3, offset % 3, 0, 0),
                (devices, height, width, group, channels),
            ).reshape(devices * rows, channels)
        )
    cols = lax.dynamic_slice_in_dim(jnp.concatenate(shifted, axis=1), channel, depth, 1)

    raw_all = lax.all_gather(own_raw, "dp", axis=0, tiled=True)
    outs = run_update(cols.T, raw_all, weights[0], first_moment[0], second_moment[0])
    return tuple(out[None] for out in outs)


def solution(mesh):
    return jax.shard_map(
        shards,
        mesh=mesh,
        in_specs=(
            P("dp", None, None, None, None),
            P("dp"),
            P(),
            P("section", "dp", None),
            P("section", "dp", None),
            P("section", "dp", None),
        ),
        out_specs=(P("section", "dp", None), P("section", "dp", None), P("section", "dp", None)),
        check_vma=False,
    )
```

```python
import functools
import jax
import jax.numpy as jnp
from jax import lax
from jax.experimental import pallas as pl
from jax.experimental.pallas import tpu as pltpu
from jax.sharding import PartitionSpec as P

leak_rate = 0.5
spike_slope = 4.0
threshold = 1.0
loss_scale = 4096.0
beta_first = 0.8
beta_second = 0.95
learn_rate = 0.5
adam_eps = 1e-08
HIGH = lax.Precision.HIGHEST
VMEM = pltpu.VMEM
LIMIT = 24 * 2**20


def slots_of(block, sections):
    return sorted({0, block, min(block + 1, sections - 1)})


offsets = (4, 0, 1, 2, 3, 5, 6, 7, 8)


def overlap(offset, height, width):
    r, c = divmod(offset, 3)
    cells = slice(max(0, 1 - r), min(height, height + 1 - r)), slice(
        max(0, 1 - c), min(width, width + 1 - c)
    )
    neighbours = slice(max(0, r - 1), min(height, height + r - 1)), slice(
        max(0, c - 1), min(width, width + c - 1)
    )
    return cells, neighbours


def fetch_weights(block, sections, scal, sources, weights, sems):
    s = scal[0]
    slot = jnp.where(block == s, 0, jnp.where(block < s, block + 1, block))
    rows = weights.shape[0] // 9

    def copy(source, offset):
        part = pl.ds(offset * rows, rows)
        return pltpu.make_async_copy(source.at[part, :], weights.at[part, :], sems.at[offset])

    for candidate, source in zip(slots_of(block, sections), sources):

        @pl.when(slot == candidate)
        def _():
            for offset in offsets:
                copy(source, offset).start()

    return lambda offset: copy(weights, offset).wait()


def forward_kernel(dims, block, scal, *refs):
    last = block == dims[0] - 1
    sections, height, width, images, steps = dims
    slices = refs[:sections]
    refs = refs[sections:]
    count = len(slots_of(block, sections))
    sources = refs[:count]
    refs = refs[count:]
    if last:
        readout, out, fired_out, logits_out, weights, held, work, sems = refs
    else:
        out, fired_out, weights, held, work, sems = refs
    wait = fetch_weights(block, sections, scal, sources, weights, sems)
    rows, lanes = slices[0].shape
    group = images * steps
    channels = sections * lanes
    held[...] = jnp.zeros_like(held)
    for k in range(sections):
        held[scal[0] ^ k, 1 : height + 1, 1 : width + 1] = slices[k][...].reshape(
            height, width, group, lanes
        )
    for offset in offsets:
        wait(offset)
    total = jnp.zeros((rows, lanes), jnp.float32)
    for offset in range(9):
        r, c = divmod(offset, 3)
        lhs = jnp.concatenate(
            [
                held[j, r : r + height, c : c + width].reshape(rows, lanes)
                for j in range(sections)
            ],
            axis=1,
        )
        total += jnp.dot(
            lhs,
            weights[offset * channels : (offset + 1) * channels, :],
            preferred_element_type=jnp.float32,
        )
    scale = float(9 * channels) ** (-0.5)
    current = total * scale
    count = rows // steps
    tiles = lanes // 128
    for tile in range(tiles):
        here, there = work.at[tile], fired_out.at[tile]
        here[...] = current[:, tile * 128 : (tile + 1) * 128]
        membrane = jnp.zeros((count, 128), jnp.float32)
        for t in range(steps):
            spot = pl.ds(t, count, stride=steps)
            h = leak_rate * membrane + here[spot, :]
            fired = jax.nn.sigmoid(spike_slope * (h - threshold))
            membrane = h - threshold * fired
            there[spot, :] = fired
    fired = jnp.concatenate([fired_out[tile] for tile in range(tiles)], axis=1)
    result = (slices[0][...].astype(jnp.float32) + fired).astype(jnp.bfloat16)
    out[...] = result
    if last:
        summed = jnp.sum(
            result.astype(jnp.float32).reshape(height * width, group, lanes), axis=0
        )
        pooled = jnp.sum(summed.reshape(images, steps, lanes), axis=1) / float(
            height * width * steps
        )
        logits_out[...] = jnp.dot(
            pooled, readout[...], precision=HIGH, preferred_element_type=jnp.float32
        )


def backward_kernel(dims, block, classes, scal, *refs):
    stage = 0 if block == dims[0] - 1 else (2 if block == 0 else 1)
    sections, height, width, images, steps = dims
    if stage == 0:
        logit_parts = refs[:sections]
        labels, readout = refs[sections : sections + 2]
        refs = refs[sections + 2 :]
    else:
        own_part = refs[0]
        arrived = refs[1:sections]
        refs = refs[sections:]
    fired = refs[0]
    refs = refs[1:]
    if stage < 2:
        count = len(slots_of(block, sections))
        sources = refs[:count]
        refs = refs[count:]
        raw_out, own_out = refs[:2]
        sends = refs[2 : 1 + sections]
        weights, held, upstream, work, total, sems = refs[1 + sections :]
        wait = fetch_weights(block, sections, scal, sources, weights, sems)
    else:
        raw_out, upstream, work = refs
    tiles, rows = fired.shape[:2]
    lanes = tiles * 128
    group = images * steps
    channels = sections * lanes
    cells = height * width
    count = rows // steps
    if stage == 0:
        logits = logit_parts[0][...]
        for part in logit_parts[1:]:
            logits = logits + part[...]
        lane = lax.broadcasted_iota(jnp.int32, logits.shape, 1)
        logits = jnp.where(lane < classes, logits, -jnp.inf)
        exponent = jnp.exp(logits - jnp.max(logits, axis=-1, keepdims=True))
        probability = exponent / jnp.sum(exponent, axis=-1, keepdims=True)
        onehot = (labels[...] == lane).astype(jnp.float32)
        dlogits = loss_scale * (probability - onehot)
        dpooled = lax.dot_general(
            dlogits,
            readout[...],
            (((1,), (1,)), ((), ())),
            precision=HIGH,
            preferred_element_type=jnp.float32,
        )
        spread = (dpooled / float(cells * steps)).astype(jnp.bfloat16).astype(jnp.float32)
        arriving = jnp.broadcast_to(
            spread[None, :, None, :], (cells, images, steps, lanes)
        ).reshape(rows, lanes)
    else:
        arriving = own_part[...]
        for part in arrived:
            arriving = arriving + part[...].astype(jnp.float32)
        arriving = arriving.astype(jnp.bfloat16).astype(jnp.float32)
    scale = float(9 * channels) ** (-0.5)
    for tile in range(tiles):
        upstream[tile] = arriving[:, tile * 128 : (tile + 1) * 128]
        here, there, fired_here = upstream.at[tile], work.at[tile], fired.at[tile]
        dmembrane = jnp.zeros((count, 128), jnp.float32)
        for t in reversed(range(steps)):
            spot = pl.ds(t, count, stride=steps)
            f = fired_here[spot, :]
            slope = spike_slope * (f * (1.0 - f))
            dh = dmembrane + (here[spot, :] - threshold * dmembrane) * slope
            there[spot, :] = dh * scale
            dmembrane = leak_rate * dh
    raw = jnp.concatenate([work[tile] for tile in range(tiles)], axis=1).astype(jnp.bfloat16)
    raw_out[...] = raw
    if stage == 2:
        return
    held[...] = raw.reshape(height, width, group, lanes)
    for k in list(range(1, sections)) + [0]:
        for offset in offsets:
            cells, neighbours = overlap(offset, height, width)
            if k == 1 or sections == 1:
                wait(offset)
            row = pl.multiple_of(offset * channels + (scal[0] ^ k) * lanes, lanes)
            part = lax.dot_general(
                held[cells].reshape(-1, lanes),
                weights[pl.ds(row, lanes), :],
                (((1,), (1,)), ((), ())),
                preferred_element_type=jnp.float32,
            ).reshape(*total[neighbours].shape)
            total[neighbours] = part if offset == offsets[0] else total[neighbours] + part
        whole = total[...].reshape(rows, lanes)
        if k == 0:
            own_out[...] = whole + jnp.concatenate([upstream[tile] for tile in range(tiles)], axis=1)
        else:
            sends[k - 1][...] = whole.astype(jnp.bfloat16)


def stay(arrays):
    return [pltpu.with_memory_space_constraint(array, pltpu.HBM) for array in arrays]


def vmem(count):
    return [pl.BlockSpec(memory_space=VMEM)] * count


def run_forward(dims, block, scal, slices, sources, readout):
    sections, height, width, images, steps = dims
    rows, lanes = slices[0].shape
    depth = 9 * sections * lanes
    last = block == sections - 1
    shapes = [
        jax.ShapeDtypeStruct((rows, lanes), jnp.bfloat16),
        pltpu.HBM((lanes // 128, rows, 128), jnp.float32),
    ]
    operands = [scal, *(slices if last else stay(slices)), *stay(sources)]
    extra = []
    if last:
        shapes.append(jax.ShapeDtypeStruct((images, readout.shape[1]), jnp.float32))
        operands.append(readout)
        extra = vmem(1)
    return pl.pallas_call(
        functools.partial(forward_kernel, dims, block),
        out_shape=shapes,
        in_specs=[pl.BlockSpec(memory_space=pltpu.SMEM)]
        + vmem(sections)
        + [pl.BlockSpec(memory_space=pltpu.HBM)] * len(sources)
        + extra,
        out_specs=vmem(len(shapes)),
        scratch_shapes=[
            VMEM((depth, lanes), jnp.bfloat16),
            VMEM((sections, height + 2, width + 2, images * steps, lanes), jnp.bfloat16),
            VMEM((lanes // 128, rows, 128), jnp.float32),
            pltpu.SemaphoreType.DMA((9,)),
        ],
        compiler_params=pltpu.CompilerParams(vmem_limit_bytes=LIMIT),
        cost_estimate=pl.CostEstimate(
            flops=2 * rows * lanes * depth,
            bytes_accessed=2 * depth * lanes,
            transcendentals=rows * lanes,
        ),
        name="forward_block",
    )(*operands)


def run_backward(dims, block, classes, scal, heads, fired, sources):
    sections, height, width, images, steps = dims
    stage = 0 if block == sections - 1 else (2 if block == 0 else 1)
    tiles, rows = fired.shape[:2]
    lanes = tiles * 128
    half = jax.ShapeDtypeStruct((rows, lanes), jnp.bfloat16)
    full = jax.ShapeDtypeStruct((rows, lanes), jnp.float32)
    operands = [scal, *heads, *stay([fired])]
    specs = [pl.BlockSpec(memory_space=pltpu.SMEM)] + vmem(len(heads) + 1)
    work = [VMEM(fired.shape, jnp.float32), VMEM(fired.shape, jnp.float32)]
    cost = 0
    if stage < 2:
        depth = 9 * sections * lanes
        operands += stay(sources)
        specs += [pl.BlockSpec(memory_space=pltpu.HBM)] * len(sources)
        shapes = [half, full] + [half] * (sections - 1)
        work = (
            [
                VMEM((depth, lanes), jnp.bfloat16),
                VMEM((height, width, images * steps, lanes), jnp.bfloat16),
            ]
            + work
            + [
                VMEM((height, width, images * steps, lanes), jnp.float32),
                pltpu.SemaphoreType.DMA((9,)),
            ]
        )
        cost = depth
    else:
        shapes = [half]
    return pl.pallas_call(
        functools.partial(backward_kernel, dims, block, classes),
        out_shape=shapes,
        in_specs=specs,
        out_specs=vmem(len(shapes)),
        scratch_shapes=work,
        compiler_params=pltpu.CompilerParams(vmem_limit_bytes=LIMIT),
        cost_estimate=pl.CostEstimate(
            flops=2 * rows * lanes * cost + rows * lanes * 100,
            bytes_accessed=2 * cost * lanes + 8 * rows * lanes,
            transcendentals=0,
        ),
        name="backward_block",
    )(*operands)


def after(value, *earlier):
    return lax.optimization_barrier((value, *earlier))[0]


def hops(step, way, ring):
    if way > 0:
        pairs = [(i, i + 1) for i in range(step - 1, ring - 1)]
    else:
        pairs = [(i, i - 1) for i in range(1, ring - step + 1)]
    return [(2 * a + core, 2 * b + core) for a, b in pairs for core in range(2)]


def swap_core(value):
    count = lax.axis_size("dp")
    return lax.ppermute(value, "dp", [(i, i ^ 1) for i in range(count)])


def update_kernel(cols, raw, weights, first_moment, second_moment, *refs):
    outs, (held, grad, sems) = refs[:3], refs[3:]
    chunks = sems.shape[0]
    size = held.shape[1] // chunks
    first = pl.program_id(0) == 0

    def copy(i):
        part = pl.ds(i * size, size)
        return pltpu.make_async_copy(cols.at[:, part], held.at[:, part], sems.at[i])

    @pl.when(first)
    def _():
        for i in range(chunks):
            copy(i).start()

    for i in range(chunks):

        @pl.when(first)
        def _():
            copy(i).wait()

        part = slice(i * size, (i + 1) * size)
        term = jnp.dot(held[:, part], raw[part, :], preferred_element_type=jnp.float32)
        grad[...] = term if i == 0 else grad[...] + term
    total = grad[...]
    new_first = beta_first * first_moment[...] + (1.0 - beta_first) * total
    new_second = beta_second * second_moment[...] + (1.0 - beta_second) * total * total
    outs[0][...] = weights[...] - learn_rate * new_first / (jnp.sqrt(new_second) + adam_eps)
    outs[1][...] = new_first
    outs[2][...] = new_second


def run_update(cols, raw, weights, first_moment, second_moment):
    depth, channels = weights.shape
    rows = raw.shape[0]
    tile = min(256, channels)
    state = pl.BlockSpec((depth, tile), lambda i: (0, i))
    return pl.pallas_call(
        update_kernel,
        grid=(channels // tile,),
        out_shape=[jax.ShapeDtypeStruct(weights.shape, jnp.float32)] * 3,
        in_specs=[
            pl.BlockSpec(memory_space=pl.ANY),
            pl.BlockSpec((rows, tile), lambda i: (0, i)),
            state,
            state,
            state,
        ],
        out_specs=[state] * 3,
        scratch_shapes=[
            VMEM((depth, rows), jnp.bfloat16),
            VMEM((depth, tile), jnp.float32),
            pltpu.SemaphoreType.DMA((4,)),
        ],
        compiler_params=pltpu.CompilerParams(vmem_limit_bytes=48 * 2**20),
        cost_estimate=pl.CostEstimate(
            flops=2 * rows * depth * channels,
            bytes_accessed=24 * depth * channels + 2 * rows * channels,
            transcendentals=0,
        ),
        name="update",
    )(*stay([cols, raw, weights, first_moment, second_moment]))


def shards(spikes, labels, readout, weights, first_moment, second_moment):
    sections = lax.axis_size("section")
    devices = lax.axis_size("dp")
    ring = devices // 2
    s = lax.axis_index("section")
    d = lax.axis_index("dp")
    z, core = d // 2, d % 2
    images, steps, height, width, channels = spikes.shape
    group = images * steps
    rows = height * width * group
    lanes = channels // sections
    depth = weights.shape[1]
    classes = readout.shape[1]
    dims = (sections, height, width, images, steps)
    scal = jnp.stack([s, z, core]).astype(jnp.int32)

    def exchange(values):
        return [
            lax.ppermute(values[k], "section", [(i, i ^ (k + 1)) for i in range(sections)])
            for k in range(sections - 1)
        ]

    def columns(array, k):
        return lax.dynamic_slice_in_dim(array, (s ^ k) * lanes, lanes, 1)

    def pick(options, index):
        return lax.dynamic_index_in_dim(jnp.stack(options), index, 0, keepdims=False)

    pieces = [columns(weights[0], k).astype(jnp.bfloat16) for k in range(sections)]
    pieces = [pieces[0]] + exchange(pieces[1:])
    field = spikes.transpose(2, 3, 0, 1, 4).reshape(rows, channels)
    slices = [columns(field, k) for k in range(sections)]
    padded_classes = -(-classes // 128) * 128
    readout_own = lax.dynamic_slice_in_dim(readout, s * lanes, lanes, 0)
    readout_own = jnp.pad(readout_own, ((0, 0), (0, padded_classes - classes)))

    inputs, results, slots, rings, done = [slices], [], {}, {}, {}
    own_inputs = jnp.stack(slices)

    def holding(b):
        return [slots[slot] for slot in slots_of(b, sections)]

    def lay_out(slot, earlier):
        held = [rings[slot]]
        for j in range(1, ring):
            near, far = done[slot, j][1], done[slot, ring - j][0]
            held.append(
                jnp.where(z + j < ring, after(near, *earlier), after(far, *earlier))
            )
        held = jnp.stack(held)
        whole = jnp.zeros((devices, depth, lanes), jnp.bfloat16)
        for place, part in ((core, held), (1 - core, swap_core(held))):
            for j in range(ring):
                spot = lax.rem(z + j, ring) * 2 + place
                whole = lax.dynamic_update_index_in_dim(whole, part[j], spot, 0)
        return whole.reshape(devices * depth, lanes)

    def forward(b):
        nonlocal own_inputs
        if b + 1 in rings:
            slots[b + 1] = lay_out(b + 1, inputs[b][1:])
        results.append(run_forward(dims, b, scal, inputs[b], holding(b), readout_own))
        if b < sections - 1:
            out = results[b][0]
            inputs.append([out] + exchange([out] * (sections - 1)))
            own_inputs = jnp.where(s == b + 1, jnp.stack(inputs[b + 1]), own_inputs)

    def piece_of(slot):
        if slot == 0:
            return pieces[0]
        return pick(pieces, jnp.where(slot - 1 < s, slot - 1, slot) ^ s)

    for slot in range(2, sections, 2):
        piece = piece_of(slot)
        gates = [readout_own, *slices] if slot == 2 else done[slot - 2, ring - 1]
        up = down = after(piece, *gates)
        for step in range(1, ring):
            up = lax.ppermute(up, "dp", hops(step, 1, ring))
            down = lax.ppermute(down, "dp", hops(step, -1, ring))
            done[slot, step] = [up, down]
        rings[slot] = piece
    gates = []
    for slot in [0] + list(range(1, sections, 2)):
        piece = after(piece_of(slot), *gates) if gates else piece_of(slot)
        gathered = lax.all_gather(piece, "dp", axis=0, tiled=True)
        slots[slot] = gathered
        gates = [gathered] + done.get((2, 1) if slot == 0 else (slot + 1, max(1, ring - 2)), [])
    for b in range(sections):
        forward(b)
    result = results[-1]
    logits = result[2]
    heads = [logits] + exchange([logits] * (sections - 1))
    heads += [labels[:, None], readout_own]

    def ordered(parts):
        return jnp.concatenate([pick(parts, s ^ j) for j in range(sections)], axis=1)

    own_x = jnp.concatenate(
        [
            lax.dynamic_index_in_dim(own_inputs, s ^ j, 0, keepdims=False)
            for j in range(sections)
        ],
        axis=1,
    )
    x_all = lax.all_gather(own_x, "dp")

    raws = [None] * sections
    for b in reversed(range(sections)):
        held = holding(b) if b > 0 else None
        result = run_backward(dims, b, classes, scal, heads, results[b][1], held)
        raws[b] = result[0]
        if b > 0:
            heads = [result[1]] + exchange(result[2:])

    sent = [pick(raws, s ^ k) for k in range(sections)]
    own_raw = ordered([sent[0]] + exchange(sent[1:]))
    start = d * depth
    channel = start % channels
    step = 1
    while channels % (2 * step) == 0 and depth % (2 * step) == 0:
        step *= 2
    spans = -(-(channels - step + depth) // channels)

    fields = x_all.reshape(devices, height, width, group, channels)
    fields = jnp.pad(fields, ((0, 0), (1, 1), (1, 1), (0, 0), (0, 0)))
    shifted = []
    for i in range(spans):
        offset = jnp.minimum(start // channels + i, 8)
        shifted.append(
            lax.dynamic_slice(
                fields,
                (0, offset // 3, offset % 3, 0, 0),
                (devices, height, width, group, channels),
            ).reshape(devices * rows, channels)
        )
    cols = lax.dynamic_slice_in_dim(jnp.concatenate(shifted, axis=1), channel, depth, 1)

    raw_all = lax.all_gather(own_raw, "dp", axis=0, tiled=True)
    outs = run_update(cols.T, raw_all, weights[0], first_moment[0], second_moment[0])
    return tuple(out[None] for out in outs)


def solution(mesh):
    return jax.shard_map(
        shards,
        mesh=mesh,
        in_specs=(
            P("dp", None, None, None, None),
            P("dp"),
            P(),
            P("section", "dp", None),
            P("section", "dp", None),
            P("section", "dp", None),
        ),
        out_specs=(P("section", "dp", None), P("section", "dp", None), P("section", "dp", None)),
        check_vma=False,
    )
```

```python
import functools
import jax
import jax.numpy as jnp
from jax import lax
from jax.experimental import pallas as pl
from jax.experimental.pallas import tpu as pltpu
from jax.sharding import PartitionSpec as P

leak_rate = 0.5
spike_slope = 4.0
threshold = 1.0
loss_scale = 4096.0
beta_first = 0.8
beta_second = 0.95
learn_rate = 0.5
adam_eps = 1e-08
HIGH = lax.Precision.HIGHEST
VMEM = pltpu.VMEM
LIMIT = 24 * 2**20


def slots_of(block, sections):
    return sorted({0, block, min(block + 1, sections - 1)})


offsets = (4, 0, 1, 2, 3, 5, 6, 7, 8)


def overlap(offset, height, width):
    r, c = divmod(offset, 3)
    cells = slice(max(0, 1 - r), min(height, height + 1 - r)), slice(
        max(0, 1 - c), min(width, width + 1 - c)
    )
    neighbours = slice(max(0, r - 1), min(height, height + r - 1)), slice(
        max(0, c - 1), min(width, width + c - 1)
    )
    return cells, neighbours


def fetch_weights(block, sections, scal, sources, weights, sems):
    s = scal[0]
    slot = jnp.where(block == s, 0, jnp.where(block < s, block + 1, block))
    rows = weights.shape[0] // 9

    def copy(source, offset):
        part = pl.ds(offset * rows, rows)
        return pltpu.make_async_copy(source.at[part, :], weights.at[part, :], sems.at[offset])

    for candidate, source in zip(slots_of(block, sections), sources):

        @pl.when(slot == candidate)
        def _():
            for offset in offsets:
                copy(source, offset).start()

    return lambda offset: copy(weights, offset).wait()


def forward_kernel(dims, block, scal, *refs):
    last = block == dims[0] - 1
    sections, height, width, images, steps = dims
    slices = refs[:sections]
    refs = refs[sections:]
    count = len(slots_of(block, sections))
    sources = refs[:count]
    refs = refs[count:]
    if last:
        readout, out, fired_out, logits_out, weights, held, work, sems = refs
    else:
        out, fired_out, weights, held, work, sems = refs
    wait = fetch_weights(block, sections, scal, sources, weights, sems)
    rows, lanes = slices[0].shape
    group = images * steps
    channels = sections * lanes
    held[...] = jnp.zeros_like(held)
    for k in range(sections):
        held[scal[0] ^ k, 1 : height + 1, 1 : width + 1] = slices[k][...].reshape(
            height, width, group, lanes
        )
    for offset in offsets:
        wait(offset)
    total = jnp.zeros((rows, lanes), jnp.float32)
    for offset in range(9):
        r, c = divmod(offset, 3)
        lhs = jnp.concatenate(
            [
                held[j, r : r + height, c : c + width].reshape(rows, lanes)
                for j in range(sections)
            ],
            axis=1,
        )
        total += jnp.dot(
            lhs,
            weights[offset * channels : (offset + 1) * channels, :],
            preferred_element_type=jnp.float32,
        )
    scale = float(9 * channels) ** (-0.5)
    current = total * scale
    count = rows // steps
    tiles = lanes // 128
    for tile in range(tiles):
        here, there = work.at[tile], fired_out.at[tile]
        here[...] = current[:, tile * 128 : (tile + 1) * 128]
        membrane = jnp.zeros((count, 128), jnp.float32)
        for t in range(steps):
            spot = pl.ds(t, count, stride=steps)
            h = leak_rate * membrane + here[spot, :]
            fired = jax.nn.sigmoid(spike_slope * (h - threshold))
            membrane = h - threshold * fired
            there[spot, :] = fired
    fired = jnp.concatenate([fired_out[tile] for tile in range(tiles)], axis=1)
    result = (slices[0][...].astype(jnp.float32) + fired).astype(jnp.bfloat16)
    out[...] = result
    if last:
        summed = jnp.sum(
            result.astype(jnp.float32).reshape(height * width, group, lanes), axis=0
        )
        pooled = jnp.sum(summed.reshape(images, steps, lanes), axis=1) / float(
            height * width * steps
        )
        logits_out[...] = jnp.dot(
            pooled, readout[...], precision=HIGH, preferred_element_type=jnp.float32
        )


def backward_kernel(dims, block, classes, scal, *refs):
    stage = 0 if block == dims[0] - 1 else (2 if block == 0 else 1)
    sections, height, width, images, steps = dims
    if stage == 0:
        logit_parts = refs[:sections]
        labels, readout = refs[sections : sections + 2]
        refs = refs[sections + 2 :]
    else:
        own_part = refs[0]
        arrived = refs[1:sections]
        refs = refs[sections:]
    fired = refs[0]
    refs = refs[1:]
    if stage < 2:
        count = len(slots_of(block, sections))
        sources = refs[:count]
        refs = refs[count:]
        raw_out, own_out = refs[:2]
        sends = refs[2 : 1 + sections]
        weights, held, upstream, work, total, sems = refs[1 + sections :]
        wait = fetch_weights(block, sections, scal, sources, weights, sems)
    else:
        raw_out, upstream, work = refs
    tiles, rows = fired.shape[:2]
    lanes = tiles * 128
    group = images * steps
    channels = sections * lanes
    cells = height * width
    count = rows // steps
    if stage == 0:
        logits = logit_parts[0][...]
        for part in logit_parts[1:]:
            logits = logits + part[...]
        lane = lax.broadcasted_iota(jnp.int32, logits.shape, 1)
        logits = jnp.where(lane < classes, logits, -jnp.inf)
        exponent = jnp.exp(logits - jnp.max(logits, axis=-1, keepdims=True))
        probability = exponent / jnp.sum(exponent, axis=-1, keepdims=True)
        onehot = (labels[...] == lane).astype(jnp.float32)
        dlogits = loss_scale * (probability - onehot)
        dpooled = lax.dot_general(
            dlogits,
            readout[...],
            (((1,), (1,)), ((), ())),
            precision=HIGH,
            preferred_element_type=jnp.float32,
        )
        spread = (dpooled / float(cells * steps)).astype(jnp.bfloat16).astype(jnp.float32)
        arriving = jnp.broadcast_to(
            spread[None, :, None, :], (cells, images, steps, lanes)
        ).reshape(rows, lanes)
    else:
        arriving = own_part[...]
        for part in arrived:
            arriving = arriving + part[...].astype(jnp.float32)
        arriving = arriving.astype(jnp.bfloat16).astype(jnp.float32)
    scale = float(9 * channels) ** (-0.5)
    for tile in range(tiles):
        upstream[tile] = arriving[:, tile * 128 : (tile + 1) * 128]
        here, there, fired_here = upstream.at[tile], work.at[tile], fired.at[tile]
        dmembrane = jnp.zeros((count, 128), jnp.float32)
        for t in reversed(range(steps)):
            spot = pl.ds(t, count, stride=steps)
            f = fired_here[spot, :]
            slope = spike_slope * (f * (1.0 - f))
            dh = dmembrane + (here[spot, :] - threshold * dmembrane) * slope
            there[spot, :] = dh * scale
            dmembrane = leak_rate * dh
    raw = jnp.concatenate([work[tile] for tile in range(tiles)], axis=1).astype(jnp.bfloat16)
    raw_out[...] = raw
    if stage == 2:
        return
    held[...] = raw.reshape(height, width, group, lanes)
    for k in list(range(1, sections)) + [0]:
        for offset in offsets:
            cells, neighbours = overlap(offset, height, width)
            if k == 1 or sections == 1:
                wait(offset)
            row = pl.multiple_of(offset * channels + (scal[0] ^ k) * lanes, lanes)
            part = lax.dot_general(
                held[cells].reshape(-1, lanes),
                weights[pl.ds(row, lanes), :],
                (((1,), (1,)), ((), ())),
                preferred_element_type=jnp.float32,
            ).reshape(*total[neighbours].shape)
            total[neighbours] = part if offset == offsets[0] else total[neighbours] + part
        whole = total[...].reshape(rows, lanes)
        if k == 0:
            own_out[...] = whole + jnp.concatenate([upstream[tile] for tile in range(tiles)], axis=1)
        else:
            sends[k - 1][...] = whole.astype(jnp.bfloat16)


def stay(arrays):
    return [pltpu.with_memory_space_constraint(array, pltpu.HBM) for array in arrays]


def vmem(count):
    return [pl.BlockSpec(memory_space=VMEM)] * count


def run_forward(dims, block, scal, slices, sources, readout):
    sections, height, width, images, steps = dims
    rows, lanes = slices[0].shape
    depth = 9 * sections * lanes
    last = block == sections - 1
    shapes = [
        jax.ShapeDtypeStruct((rows, lanes), jnp.bfloat16),
        pltpu.HBM((lanes // 128, rows, 128), jnp.float32),
    ]
    operands = [scal, *(slices if last else stay(slices)), *stay(sources)]
    extra = []
    if last:
        shapes.append(jax.ShapeDtypeStruct((images, readout.shape[1]), jnp.float32))
        operands.append(readout)
        extra = vmem(1)
    return pl.pallas_call(
        functools.partial(forward_kernel, dims, block),
        out_shape=shapes,
        in_specs=[pl.BlockSpec(memory_space=pltpu.SMEM)]
        + vmem(sections)
        + [pl.BlockSpec(memory_space=pltpu.HBM)] * len(sources)
        + extra,
        out_specs=vmem(len(shapes)),
        scratch_shapes=[
            VMEM((depth, lanes), jnp.bfloat16),
            VMEM((sections, height + 2, width + 2, images * steps, lanes), jnp.bfloat16),
            VMEM((lanes // 128, rows, 128), jnp.float32),
            pltpu.SemaphoreType.DMA((9,)),
        ],
        compiler_params=pltpu.CompilerParams(vmem_limit_bytes=LIMIT),
        cost_estimate=pl.CostEstimate(
            flops=2 * rows * lanes * depth,
            bytes_accessed=2 * depth * lanes,
            transcendentals=rows * lanes,
        ),
        name="forward_block",
    )(*operands)


def run_backward(dims, block, classes, scal, heads, fired, sources):
    sections, height, width, images, steps = dims
    stage = 0 if block == sections - 1 else (2 if block == 0 else 1)
    tiles, rows = fired.shape[:2]
    lanes = tiles * 128
    half = jax.ShapeDtypeStruct((rows, lanes), jnp.bfloat16)
    full = jax.ShapeDtypeStruct((rows, lanes), jnp.float32)
    operands = [scal, *heads, *stay([fired])]
    specs = [pl.BlockSpec(memory_space=pltpu.SMEM)] + vmem(len(heads) + 1)
    work = [VMEM(fired.shape, jnp.float32), VMEM(fired.shape, jnp.float32)]
    cost = 0
    if stage < 2:
        depth = 9 * sections * lanes
        operands += stay(sources)
        specs += [pl.BlockSpec(memory_space=pltpu.HBM)] * len(sources)
        shapes = [half, full] + [half] * (sections - 1)
        work = (
            [
                VMEM((depth, lanes), jnp.bfloat16),
                VMEM((height, width, images * steps, lanes), jnp.bfloat16),
            ]
            + work
            + [
                VMEM((height, width, images * steps, lanes), jnp.float32),
                pltpu.SemaphoreType.DMA((9,)),
            ]
        )
        cost = depth
    else:
        shapes = [half]
    return pl.pallas_call(
        functools.partial(backward_kernel, dims, block, classes),
        out_shape=shapes,
        in_specs=specs,
        out_specs=vmem(len(shapes)),
        scratch_shapes=work,
        compiler_params=pltpu.CompilerParams(vmem_limit_bytes=LIMIT),
        cost_estimate=pl.CostEstimate(
            flops=2 * rows * lanes * cost + rows * lanes * 100,
            bytes_accessed=2 * cost * lanes + 8 * rows * lanes,
            transcendentals=0,
        ),
        name="backward_block",
    )(*operands)


def after(value, *earlier):
    return lax.optimization_barrier((value, *earlier))[0]


def hops(step, way, ring):
    if way > 0:
        pairs = [(i, i + 1) for i in range(step - 1, ring - 1)]
    else:
        pairs = [(i, i - 1) for i in range(1, ring - step + 1)]
    return [(2 * a + core, 2 * b + core) for a, b in pairs for core in range(2)]


def swap_core(value):
    count = lax.axis_size("dp")
    return lax.ppermute(value, "dp", [(i, i ^ 1) for i in range(count)])


def update_kernel(cols, raw, weights, first_moment, second_moment, *outs):
    grad = jnp.dot(cols[...], raw[...], preferred_element_type=jnp.float32)
    new_first = beta_first * first_moment[...] + (1.0 - beta_first) * grad
    new_second = beta_second * second_moment[...] + (1.0 - beta_second) * grad * grad
    outs[0][...] = weights[...] - learn_rate * new_first / (jnp.sqrt(new_second) + adam_eps)
    outs[1][...] = new_first
    outs[2][...] = new_second


def run_update(cols, raw, weights, first_moment, second_moment):
    depth, channels = weights.shape
    rows = raw.shape[0]
    tile = min(256, channels)
    state = pl.BlockSpec((depth, tile), lambda i: (0, i))
    return pl.pallas_call(
        update_kernel,
        grid=(channels // tile,),
        out_shape=[jax.ShapeDtypeStruct(weights.shape, jnp.float32)] * 3,
        in_specs=[
            pl.BlockSpec(memory_space=VMEM),
            pl.BlockSpec((rows, tile), lambda i: (0, i)),
            state,
            state,
            state,
        ],
        out_specs=[state] * 3,
        compiler_params=pltpu.CompilerParams(vmem_limit_bytes=48 * 2**20),
        cost_estimate=pl.CostEstimate(
            flops=2 * rows * depth * channels,
            bytes_accessed=24 * depth * channels + 2 * rows * channels,
            transcendentals=0,
        ),
        name="update",
    )(
        *stay([cols, raw, weights, first_moment, second_moment])
    )


def shards(spikes, labels, readout, weights, first_moment, second_moment):
    sections = lax.axis_size("section")
    devices = lax.axis_size("dp")
    ring = devices // 2
    s = lax.axis_index("section")
    d = lax.axis_index("dp")
    z, core = d // 2, d % 2
    images, steps, height, width, channels = spikes.shape
    group = images * steps
    rows = height * width * group
    lanes = channels // sections
    depth = weights.shape[1]
    classes = readout.shape[1]
    dims = (sections, height, width, images, steps)
    scal = jnp.stack([s, z, core]).astype(jnp.int32)

    def exchange(values):
        return [
            lax.ppermute(values[k], "section", [(i, i ^ (k + 1)) for i in range(sections)])
            for k in range(sections - 1)
        ]

    def columns(array, k):
        return lax.dynamic_slice_in_dim(array, (s ^ k) * lanes, lanes, 1)

    def pick(options, index):
        return lax.dynamic_index_in_dim(jnp.stack(options), index, 0, keepdims=False)

    pieces = [columns(weights[0], k).astype(jnp.bfloat16) for k in range(sections)]
    pieces = [pieces[0]] + exchange(pieces[1:])
    field = spikes.transpose(2, 3, 0, 1, 4).reshape(rows, channels)
    slices = [columns(field, k) for k in range(sections)]
    padded_classes = -(-classes // 128) * 128
    readout_own = lax.dynamic_slice_in_dim(readout, s * lanes, lanes, 0)
    readout_own = jnp.pad(readout_own, ((0, 0), (0, padded_classes - classes)))

    inputs, results, slots, rings, done = [slices], [], {}, {}, {}
    own_inputs = jnp.stack(slices)

    def holding(b):
        return [slots[slot] for slot in slots_of(b, sections)]

    def lay_out(slot, earlier):
        whole = jnp.zeros((devices, depth, lanes), jnp.bfloat16)
        for place, pieces_held in zip((core, 1 - core), rings[slot]):
            pieces_held = after(pieces_held, earlier)
            for j in range(ring):
                spot = lax.rem(z + j, ring) * 2 + place
                whole = lax.dynamic_update_index_in_dim(whole, pieces_held[j], spot, 0)
        return whole.reshape(devices * depth, lanes)

    def forward(b):
        nonlocal own_inputs
        if b + 1 in rings:
            slots[b + 1] = lay_out(b + 1, results[b - 1][0])
        results.append(run_forward(dims, b, scal, inputs[b], holding(b), readout_own))
        if b < sections - 1:
            out = results[b][0]
            inputs.append([out] + exchange([out] * (sections - 1)))
            own_inputs = jnp.where(s == b + 1, jnp.stack(inputs[b + 1]), own_inputs)

    def piece_of(slot):
        if slot == 0:
            return pieces[0]
        return pick(pieces, jnp.where(slot - 1 < s, slot - 1, slot) ^ s)

    for slot in range(2, sections, 2):
        piece = piece_of(slot)
        gates = [readout_own, *slices] if slot == 2 else done[slot - 2, ring - 1]
        up = down = after(piece, *gates)
        for step in range(1, ring):
            up = lax.ppermute(up, "dp", hops(step, 1, ring))
            down = lax.ppermute(down, "dp", hops(step, -1, ring))
            done[slot, step] = [up, down]
        held = [piece]
        for j in range(1, ring):
            held.append(jnp.where(z + j < ring, done[slot, j][1], done[slot, ring - j][0]))
        held = jnp.stack(held)
        rings[slot] = (held, swap_core(held))
    gates = []
    for slot in [0] + list(range(1, sections, 2)):
        piece = after(piece_of(slot), *gates) if gates else piece_of(slot)
        gathered = lax.all_gather(piece, "dp", axis=0, tiled=True)
        slots[slot] = gathered
        gates = [gathered] + done.get((2, 1) if slot == 0 else (slot + 1, ring - 1), [])
    for b in range(sections):
        forward(b)
    result = results[-1]
    logits = result[2]
    heads = [logits] + exchange([logits] * (sections - 1))
    heads += [labels[:, None], readout_own]

    def ordered(parts):
        return jnp.concatenate([pick(parts, s ^ j) for j in range(sections)], axis=1)

    x_all = lax.all_gather(own_inputs.reshape(sections * rows, lanes), "dp")

    raws = [None] * sections
    for b in reversed(range(sections)):
        held = holding(b) if b > 0 else None
        result = run_backward(dims, b, classes, scal, heads, results[b][1], held)
        raws[b] = result[0]
        if b > 0:
            heads = [result[1]] + exchange(result[2:])

    sent = [pick(raws, s ^ k) for k in range(sections)]
    own_raw = ordered([sent[0]] + exchange(sent[1:]))
    start = d * depth
    channel = start % channels
    step = 1
    while channels % (2 * step) == 0 and depth % (2 * step) == 0:
        step *= 2
    spans = -(-(channels - step + depth) // channels)

    x_all = x_all.reshape(devices, sections, height, width, group, lanes)
    fields = jnp.concatenate(
        [
            lax.dynamic_index_in_dim(x_all, s ^ j, 1, keepdims=False)
            for j in range(sections)
        ],
        axis=-1,
    )
    fields = jnp.pad(fields, ((0, 0), (1, 1), (1, 1), (0, 0), (0, 0)))
    shifted = []
    for i in range(spans):
        offset = jnp.minimum(start // channels + i, 8)
        shifted.append(
            lax.dynamic_slice(
                fields,
                (0, offset // 3, offset % 3, 0, 0),
                (devices, height, width, group, channels),
            ).reshape(devices * rows, channels)
        )
    cols = lax.dynamic_slice_in_dim(jnp.concatenate(shifted, axis=1), channel, depth, 1)

    raw_all = lax.all_gather(own_raw, "dp", axis=0, tiled=True)
    outs = run_update(cols.T, raw_all, weights[0], first_moment[0], second_moment[0])
    return tuple(out[None] for out in outs)


def solution(mesh):
    return jax.shard_map(
        shards,
        mesh=mesh,
        in_specs=(
            P("dp", None, None, None, None),
            P("dp"),
            P(),
            P("section", "dp", None),
            P("section", "dp", None),
            P("section", "dp", None),
        ),
        out_specs=(P("section", "dp", None), P("section", "dp", None), P("section", "dp", None)),
        check_vma=False,
    )
```

```python
import functools
import jax
import jax.numpy as jnp
from jax import lax
from jax.experimental import pallas as pl
from jax.experimental.pallas import tpu as pltpu
from jax.sharding import PartitionSpec as P

leak_rate = 0.5
spike_slope = 4.0
threshold = 1.0
loss_scale = 4096.0
beta_first = 0.8
beta_second = 0.95
learn_rate = 0.5
adam_eps = 1e-08
HIGH = lax.Precision.HIGHEST
VMEM = pltpu.VMEM
LIMIT = 24 * 2**20


def slots_of(block, sections):
    return sorted({0, block, min(block + 1, sections - 1)})


offsets = (4, 0, 1, 2, 3, 5, 6, 7, 8)


def overlap(offset, height, width):
    r, c = divmod(offset, 3)
    cells = slice(max(0, 1 - r), min(height, height + 1 - r)), slice(
        max(0, 1 - c), min(width, width + 1 - c)
    )
    neighbours = slice(max(0, r - 1), min(height, height + r - 1)), slice(
        max(0, c - 1), min(width, width + c - 1)
    )
    return cells, neighbours


def fetch_weights(block, sections, scal, sources, weights, sems, order=offsets):
    s = scal[0]
    slot = jnp.where(block == s, 0, jnp.where(block < s, block + 1, block))
    rows = weights.shape[0] // len(order)

    def copy(source, offset):
        part = pl.ds(offset * rows, rows)
        return pltpu.make_async_copy(source.at[part, :], weights.at[part, :], sems.at[offset])

    for candidate, source in zip(slots_of(block, sections), sources):

        @pl.when(slot == candidate)
        def _():
            for offset in order:
                copy(source, offset).start()

    return lambda offset: copy(weights, offset).wait()


def forward_kernel(dims, block, scal, *refs):
    last = block == dims[0] - 1
    sections, height, width, images, steps = dims
    slices = refs[:sections]
    refs = refs[sections:]
    count = len(slots_of(block, sections))
    sources = refs[:count]
    refs = refs[count:]
    if last:
        readout, out, fired_out, logits_out, weights, held, work, total, sems = refs
    else:
        out, fired_out, weights, held, work, total, sems = refs
    wait = fetch_weights(block, sections, scal, sources, weights, sems, (0,))
    rows, lanes = slices[0].shape
    group = images * steps
    channels = sections * lanes
    for k in range(sections):
        held[scal[0] ^ k] = slices[k][...].reshape(height, width, group, lanes)
    wait(0)
    for offset in offsets:
        cells, neighbours = overlap(offset, height, width)
        lhs = jnp.concatenate(
            [held[(j, *neighbours)].reshape(-1, lanes) for j in range(sections)], axis=1
        )
        part = jnp.dot(
            lhs,
            weights[offset * channels : (offset + 1) * channels, :],
            preferred_element_type=jnp.float32,
        ).reshape(*total[cells].shape)
        total[cells] = part if offset == offsets[0] else total[cells] + part
    scale = float(9 * channels) ** (-0.5)
    current = total[...].reshape(rows, lanes) * scale
    count = rows // steps
    tiles = lanes // 128
    for tile in range(tiles):
        here, there = work.at[tile], fired_out.at[tile]
        here[...] = current[:, tile * 128 : (tile + 1) * 128]
        membrane = jnp.zeros((count, 128), jnp.float32)
        for t in range(steps):
            spot = pl.ds(t, count, stride=steps)
            h = leak_rate * membrane + here[spot, :]
            fired = jax.nn.sigmoid(spike_slope * (h - threshold))
            membrane = h - threshold * fired
            there[spot, :] = fired
    fired = jnp.concatenate([fired_out[tile] for tile in range(tiles)], axis=1)
    result = (slices[0][...].astype(jnp.float32) + fired).astype(jnp.bfloat16)
    out[...] = result
    if last:
        summed = jnp.sum(
            result.astype(jnp.float32).reshape(height * width, group, lanes), axis=0
        )
        pooled = jnp.sum(summed.reshape(images, steps, lanes), axis=1) / float(
            height * width * steps
        )
        logits_out[...] = jnp.dot(
            pooled, readout[...], precision=HIGH, preferred_element_type=jnp.float32
        )


def backward_kernel(dims, block, classes, scal, *refs):
    stage = 0 if block == dims[0] - 1 else (2 if block == 0 else 1)
    sections, height, width, images, steps = dims
    if stage == 0:
        logit_parts = refs[:sections]
        labels, readout = refs[sections : sections + 2]
        refs = refs[sections + 2 :]
    else:
        own_part = refs[0]
        arrived = refs[1:sections]
        refs = refs[sections:]
    fired = refs[0]
    refs = refs[1:]
    if stage < 2:
        count = len(slots_of(block, sections))
        sources = refs[:count]
        refs = refs[count:]
        raw_out, own_out = refs[:2]
        sends = refs[2 : 1 + sections]
        weights, held, upstream, work, total, sems = refs[1 + sections :]
        wait = fetch_weights(block, sections, scal, sources, weights, sems)
    else:
        raw_out, upstream, work = refs
    tiles, rows = fired.shape[:2]
    lanes = tiles * 128
    group = images * steps
    channels = sections * lanes
    cells = height * width
    count = rows // steps
    if stage == 0:
        logits = logit_parts[0][...]
        for part in logit_parts[1:]:
            logits = logits + part[...]
        lane = lax.broadcasted_iota(jnp.int32, logits.shape, 1)
        logits = jnp.where(lane < classes, logits, -jnp.inf)
        exponent = jnp.exp(logits - jnp.max(logits, axis=-1, keepdims=True))
        probability = exponent / jnp.sum(exponent, axis=-1, keepdims=True)
        onehot = (labels[...] == lane).astype(jnp.float32)
        dlogits = loss_scale * (probability - onehot)
        dpooled = lax.dot_general(
            dlogits,
            readout[...],
            (((1,), (1,)), ((), ())),
            precision=HIGH,
            preferred_element_type=jnp.float32,
        )
        spread = (dpooled / float(cells * steps)).astype(jnp.bfloat16).astype(jnp.float32)
        arriving = jnp.broadcast_to(
            spread[None, :, None, :], (cells, images, steps, lanes)
        ).reshape(rows, lanes)
    else:
        arriving = own_part[...]
        for part in arrived:
            arriving = arriving + part[...].astype(jnp.float32)
        arriving = arriving.astype(jnp.bfloat16).astype(jnp.float32)
    scale = float(9 * channels) ** (-0.5)
    for tile in range(tiles):
        upstream[tile] = arriving[:, tile * 128 : (tile + 1) * 128]
        here, there, fired_here = upstream.at[tile], work.at[tile], fired.at[tile]
        dmembrane = jnp.zeros((count, 128), jnp.float32)
        for t in reversed(range(steps)):
            spot = pl.ds(t, count, stride=steps)
            f = fired_here[spot, :]
            slope = spike_slope * (f * (1.0 - f))
            dh = dmembrane + (here[spot, :] - threshold * dmembrane) * slope
            there[spot, :] = dh * scale
            dmembrane = leak_rate * dh
    raw = jnp.concatenate([work[tile] for tile in range(tiles)], axis=1).astype(jnp.bfloat16)
    raw_out[...] = raw
    if stage == 2:
        return
    held[...] = raw.reshape(height, width, group, lanes)
    for k in list(range(1, sections)) + [0]:
        for offset in offsets:
            cells, neighbours = overlap(offset, height, width)
            if k == 1 or sections == 1:
                wait(offset)
            row = pl.multiple_of(offset * channels + (scal[0] ^ k) * lanes, lanes)
            part = lax.dot_general(
                held[cells].reshape(-1, lanes),
                weights[pl.ds(row, lanes), :],
                (((1,), (1,)), ((), ())),
                preferred_element_type=jnp.float32,
            ).reshape(*total[neighbours].shape)
            total[neighbours] = part if offset == offsets[0] else total[neighbours] + part
        whole = total[...].reshape(rows, lanes)
        if k == 0:
            own_out[...] = whole + jnp.concatenate([upstream[tile] for tile in range(tiles)], axis=1)
        else:
            sends[k - 1][...] = whole.astype(jnp.bfloat16)


def stay(arrays):
    return [pltpu.with_memory_space_constraint(array, pltpu.HBM) for array in arrays]


def vmem(count):
    return [pl.BlockSpec(memory_space=VMEM)] * count


def run_forward(dims, block, scal, slices, sources, readout):
    sections, height, width, images, steps = dims
    rows, lanes = slices[0].shape
    depth = 9 * sections * lanes
    last = block == sections - 1
    shapes = [
        jax.ShapeDtypeStruct((rows, lanes), jnp.bfloat16),
        pltpu.HBM((lanes // 128, rows, 128), jnp.float32),
    ]
    operands = [scal, *(slices if last else stay(slices)), *stay(sources)]
    extra = []
    if last:
        shapes.append(jax.ShapeDtypeStruct((images, readout.shape[1]), jnp.float32))
        operands.append(readout)
        extra = vmem(1)
    return pl.pallas_call(
        functools.partial(forward_kernel, dims, block),
        out_shape=shapes,
        in_specs=[pl.BlockSpec(memory_space=pltpu.SMEM)]
        + vmem(sections)
        + [pl.BlockSpec(memory_space=pltpu.HBM)] * len(sources)
        + extra,
        out_specs=vmem(len(shapes)),
        scratch_shapes=[
            VMEM((depth, lanes), jnp.bfloat16),
            VMEM((sections, height, width, images * steps, lanes), jnp.bfloat16),
            VMEM((lanes // 128, rows, 128), jnp.float32),
            VMEM((height, width, images * steps, lanes), jnp.float32),
            pltpu.SemaphoreType.DMA((1,)),
        ],
        compiler_params=pltpu.CompilerParams(vmem_limit_bytes=LIMIT),
        cost_estimate=pl.CostEstimate(
            flops=2 * rows * lanes * depth,
            bytes_accessed=2 * depth * lanes,
            transcendentals=rows * lanes,
        ),
        name="forward_block",
    )(*operands)


def run_backward(dims, block, classes, scal, heads, fired, sources):
    sections, height, width, images, steps = dims
    stage = 0 if block == sections - 1 else (2 if block == 0 else 1)
    tiles, rows = fired.shape[:2]
    lanes = tiles * 128
    half = jax.ShapeDtypeStruct((rows, lanes), jnp.bfloat16)
    full = jax.ShapeDtypeStruct((rows, lanes), jnp.float32)
    operands = [scal, *heads, *stay([fired])]
    specs = [pl.BlockSpec(memory_space=pltpu.SMEM)] + vmem(len(heads) + 1)
    work = [VMEM(fired.shape, jnp.float32), VMEM(fired.shape, jnp.float32)]
    cost = 0
    if stage < 2:
        depth = 9 * sections * lanes
        operands += stay(sources)
        specs += [pl.BlockSpec(memory_space=pltpu.HBM)] * len(sources)
        shapes = [half, full] + [half] * (sections - 1)
        work = (
            [
                VMEM((depth, lanes), jnp.bfloat16),
                VMEM((height, width, images * steps, lanes), jnp.bfloat16),
            ]
            + work
            + [
                VMEM((height, width, images * steps, lanes), jnp.float32),
                pltpu.SemaphoreType.DMA((9,)),
            ]
        )
        cost = depth
    else:
        shapes = [half]
    return pl.pallas_call(
        functools.partial(backward_kernel, dims, block, classes),
        out_shape=shapes,
        in_specs=specs,
        out_specs=vmem(len(shapes)),
        scratch_shapes=work,
        compiler_params=pltpu.CompilerParams(vmem_limit_bytes=LIMIT),
        cost_estimate=pl.CostEstimate(
            flops=2 * rows * lanes * cost + rows * lanes * 100,
            bytes_accessed=2 * cost * lanes + 8 * rows * lanes,
            transcendentals=0,
        ),
        name="backward_block",
    )(*operands)


def after(value, *earlier):
    return lax.optimization_barrier((value, *earlier))[0]


def hops(step, way, ring):
    if way > 0:
        pairs = [(i, i + 1) for i in range(step - 1, ring - 1)]
    else:
        pairs = [(i, i - 1) for i in range(1, ring - step + 1)]
    return [(2 * a + core, 2 * b + core) for a, b in pairs for core in range(2)]


def swap_core(value):
    count = lax.axis_size("dp")
    return lax.ppermute(value, "dp", [(i, i ^ 1) for i in range(count)])


def update_kernel(cols, raw, weights, first_moment, second_moment, *outs):
    grad = jnp.dot(cols[...], raw[...], preferred_element_type=jnp.float32)
    new_first = beta_first * first_moment[...] + (1.0 - beta_first) * grad
    new_second = beta_second * second_moment[...] + (1.0 - beta_second) * grad * grad
    outs[0][...] = weights[...] - learn_rate * new_first / (jnp.sqrt(new_second) + adam_eps)
    outs[1][...] = new_first
    outs[2][...] = new_second


def run_update(cols, raw, weights, first_moment, second_moment):
    depth, channels = weights.shape
    rows = raw.shape[0]
    tile = min(256, channels)
    state = pl.BlockSpec((depth, tile), lambda i: (0, i))
    return pl.pallas_call(
        update_kernel,
        grid=(channels // tile,),
        out_shape=[jax.ShapeDtypeStruct(weights.shape, jnp.float32)] * 3,
        in_specs=[
            pl.BlockSpec(memory_space=VMEM),
            pl.BlockSpec((rows, tile), lambda i: (0, i)),
            state,
            state,
            state,
        ],
        out_specs=[state] * 3,
        compiler_params=pltpu.CompilerParams(vmem_limit_bytes=48 * 2**20),
        cost_estimate=pl.CostEstimate(
            flops=2 * rows * depth * channels,
            bytes_accessed=24 * depth * channels + 2 * rows * channels,
            transcendentals=0,
        ),
        name="update",
    )(
        *stay([cols, raw, weights, first_moment, second_moment])
    )


def shards(spikes, labels, readout, weights, first_moment, second_moment):
    sections = lax.axis_size("section")
    devices = lax.axis_size("dp")
    ring = devices // 2
    s = lax.axis_index("section")
    d = lax.axis_index("dp")
    z, core = d // 2, d % 2
    images, steps, height, width, channels = spikes.shape
    group = images * steps
    rows = height * width * group
    lanes = channels // sections
    depth = weights.shape[1]
    classes = readout.shape[1]
    dims = (sections, height, width, images, steps)
    scal = jnp.stack([s, z, core]).astype(jnp.int32)

    def exchange(values):
        return [
            lax.ppermute(values[k], "section", [(i, i ^ (k + 1)) for i in range(sections)])
            for k in range(sections - 1)
        ]

    def columns(array, k):
        return lax.dynamic_slice_in_dim(array, (s ^ k) * lanes, lanes, 1)

    def pick(options, index):
        return lax.dynamic_index_in_dim(jnp.stack(options), index, 0, keepdims=False)

    pieces = [columns(weights[0], k).astype(jnp.bfloat16) for k in range(sections)]
    pieces = [pieces[0]] + exchange(pieces[1:])
    field = spikes.transpose(2, 3, 0, 1, 4).reshape(rows, channels)
    slices = [columns(field, k) for k in range(sections)]
    padded_classes = -(-classes // 128) * 128
    readout_own = lax.dynamic_slice_in_dim(readout, s * lanes, lanes, 0)
    readout_own = jnp.pad(readout_own, ((0, 0), (0, padded_classes - classes)))

    inputs, results, slots, rings, done = [slices], [], {}, {}, {}
    own_inputs = jnp.stack(slices)

    def holding(b):
        return [slots[slot] for slot in slots_of(b, sections)]

    def lay_out(slot, earlier):
        whole = jnp.zeros((devices, depth, lanes), jnp.bfloat16)
        for place, pieces_held in zip((core, 1 - core), rings[slot]):
            pieces_held = after(pieces_held, earlier)
            for j in range(ring):
                spot = lax.rem(z + j, ring) * 2 + place
                whole = lax.dynamic_update_index_in_dim(whole, pieces_held[j], spot, 0)
        return whole.reshape(devices * depth, lanes)

    def forward(b):
        nonlocal own_inputs
        if b + 1 in rings:
            slots[b + 1] = lay_out(b + 1, results[b - 1][0])
        results.append(run_forward(dims, b, scal, inputs[b], holding(b), readout_own))
        if b < sections - 1:
            out = results[b][0]
            inputs.append([out] + exchange([out] * (sections - 1)))
            own_inputs = jnp.where(s == b + 1, jnp.stack(inputs[b + 1]), own_inputs)

    def piece_of(slot):
        if slot == 0:
            return pieces[0]
        return pick(pieces, jnp.where(slot - 1 < s, slot - 1, slot) ^ s)

    for slot in range(2, sections, 2):
        piece = piece_of(slot)
        gates = [readout_own, *slices] if slot == 2 else done[slot - 2, ring - 1]
        up = down = after(piece, *gates)
        for step in range(1, ring):
            up = lax.ppermute(up, "dp", hops(step, 1, ring))
            down = lax.ppermute(down, "dp", hops(step, -1, ring))
            done[slot, step] = [up, down]
        held = [piece]
        for j in range(1, ring):
            held.append(jnp.where(z + j < ring, done[slot, j][1], done[slot, ring - j][0]))
        held = jnp.stack(held)
        rings[slot] = (held, swap_core(held))
    gates = []
    for slot in [0] + list(range(1, sections, 2)):
        piece = after(piece_of(slot), *gates) if gates else piece_of(slot)
        gathered = lax.all_gather(piece, "dp", axis=0, tiled=True)
        slots[slot] = gathered
        gates = [gathered] + done.get((2, 1) if slot == 0 else (slot + 1, ring - 1), [])
    for b in range(sections):
        forward(b)
    result = results[-1]
    logits = result[2]
    heads = [logits] + exchange([logits] * (sections - 1))
    heads += [labels[:, None], readout_own]

    def ordered(parts):
        return jnp.concatenate([pick(parts, s ^ j) for j in range(sections)], axis=1)

    x_all = lax.all_gather(own_inputs.reshape(sections * rows, lanes), "dp")

    raws = [None] * sections
    for b in reversed(range(sections)):
        held = holding(b) if b > 0 else None
        result = run_backward(dims, b, classes, scal, heads, results[b][1], held)
        raws[b] = result[0]
        if b > 0:
            heads = [result[1]] + exchange(result[2:])

    sent = [pick(raws, s ^ k) for k in range(sections)]
    own_raw = ordered([sent[0]] + exchange(sent[1:]))
    start = d * depth
    channel = start % channels
    step = 1
    while channels % (2 * step) == 0 and depth % (2 * step) == 0:
        step *= 2
    spans = -(-(channels - step + depth) // channels)

    x_all = x_all.reshape(devices, sections, height, width, group, lanes)
    fields = jnp.concatenate(
        [
            lax.dynamic_index_in_dim(x_all, s ^ j, 1, keepdims=False)
            for j in range(sections)
        ],
        axis=-1,
    )
    fields = jnp.pad(fields, ((0, 0), (1, 1), (1, 1), (0, 0), (0, 0)))
    shifted = []
    for i in range(spans):
        offset = jnp.minimum(start // channels + i, 8)
        shifted.append(
            lax.dynamic_slice(
                fields,
                (0, offset // 3, offset % 3, 0, 0),
                (devices, height, width, group, channels),
            ).reshape(devices * rows, channels)
        )
    cols = lax.dynamic_slice_in_dim(jnp.concatenate(shifted, axis=1), channel, depth, 1)

    raw_all = lax.all_gather(own_raw, "dp", axis=0, tiled=True)
    outs = run_update(cols.T, raw_all, weights[0], first_moment[0], second_moment[0])
    return tuple(out[None] for out in outs)


def solution(mesh):
    return jax.shard_map(
        shards,
        mesh=mesh,
        in_specs=(
            P("dp", None, None, None, None),
            P("dp"),
            P(),
            P("section", "dp", None),
            P("section", "dp", None),
            P("section", "dp", None),
        ),
        out_specs=(P("section", "dp", None), P("section", "dp", None), P("section", "dp", None)),
        check_vma=False,
    )
```

```python
import functools
import jax
import jax.numpy as jnp
from jax import lax
from jax.experimental import pallas as pl
from jax.experimental.pallas import tpu as pltpu
from jax.sharding import PartitionSpec as P

leak_rate = 0.5
spike_slope = 4.0
threshold = 1.0
loss_scale = 4096.0
beta_first = 0.8
beta_second = 0.95
learn_rate = 0.5
adam_eps = 1e-08
HIGH = lax.Precision.HIGHEST
VMEM = pltpu.VMEM
LIMIT = 24 * 2**20


def slots_of(block, sections):
    return sorted({0, block, min(block + 1, sections - 1)})


offsets = (4, 0, 1, 2, 3, 5, 6, 7, 8)


def overlap(offset, height, width):
    r, c = divmod(offset, 3)
    cells = slice(max(0, 1 - r), min(height, height + 1 - r)), slice(
        max(0, 1 - c), min(width, width + 1 - c)
    )
    neighbours = slice(max(0, r - 1), min(height, height + r - 1)), slice(
        max(0, c - 1), min(width, width + c - 1)
    )
    return cells, neighbours


def fetch_weights(block, sections, scal, sources, weights, sems, order=offsets):
    s = scal[0]
    slot = jnp.where(block == s, 0, jnp.where(block < s, block + 1, block))
    rows = weights.shape[0] // len(order)

    def copy(source, offset):
        part = pl.ds(offset * rows, rows)
        return pltpu.make_async_copy(source.at[part, :], weights.at[part, :], sems.at[offset])

    for candidate, source in zip(slots_of(block, sections), sources):

        @pl.when(slot == candidate)
        def _():
            for offset in order:
                copy(source, offset).start()

    return lambda offset: copy(weights, offset).wait()


def forward_kernel(dims, block, scal, *refs):
    last = block == dims[0] - 1
    sections, height, width, images, steps = dims
    slices = refs[:sections]
    refs = refs[sections:]
    count = len(slots_of(block, sections))
    sources = refs[:count]
    refs = refs[count:]
    if last:
        readout, out, fired_out, logits_out, weights, held, work, total, sems = refs
    else:
        out, fired_out, weights, held, work, total, sems = refs
    wait = fetch_weights(block, sections, scal, sources, weights, sems, (0,))
    rows, lanes = slices[0].shape
    group = images * steps
    channels = sections * lanes
    for k in range(sections):
        held[scal[0] ^ k] = slices[k][...].reshape(height, width, group, lanes)
    wait(0)
    for offset in offsets:
        cells, neighbours = overlap(offset, height, width)
        lhs = jnp.concatenate(
            [held[(j, *neighbours)].reshape(-1, lanes) for j in range(sections)], axis=1
        )
        part = jnp.dot(
            lhs,
            weights[offset * channels : (offset + 1) * channels, :],
            preferred_element_type=jnp.float32,
        ).reshape(*total[cells].shape)
        total[cells] = part if offset == offsets[0] else total[cells] + part
    scale = float(9 * channels) ** (-0.5)
    current = total[...].reshape(rows, lanes) * scale
    count = rows // steps
    tiles = lanes // 128
    for tile in range(tiles):
        here, there = work.at[tile], fired_out.at[tile]
        here[...] = current[:, tile * 128 : (tile + 1) * 128]
        membrane = jnp.zeros((count, 128), jnp.float32)
        for t in range(steps):
            spot = pl.ds(t, count, stride=steps)
            h = leak_rate * membrane + here[spot, :]
            fired = jax.nn.sigmoid(spike_slope * (h - threshold))
            membrane = h - threshold * fired
            there[spot, :] = fired
    fired = jnp.concatenate([fired_out[tile] for tile in range(tiles)], axis=1)
    result = (slices[0][...].astype(jnp.float32) + fired).astype(jnp.bfloat16)
    out[...] = result
    if last:
        summed = jnp.sum(
            result.astype(jnp.float32).reshape(height * width, group, lanes), axis=0
        )
        pooled = jnp.sum(summed.reshape(images, steps, lanes), axis=1) / float(
            height * width * steps
        )
        logits_out[...] = jnp.dot(
            pooled, readout[...], precision=HIGH, preferred_element_type=jnp.float32
        )


def backward_kernel(dims, block, classes, scal, *refs):
    stage = 0 if block == dims[0] - 1 else (2 if block == 0 else 1)
    sections, height, width, images, steps = dims
    if stage == 0:
        logit_parts = refs[:sections]
        labels, readout = refs[sections : sections + 2]
        refs = refs[sections + 2 :]
    else:
        own_part = refs[0]
        arrived = refs[1:sections]
        refs = refs[sections:]
    fired = refs[0]
    refs = refs[1:]
    if stage < 2:
        count = len(slots_of(block, sections))
        sources = refs[:count]
        refs = refs[count:]
        raw_out, own_out = refs[:2]
        sends = refs[2 : 1 + sections]
        weights, held, upstream, work, total, sems = refs[1 + sections :]
        wait = fetch_weights(block, sections, scal, sources, weights, sems)
    else:
        raw_out, upstream, work = refs
    tiles, rows = fired.shape[:2]
    lanes = tiles * 128
    group = images * steps
    channels = sections * lanes
    cells = height * width
    count = rows // steps
    if stage == 0:
        logits = logit_parts[0][...]
        for part in logit_parts[1:]:
            logits = logits + part[...]
        lane = lax.broadcasted_iota(jnp.int32, logits.shape, 1)
        logits = jnp.where(lane < classes, logits, -jnp.inf)
        exponent = jnp.exp(logits - jnp.max(logits, axis=-1, keepdims=True))
        probability = exponent / jnp.sum(exponent, axis=-1, keepdims=True)
        onehot = (labels[...] == lane).astype(jnp.float32)
        dlogits = loss_scale * (probability - onehot)
        dpooled = lax.dot_general(
            dlogits,
            readout[...],
            (((1,), (1,)), ((), ())),
            precision=HIGH,
            preferred_element_type=jnp.float32,
        )
        spread = (dpooled / float(cells * steps)).astype(jnp.bfloat16).astype(jnp.float32)
        arriving = jnp.broadcast_to(
            spread[None, :, None, :], (cells, images, steps, lanes)
        ).reshape(rows, lanes)
    else:
        arriving = own_part[...]
        for part in arrived:
            arriving = arriving + part[...].astype(jnp.float32)
        arriving = arriving.astype(jnp.bfloat16).astype(jnp.float32)
    scale = float(9 * channels) ** (-0.5)
    for tile in range(tiles):
        upstream[tile] = arriving[:, tile * 128 : (tile + 1) * 128]
        here, there, fired_here = upstream.at[tile], work.at[tile], fired.at[tile]
        dmembrane = jnp.zeros((count, 128), jnp.float32)
        for t in reversed(range(steps)):
            spot = pl.ds(t, count, stride=steps)
            f = fired_here[spot, :]
            slope = spike_slope * (f * (1.0 - f))
            dh = dmembrane + (here[spot, :] - threshold * dmembrane) * slope
            there[spot, :] = dh * scale
            dmembrane = leak_rate * dh
    raw = jnp.concatenate([work[tile] for tile in range(tiles)], axis=1).astype(jnp.bfloat16)
    raw_out[...] = raw
    if stage == 2:
        return
    held[...] = raw.reshape(height, width, group, lanes)
    for k in list(range(1, sections)) + [0]:
        for offset in offsets:
            cells, neighbours = overlap(offset, height, width)
            if k == 1 or sections == 1:
                wait(offset)
            row = pl.multiple_of(offset * channels + (scal[0] ^ k) * lanes, lanes)
            part = lax.dot_general(
                held[cells].reshape(-1, lanes),
                weights[pl.ds(row, lanes), :],
                (((1,), (1,)), ((), ())),
                preferred_element_type=jnp.float32,
            ).reshape(*total[neighbours].shape)
            total[neighbours] = part if offset == offsets[0] else total[neighbours] + part
        whole = total[...].reshape(rows, lanes)
        if k == 0:
            own_out[...] = whole + jnp.concatenate([upstream[tile] for tile in range(tiles)], axis=1)
        else:
            sends[k - 1][...] = whole.astype(jnp.bfloat16)


def stay(arrays):
    return [pltpu.with_memory_space_constraint(array, pltpu.HBM) for array in arrays]


def vmem(count):
    return [pl.BlockSpec(memory_space=VMEM)] * count


def run_forward(dims, block, scal, slices, sources, readout):
    sections, height, width, images, steps = dims
    rows, lanes = slices[0].shape
    depth = 9 * sections * lanes
    last = block == sections - 1
    shapes = [
        jax.ShapeDtypeStruct((rows, lanes), jnp.bfloat16),
        pltpu.HBM((lanes // 128, rows, 128), jnp.float32),
    ]
    operands = [scal, *(slices if last else stay(slices)), *stay(sources)]
    extra = []
    if last:
        shapes.append(jax.ShapeDtypeStruct((images, readout.shape[1]), jnp.float32))
        operands.append(readout)
        extra = vmem(1)
    return pl.pallas_call(
        functools.partial(forward_kernel, dims, block),
        out_shape=shapes,
        in_specs=[pl.BlockSpec(memory_space=pltpu.SMEM)]
        + vmem(sections)
        + [pl.BlockSpec(memory_space=pltpu.HBM)] * len(sources)
        + extra,
        out_specs=vmem(len(shapes)),
        scratch_shapes=[
            VMEM((depth, lanes), jnp.bfloat16),
            VMEM((sections, height, width, images * steps, lanes), jnp.bfloat16),
            VMEM((lanes // 128, rows, 128), jnp.float32),
            VMEM((height, width, images * steps, lanes), jnp.float32),
            pltpu.SemaphoreType.DMA((1,)),
        ],
        compiler_params=pltpu.CompilerParams(vmem_limit_bytes=LIMIT),
        cost_estimate=pl.CostEstimate(
            flops=2 * rows * lanes * depth,
            bytes_accessed=2 * depth * lanes,
            transcendentals=rows * lanes,
        ),
        name="forward_block",
    )(*operands)


def run_backward(dims, block, classes, scal, heads, fired, sources):
    sections, height, width, images, steps = dims
    stage = 0 if block == sections - 1 else (2 if block == 0 else 1)
    tiles, rows = fired.shape[:2]
    lanes = tiles * 128
    half = jax.ShapeDtypeStruct((rows, lanes), jnp.bfloat16)
    full = jax.ShapeDtypeStruct((rows, lanes), jnp.float32)
    operands = [scal, *heads, *stay([fired])]
    specs = [pl.BlockSpec(memory_space=pltpu.SMEM)] + vmem(len(heads) + 1)
    work = [VMEM(fired.shape, jnp.float32), VMEM(fired.shape, jnp.float32)]
    cost = 0
    if stage < 2:
        depth = 9 * sections * lanes
        operands += stay(sources)
        specs += [pl.BlockSpec(memory_space=pltpu.HBM)] * len(sources)
        shapes = [half, full] + [half] * (sections - 1)
        work = (
            [
                VMEM((depth, lanes), jnp.bfloat16),
                VMEM((height, width, images * steps, lanes), jnp.bfloat16),
            ]
            + work
            + [
                VMEM((height, width, images * steps, lanes), jnp.float32),
                pltpu.SemaphoreType.DMA((9,)),
            ]
        )
        cost = depth
    else:
        shapes = [half]
    return pl.pallas_call(
        functools.partial(backward_kernel, dims, block, classes),
        out_shape=shapes,
        in_specs=specs,
        out_specs=vmem(len(shapes)),
        scratch_shapes=work,
        compiler_params=pltpu.CompilerParams(vmem_limit_bytes=LIMIT),
        cost_estimate=pl.CostEstimate(
            flops=2 * rows * lanes * cost + rows * lanes * 100,
            bytes_accessed=2 * cost * lanes + 8 * rows * lanes,
            transcendentals=0,
        ),
        name="backward_block",
    )(*operands)


def after(value, *earlier):
    return lax.optimization_barrier((value, *earlier))[0]


def hops(step, way, ring):
    if way > 0:
        pairs = [(i, i + 1) for i in range(step - 1, ring - 1)]
    else:
        pairs = [(i, i - 1) for i in range(1, ring - step + 1)]
    return [(2 * a + core, 2 * b + core) for a, b in pairs for core in range(2)]


def swap_core(value):
    count = lax.axis_size("dp")
    return lax.ppermute(value, "dp", [(i, i ^ 1) for i in range(count)])


def update_kernel(cols, raw, weights, first_moment, second_moment, *outs):
    grad = jnp.dot(cols[...], raw[...], preferred_element_type=jnp.float32)
    new_first = beta_first * first_moment[...] + (1.0 - beta_first) * grad
    new_second = beta_second * second_moment[...] + (1.0 - beta_second) * grad * grad
    outs[0][...] = weights[...] - learn_rate * new_first / (jnp.sqrt(new_second) + adam_eps)
    outs[1][...] = new_first
    outs[2][...] = new_second


def run_update(cols, raw, weights, first_moment, second_moment):
    depth, channels = weights.shape
    rows = raw.shape[0]
    tile = min(256, channels)
    state = pl.BlockSpec((depth, tile), lambda i: (0, i))
    return pl.pallas_call(
        update_kernel,
        grid=(channels // tile,),
        out_shape=[jax.ShapeDtypeStruct(weights.shape, jnp.float32)] * 3,
        in_specs=[
            pl.BlockSpec(memory_space=VMEM),
            pl.BlockSpec((rows, tile), lambda i: (0, i)),
            state,
            state,
            state,
        ],
        out_specs=[state] * 3,
        compiler_params=pltpu.CompilerParams(vmem_limit_bytes=48 * 2**20),
        cost_estimate=pl.CostEstimate(
            flops=2 * rows * depth * channels,
            bytes_accessed=24 * depth * channels + 2 * rows * channels,
            transcendentals=0,
        ),
        name="update",
    )(
        *stay([cols, raw, weights, first_moment, second_moment])
    )


def shards(spikes, labels, readout, weights, first_moment, second_moment):
    sections = lax.axis_size("section")
    devices = lax.axis_size("dp")
    ring = devices // 2
    s = lax.axis_index("section")
    d = lax.axis_index("dp")
    z, core = d // 2, d % 2
    images, steps, height, width, channels = spikes.shape
    group = images * steps
    rows = height * width * group
    lanes = channels // sections
    depth = weights.shape[1]
    classes = readout.shape[1]
    dims = (sections, height, width, images, steps)
    scal = jnp.stack([s, z, core]).astype(jnp.int32)

    def exchange(values):
        return [
            lax.ppermute(values[k], "section", [(i, i ^ (k + 1)) for i in range(sections)])
            for k in range(sections - 1)
        ]

    def columns(array, k):
        return lax.dynamic_slice_in_dim(array, (s ^ k) * lanes, lanes, 1)

    def pick(options, index):
        return lax.dynamic_index_in_dim(jnp.stack(options), index, 0, keepdims=False)

    pieces = [columns(weights[0], k).astype(jnp.bfloat16) for k in range(sections)]
    pieces = [pieces[0]] + exchange(pieces[1:])
    field = spikes.transpose(2, 3, 0, 1, 4).reshape(rows, channels)
    slices = [columns(field, k) for k in range(sections)]
    padded_classes = -(-classes // 128) * 128
    readout_own = lax.dynamic_slice_in_dim(readout, s * lanes, lanes, 0)
    readout_own = jnp.pad(readout_own, ((0, 0), (0, padded_classes - classes)))

    inputs, results, slots, rings, done = [slices], [], {}, {}, {}
    own_inputs = jnp.stack(slices)

    def holding(b):
        return [slots[slot] for slot in slots_of(b, sections)]

    def lay_out(slot, earlier):
        whole = jnp.zeros((devices, depth, lanes), jnp.bfloat16)
        for place, pieces_held in zip((core, 1 - core), rings[slot]):
            pieces_held = after(pieces_held, earlier)
            for j in range(ring):
                spot = lax.rem(z + j, ring) * 2 + place
                whole = lax.dynamic_update_index_in_dim(whole, pieces_held[j], spot, 0)
        return whole.reshape(devices * depth, lanes)

    def forward(b):
        nonlocal own_inputs
        if b + 1 in rings:
            slots[b + 1] = lay_out(b + 1, results[b - 1][0])
        results.append(run_forward(dims, b, scal, inputs[b], holding(b), readout_own))
        if b < sections - 1:
            out = results[b][0]
            inputs.append([out] + exchange([out] * (sections - 1)))
            for k in [0] + list(range(sections - 1, 0, -1)):
                value = jnp.where(s == b + 1, inputs[b + 1][k], own_inputs[k])
                own_inputs = lax.dynamic_update_index_in_dim(own_inputs, value, k, 0)

    def piece_of(slot):
        if slot == 0:
            return pieces[0]
        return pick(pieces, jnp.where(slot - 1 < s, slot - 1, slot) ^ s)

    for slot in range(2, sections, 2):
        piece = piece_of(slot)
        gates = [readout_own, *slices] if slot == 2 else done[slot - 2, ring - 1]
        up = down = after(piece, *gates)
        for step in range(1, ring):
            up = lax.ppermute(up, "dp", hops(step, 1, ring))
            down = lax.ppermute(down, "dp", hops(step, -1, ring))
            done[slot, step] = [up, down]
        held = [piece]
        for j in range(1, ring):
            held.append(jnp.where(z + j < ring, done[slot, j][1], done[slot, ring - j][0]))
        held = jnp.stack(held)
        rings[slot] = (held, swap_core(held))
    gates = []
    for slot in [0] + list(range(1, sections, 2)):
        piece = after(piece_of(slot), *gates) if gates else piece_of(slot)
        gathered = lax.all_gather(piece, "dp", axis=0, tiled=True)
        slots[slot] = gathered
        gates = [gathered] + done.get((2, 1) if slot == 0 else (slot + 1, ring - 1), [])
    for b in range(sections):
        forward(b)
    result = results[-1]
    logits = result[2]
    heads = [logits] + exchange([logits] * (sections - 1))
    heads += [labels[:, None], readout_own]

    def ordered(parts):
        return jnp.concatenate([pick(parts, s ^ j) for j in range(sections)], axis=1)

    x_all = lax.all_gather(own_inputs.reshape(sections * rows, lanes), "dp")

    raws = [None] * sections
    for b in reversed(range(sections)):
        held = holding(b) if b > 0 else None
        result = run_backward(dims, b, classes, scal, heads, results[b][1], held)
        raws[b] = result[0]
        if b > 0:
            heads = [result[1]] + exchange(result[2:])

    sent = [pick(raws, s ^ k) for k in range(sections)]
    own_raw = ordered([sent[0]] + exchange(sent[1:]))
    start = d * depth
    channel = start % channels
    step = 1
    while channels % (2 * step) == 0 and depth % (2 * step) == 0:
        step *= 2
    spans = -(-(channels - step + depth) // channels)

    x_all = x_all.reshape(devices, sections, height, width, group, lanes)
    fields = jnp.concatenate(
        [
            lax.dynamic_index_in_dim(x_all, s ^ j, 1, keepdims=False)
            for j in range(sections)
        ],
        axis=-1,
    )
    fields = jnp.pad(fields, ((0, 0), (1, 1), (1, 1), (0, 0), (0, 0)))
    shifted = []
    for i in range(spans):
        offset = jnp.minimum(start // channels + i, 8)
        shifted.append(
            lax.dynamic_slice(
                fields,
                (0, offset // 3, offset % 3, 0, 0),
                (devices, height, width, group, channels),
            ).reshape(devices * rows, channels)
        )
    cols = lax.dynamic_slice_in_dim(jnp.concatenate(shifted, axis=1), channel, depth, 1)

    raw_all = lax.all_gather(own_raw, "dp", axis=0, tiled=True)
    outs = run_update(cols.T, raw_all, weights[0], first_moment[0], second_moment[0])
    return tuple(out[None] for out in outs)


def solution(mesh):
    return jax.shard_map(
        shards,
        mesh=mesh,
        in_specs=(
            P("dp", None, None, None, None),
            P("dp"),
            P(),
            P("section", "dp", None),
            P("section", "dp", None),
            P("section", "dp", None),
        ),
        out_specs=(P("section", "dp", None), P("section", "dp", None), P("section", "dp", None)),
        check_vma=False,
    )
```
